128 devices in a mesh: gx: 8 (over z, core), gy: 4 (over x), gz: 4 (over y).
Axes of the slice: x: 4, y: 4, z: 4, core: 2. Of those that a mesh axis runs over, the one named last changes fastest.
Arguments:
- fields: bfloat16 [131072, 4, 512], P(('gx', 'gy', 'gz')), may hold values from -16 to 16
- jacobian: bfloat16 [131072, 512], P(('gx', 'gy', 'gz')), may hold values from 0.25 to 4
- home_slot: int32 [131072], P(('gx', 'gy', 'gz')), may hold values from 0 to 131071, as said below
Outputs:
- mid_level: float32 [4, 64, 256, 512], P(None, 'gx', 'gy', 'gz')
- coarse_level: float32 [4, 32, 128, 256], P(None, 'gx', 'gy', 'gz')
The draws below stay inside these ranges and needn't reach their ends.
Inputs may be any that keep to these rules, and one draw needn't show every extreme that they name: home_slot is a permutation of the lattice slots. Slot s lies in the brick of device s // 1024 in the order gx, gy, gz (gx slowest). Each element's brick is the holder's own or one whose brick coordinates differ from the holder's by one in exactly one direction, without wrap-around. One device sends at most 16 elements to any other brick, and in every draw some device sends exactly 16 to a neighbour along gx.
All inputs are finite; a program needn't handle non-finite values.
Results may differ from the reference program's by a relative error of at most 0.0033.
Values may be sent and summed in bfloat16 or wider, within the bound.
No kernel may reach another device: no remote copies, remote signals or barrier semaphores. Data moves between devices by JAX's collectives and lax.ppermute only.
A program may use at most 192 MiB of HBM per device.

```python
import math
import jax
import jax.numpy as jnp
import numpy as np
from jax import lax

FIELDS = 4
POINTS = 512
EX = 2
EY = 16
EZ = 32
CAP = 16
ELEM_DEV = 1024
ELEMS = 131072
N_GX = 8
N_GY = 4
N_GZ = 4


def draw_home_slot(key, part):
    devices = N_GX * N_GY * N_GZ
    elem_count = ELEM_DEV
    region = elem_count // 6
    key_amount = jax.random.fold_in(key, 11)
    key_pick = jax.random.fold_in(key, 12)
    key_order = jax.random.fold_in(key, 13)
    amounts = jax.random.randint(key_amount, (devices, 3), max(CAP // 2, 1), CAP + 1)
    device_ids = jnp.arange(devices, dtype=jnp.int32)
    coord_x = device_ids // (N_GY * N_GZ)
    coord_y = device_ids // N_GZ % N_GY
    coord_z = device_ids % N_GZ
    pick_x = jax.random.randint(jax.random.fold_in(key_pick, 1), (), 0, N_GX - 1)
    pick_y = jax.random.randint(jax.random.fold_in(key_pick, 2), (), 0, N_GY)
    pick_z = jax.random.randint(jax.random.fold_in(key_pick, 3), (), 0, N_GZ)
    chosen = (pick_x * N_GY + pick_y) * N_GZ + pick_z
    amounts = amounts.at[chosen, 0].set(CAP)
    home = jnp.arange(devices * elem_count, dtype=jnp.int32).reshape(devices, elem_count)
    span = jnp.arange(region, dtype=jnp.int32)
    layout = [(coord_x, N_GX, N_GY * N_GZ), (coord_y, N_GY, N_GZ), (coord_z, N_GZ, 1)]
    for axis_position_index in range(3):
        coords, extent, stride = layout[axis_position_index]
        valid = (coords[:, None] < extent - 1) & (span[None, :] < amounts[:, axis_position_index:axis_position_index + 1])
        neighbour = device_ids + stride
        upper_pos = 2 * axis_position_index * region + span
        lower_pos = (2 * axis_position_index + 1) * region + span
        upper_vals = neighbour[:, None] * elem_count + lower_pos[None, :]
        home = home.at[:, upper_pos].set(jnp.where(valid, upper_vals, home[:, upper_pos]))
        target_rows = jnp.where(valid, neighbour[:, None], devices)
        lower_vals = device_ids[:, None] * elem_count + upper_pos[None, :]
        home = home.at[target_rows, jnp.broadcast_to(lower_pos[None, :], (devices, region))].set(lower_vals, mode='drop')
    order_keys = jax.random.split(key_order, devices)
    orders = jax.vmap(lambda single_key: jax.random.permutation(single_key, elem_count))(order_keys)
    home = jnp.take_along_axis(home, orders, axis=1)
    return home.reshape(-1).astype(jnp.int32)


def shard_levels(stream_key, shape, pieces, low, largest):
    def one(dim, parts):
        heights = jax.random.uniform(jax.random.fold_in(jax.random.fold_in(stream_key, 6), dim), (parts,), jnp.float32, low / len(pieces), largest / len(pieces))
        return jnp.repeat(jnp.exp(heights), shape[dim] // parts).reshape((-1,) + (1,) * (len(shape) - dim - 1))

    gain = one(*pieces[0])
    for cut in pieces[1:]:
        gain = gain * one(*cut)
    return gain


def gaussian(key, shape, spread, bound, shards=(), kind=jnp.bfloat16):
    factor_of = shard_levels(key, shape, shards, -0.22, 0.18) if shards else 1.0
    entries = jax.random.normal(key, shape, jnp.float32) * spread * factor_of
    return jnp.minimum(jnp.maximum(entries, -bound), bound).astype(kind)


def setup_inputs(seed: int = 0) -> dict:
    splits = jax.random.split(jax.random.key(seed), 4)
    fields = gaussian(splits[0], (ELEMS, FIELDS, POINTS), 4.0, 16.0, ((0, 128),))
    jacobian = jnp.clip(jnp.exp(math.log(4.0) - 2.7725887 * jax.random.uniform(splits[1], (ELEMS, POINTS), jnp.float32) ** shard_levels(splits[1], (ELEMS, POINTS), ((0, 128),), -0.2, 0.2)), 0.25, 4.0).astype(jnp.bfloat16)
    home_slot = draw_home_slot(jax.random.fold_in(splits[3], 71), 0)
    return {"fields": fields, "jacobian": jacobian, "home_slot": home_slot}


GLL_NODES = np.array([-1.0, -0.8717401485096066, -0.5917001814331423, -0.2092992179024789, 0.2092992179024789, 0.5917001814331423, 0.8717401485096066, 1.0])


def gll_basis():
    targets = -1.0 + (2.0 * np.arange(8) + 1.0) / 8.0
    basis_table = np.ones((8, 8))
    for node_index in range(8):
        for other_index in range(8):
            if other_index != node_index:
                basis_table[:, node_index] *= (targets - GLL_NODES[other_index]) / (GLL_NODES[node_index] - GLL_NODES[other_index])
    return basis_table


def plain_sinc(points):
    return np.sin(np.pi * points) / (np.pi * points)


def lanczos_taps():
    offsets = np.arange(8) - 3.5
    sample_values = plain_sinc(offsets / 2.0) * plain_sinc(offsets / 4.0)
    return sample_values / np.sum(sample_values)


def reduce_resolution(volume_block, axis_position_index, filter_weight_vector):
    length = volume_block.shape[axis_position_index]
    widths = [(0, 0), (0, 0), (0, 0)]
    widths[axis_position_index] = (3, 3)
    padded = jnp.pad(volume_block, widths)
    result = jnp.zeros_like(lax.slice_in_dim(padded, 0, length - 1, 2, axis_position_index))
    for tap_index in range(8):
        result = result + filter_weight_vector[tap_index] * lax.slice_in_dim(padded, tap_index, tap_index + length - 1, 2, axis_position_index)
    return result


def reference(fields, jacobian, home_slot):
    basis_table = jnp.asarray(gll_basis(), jnp.float32)
    total = fields.shape[0]

    def interpolate(pair):
        block_fields, block_jac = pair
        sample_values = block_fields.astype(jnp.float32).reshape(-1, 4, 8, 8, 8)
        sample_values = jnp.einsum("nfabc,ia->nfibc", sample_values, basis_table, precision=lax.Precision.HIGHEST)
        sample_values = jnp.einsum("nfibc,jb->nfijc", sample_values, basis_table, precision=lax.Precision.HIGHEST)
        sample_values = jnp.einsum("nfijc,kc->nfijk", sample_values, basis_table, precision=lax.Precision.HIGHEST)
        sample_values = sample_values.reshape(-1, 4, 512) * block_jac.astype(jnp.float32)[:, None, :]
        return sample_values.astype(jnp.bfloat16)

    uniform = lax.map(interpolate, (fields.reshape(-1, ELEM_DEV, 4, 512), jacobian.reshape(-1, ELEM_DEV, 512)))
    uniform = uniform.reshape(total, 4, 512)
    placed = jnp.zeros_like(uniform).at[home_slot.astype(jnp.int32)].set(uniform)
    grid = placed.reshape(N_GX, N_GY, N_GZ, EX, EY, EZ, 4, 8, 8, 8)
    grid = grid.transpose(6, 0, 3, 7, 1, 4, 8, 2, 5, 9).reshape(4, N_GX * EX * 8, N_GY * EY * 8, N_GZ * EZ * 8)
    complete_filter_weights = jnp.asarray(lanczos_taps(), jnp.float32)
    lowpass_filter_weights = complete_filter_weights.astype(jnp.bfloat16).astype(jnp.float32)

    def coarsen(uniform_field_block):
        sample_values = reduce_resolution(uniform_field_block.astype(jnp.float32), 2, lowpass_filter_weights)
        sample_values = reduce_resolution(sample_values, 1, complete_filter_weights)
        middle_field_grid = reduce_resolution(sample_values, 0, complete_filter_weights)
        sample_values = reduce_resolution(middle_field_grid, 2, complete_filter_weights)
        sample_values = reduce_resolution(sample_values, 1, complete_filter_weights)
        coarsest_field_grid = reduce_resolution(sample_values, 0, complete_filter_weights)
        return middle_field_grid, coarsest_field_grid

    mid_level, coarse_level = lax.map(coarsen, grid)
    return mid_level, coarse_level
```

```python
import jax
import jax.numpy as jnp
import numpy as np
from jax import lax
from jax.experimental import pallas as pl
from jax.experimental.pallas import tpu as pltpu
from jax.sharding import PartitionSpec as P

F32 = jnp.float32
BF16 = jnp.bfloat16
MIB = 1024 * 1024

GLL_NODES = np.array(
    [
        -1.0,
        -0.8717401485096066,
        -0.5917001814331423,
        -0.2092992179024789,
        0.2092992179024789,
        0.5917001814331423,
        0.8717401485096066,
        1.0,
    ]
)

SHIFTS = (("gx", 1), ("gx", -1), ("gy", 1), ("gy", -1), ("gz", 1), ("gz", -1))
STEPS = (16, -16, 4, -4, 1, -1)
PAYLOAD = 336


def gll_basis():
    targets = -1.0 + (2.0 * np.arange(8) + 1.0) / 8.0
    table = np.ones((8, 8))
    for node in range(8):
        for other in range(8):
            if other != node:
                table[:, node] *= (targets - GLL_NODES[other]) / (
                    GLL_NODES[node] - GLL_NODES[other]
                )
    return table


def plain_sinc(points):
    return np.sin(np.pi * points) / (np.pi * points)


def lanczos_taps():
    offsets = np.arange(8) - 3.5
    values = plain_sinc(offsets / 2.0) * plain_sinc(offsets / 4.0)
    return values / np.sum(values)


TAPS = [float(v) for v in lanczos_taps()]


def bf16_of(table):
    return np.asarray(table, np.float32).astype(jnp.bfloat16)


def interp_table():
    basis = gll_basis()
    table = np.einsum("ia,jb,kc->kijabc", basis, basis, basis).reshape(512, 512)
    return bf16_of(table)


def point_order():
    table = np.zeros((8, 8, 8, 8, 8, 8))
    for i in range(8):
        for j in range(8):
            for k in range(8):
                table[k, i, j, i, j, k] = 1.0
    return bf16_of(table.reshape(512, 512))


def depth_tables():
    taps = lanczos_taps()
    low = taps.astype(np.float32).astype(jnp.bfloat16).astype(np.float64)
    first = np.zeros((256, 132))
    for column in range(132):
        for tap in range(8):
            z = 2 * (column - 2) - 3 + tap
            if 0 <= z < 256:
                first[z, column] = low[tap]
    second = np.zeros((132, 70))
    for column in range(70):
        for tap in range(8):
            z = 2 * (column - 3) - 3 + tap + 2
            if 0 <= z < 132:
                second[z, column] = taps[tap]
    out = []
    for place in range(3):
        mid = first.copy()
        if place == 0:
            mid[:, :2] = 0.0
        if place == 2:
            mid[:, 130:] = 0.0
        both = mid @ second
        if place == 0:
            both[:, :3] = 0.0
        if place == 2:
            both[:, 67:] = 0.0
        columns = np.zeros((256, 256))
        columns[:, :128] = mid[:, 2:130]
        columns[:, 128:192] = both[:, 3:67]
        columns[:, 192:194] = mid[:, :2]
        columns[:, 194:196] = mid[:, 130:]
        columns[:, 196:199] = both[:, :3]
        columns[:, 199:202] = both[:, 67:]
        out.append(columns.reshape(32, 8, 256).transpose(1, 0, 2).reshape(256, 256))
    return bf16_of(np.stack(out))


def nt(a, b):
    return lax.dot_general(a, b, (((1,), (1,)), ((), ())), preferred_element_type=F32)


def nn(a, b):
    return lax.dot_general(a, b, (((1,), (0,)), ((), ())), preferred_element_type=F32)


def tn(a, b):
    return lax.dot_general(a, b, (((0,), (0,)), ((), ())), preferred_element_type=F32)


def pack_kernel(coords, home, jac, utri, fields, *rest):
    outs = rest[:6]
    picker, index_v, index_s, sem_index, sem_rows = rest[6:]
    me = coords[3]
    slots = home[...]
    diff = (slots >> 10) - me
    tag = (slots & 1023) + 1
    masks = jnp.concatenate([jnp.where(diff == step, 1.0, 0.0) for step in STEPS], axis=0)
    counts = nn(masks.astype(BF16), utri[...])
    row = lax.broadcasted_iota(jnp.int32, (8, 128), 0)
    slot_id = lax.broadcasted_iota(jnp.int32, (16, 128), 0).astype(F32)
    for d in range(6):
        count = counts[d * 8 : d * 8 + 8]
        total = jnp.broadcast_to(count[:, 127:128], (8, 128))
        rank = count - 1.0
        for r in range(7):
            rank = rank + jnp.where(row > r, jnp.broadcast_to(total[r : r + 1], (8, 128)), 0.0)
        rank = jnp.where(masks[d * 8 : d * 8 + 8] > 0.5, rank, -1.0)
        for r in range(8):
            hit = jnp.broadcast_to(rank[r : r + 1], (16, 128)) == slot_id
            picker[d * 16 : d * 16 + 16, r * 128 : r * 128 + 128] = jnp.where(
                hit, 1.0, 0.0
            ).astype(BF16)
    picker[96:128, :] = jnp.zeros((32, 1024), BF16)
    lane = lax.broadcasted_iota(jnp.int32, (8, 128), 1)
    pieces = []
    for r in range(8):
        own_tag = jnp.broadcast_to(tag[r : r + 1], (8, 128))
        elem = lane + r * 128
        value = jnp.where(
            row == 0,
            elem >> 5,
            jnp.where(row == 1, elem & 31, jnp.where(row == 2, own_tag >> 5, own_tag & 31)),
        )
        pieces.append(value.astype(F32).astype(BF16))
    values = jnp.concatenate(pieces, axis=1)
    found = nt(values, picker[...])
    index = found[0:1] * 32.0 + found[1:2]
    index_v[...] = jnp.broadcast_to(index, (8, 128)).astype(jnp.int32)
    copy_index = pltpu.make_async_copy(index_v, index_s, sem_index)
    copy_index.start()
    copy_index.wait()
    copies = []
    for d in range(6):
        for s in range(16):
            start = pl.multiple_of(index_s[0, d * 16 + s] * 16, 16)
            copy = pltpu.make_async_copy(
                fields.at[pl.ds(start, 16)], outs[d].at[pl.ds(s * 16, 16)], sem_rows.at[d]
            )
            copy.start()
    jac_rows = nn(picker[...], jac[...]).astype(BF16)
    tag_lane = lax.broadcasted_iota(jnp.int32, (16, 128), 1)
    tag_row = lax.broadcasted_iota(jnp.int32, (16, 128), 0)
    tag_hi = jnp.broadcast_to(found[2:3], (16, 128))
    tag_lo = jnp.broadcast_to(found[3:4], (16, 128))
    both = jnp.where(tag_row == 0, tag_hi, jnp.where(tag_row == 1, tag_lo, 0.0))
    for d in range(6):
        for c in range(4):
            outs[d][256 + c * 16 : 272 + c * 16, :] = jac_rows[
                d * 16 : d * 16 + 16, c * 128 : c * 128 + 128
            ]
        outs[d][320:336, :] = jnp.where((tag_lane >> 4) == d, both, 0.0).astype(BF16)
    for d in range(6):
        pltpu.make_async_copy(
            fields.at[pl.ds(0, 256)], outs[d].at[pl.ds(0, 256)], sem_rows.at[d]
        ).wait()


def pack(coords, home, jac, fields_rows):
    utri = np.triu(np.ones((128, 128)))
    vmem = pl.BlockSpec(memory_space=pltpu.VMEM)
    return pl.pallas_call(
        pack_kernel,
        out_shape=[jax.ShapeDtypeStruct((PAYLOAD, 128), BF16)] * 6,
        in_specs=[
            pl.BlockSpec(memory_space=pltpu.SMEM),
            vmem,
            vmem,
            vmem,
            pl.BlockSpec(memory_space=pl.ANY),
        ],
        out_specs=[vmem] * 6,
        scratch_shapes=[
            pltpu.VMEM((128, 1024), BF16),
            pltpu.VMEM((8, 128), jnp.int32),
            pltpu.SMEM((8, 128), jnp.int32),
            pltpu.SemaphoreType.DMA,
            pltpu.SemaphoreType.DMA((6,)),
        ],
        compiler_params=pltpu.CompilerParams(vmem_limit_bytes=16 * MIB),
        name="pack",
    )(coords, home, jac, jnp.asarray(bf16_of(utri)), fields_rows)


def own_kernel(coords, home_s, home_row, fields, jac, table, order, out, rows, jac_t):
    n = pl.program_id(0)

    @pl.when(n == 0)
    def _():
        me = coords[3]

        def clear(e, carry):
            rows[pl.ds(pl.multiple_of(e * 256, 256), 256), :] = jnp.zeros((256, 128), F32)
            return carry

        lax.fori_loop(0, 64, clear, 0)

        def place(e, carry):
            for u in range(8):
                elem = e * 8 + u
                slot = home_s[elem]
                spot = jnp.where((slot >> 10) == me, slot & 1023, 1024)
                rows[pl.ds(pl.multiple_of(spot * 16, 16), 16), :] = fields[
                    pl.ds(pl.multiple_of(elem * 16, 16), 16), :
                ].astype(F32)
            return carry

        lax.fori_loop(0, 128, place, 0)
        slots = home_row[...]
        spot = jnp.where((slots >> 10) == me, slots & 1023, -1)
        ordered = nt(order[...], jac[...]).astype(BF16)
        for c in range(4):
            ids = lax.broadcasted_iota(jnp.int32, (256, 1024), 0) + c * 256
            hit = jnp.where(ids == jnp.broadcast_to(spot, (256, 1024)), 1.0, 0.0).astype(BF16)
            jac_t[:, c * 256 : c * 256 + 256] = nt(ordered, hit)

    base = n * 4096
    for f in range(4):
        pieces = [
            rows[pl.ds(base + c * 4 + f, 256, stride=16), :].astype(BF16) for c in range(4)
        ]
        values = nt(table[...], jnp.concatenate(pieces, axis=1))
        out[f * 512 : f * 512 + 512, :] = (
            values * jac_t[:, pl.ds(pl.multiple_of(n * 256, 256), 256)]
        ).astype(BF16)


def own_elements(coords, home_slot, home_row, fields_rows, jac):
    whole = lambda *shape: pl.BlockSpec(shape, lambda n: (0,) * len(shape))
    smem = pl.BlockSpec(memory_space=pltpu.SMEM)
    return pl.pallas_call(
        own_kernel,
        grid=(4,),
        out_shape=jax.ShapeDtypeStruct((2048, 1024), BF16),
        in_specs=[
            smem,
            smem,
            whole(1, 1024),
            whole(16384, 128),
            whole(1024, 512),
            whole(512, 512),
            whole(512, 512),
        ],
        out_specs=pl.BlockSpec((2048, 256), lambda n: (0, n)),
        scratch_shapes=[
            pltpu.VMEM((1025 * 16, 128), F32),
            pltpu.VMEM((512, 1024), F32),
        ],
        compiler_params=pltpu.CompilerParams(vmem_limit_bytes=48 * MIB),
        cost_estimate=pl.CostEstimate(
            flops=6_000_000_000, bytes_accessed=10_000_000, transcendentals=0
        ),
        name="own_elements",
    )(
        coords,
        home_slot,
        home_row,
        fields_rows,
        jac,
        jnp.asarray(interp_table()),
        jnp.asarray(point_order()),
    )


def halve(values, outputs, shift):
    results = []
    for o in range(outputs):
        total = None
        for tap in range(8):
            at = 2 * o + tap - shift
            if 0 <= at < len(values):
                term = TAPS[tap] * values[at]
                total = term if total is None else total + term
        results.append(total)
    return results


def filter_kernel(
    coords, ut0, ut1, a0, a1, a2, a3, a4, a5, table, order, depth,
    main_a, edge_a, main_c, edge_c, to_low, to_high,
    raw, arrived, rhs, lhs, wide, ya, yb, mb, yc, pbz, pcz,
):
    t = pl.program_id(0)
    arrays = (a0, a1, a2, a3, a4, a5)
    one = lambda flag: jnp.where(flag, 1.0, 0.0)
    x_low = one(coords[0] > 0)
    x_high = one(coords[0] < 7)
    y_low = one(coords[1] > 0)
    y_high = one(coords[1] < 3)

    @pl.when(t == 0)
    def _():
        raw[1536:2048, :] = jnp.zeros((512, 128), F32)
        for d in range(6):
            raw[d * 256 : d * 256 + 256, :] = arrays[d][0:256, :].astype(F32)
        jac = jnp.concatenate(
            [
                jnp.concatenate(
                    [arrays[d][256 + c * 16 : 272 + c * 16, :] for c in range(4)], axis=1
                )
                for d in range(6)
            ]
            + [jnp.zeros((32, 512), BF16)],
            axis=0,
        )
        jac_t = nt(order[...], jac)
        for f in range(4):
            pieces = [
                raw[pl.ds(c * 4 + f, 128, stride=16), :].astype(BF16) for c in range(4)
            ]
            values = nt(table[...], jnp.concatenate(pieces, axis=1))
            arrived[f * 512 : f * 512 + 512, :] = (values * jac_t).astype(BF16)
        rhs[...] = jnp.zeros((1024, 1024), BF16)
        for k in range(8):
            block = depth[k * 32 : k * 32 + 32, :]
            for e in range(4):
                rhs[k * 128 + e * 32 : k * 128 + e * 32 + 32, e * 256 : e * 256 + 256] = block

        def pads(q, carry):
            zero = jnp.zeros((24, 128), F32)
            base = pl.multiple_of(q * 176, 8)
            for ref in (ya, yb):
                ref[pl.ds(base, 24), :] = zero
                ref[pl.ds(base + 152, 24), :] = zero
            return carry

        lax.fori_loop(0, 48, pads, 0)

        def more_pads(q, carry):
            zero = jnp.zeros((16, 128), F32)
            base = pl.multiple_of(q * 112, 8)
            yc[pl.ds(base, 16), :] = zero
            yc[pl.ds(base + 96, 16), :] = zero
            return carry

        lax.fori_loop(0, 40, more_pads, 0)

    tags = jnp.zeros((8, 128), F32)
    for d in range(6):
        tags = tags + arrays[d][320:336, :].astype(F32)[0:8]
    spot = (tags[0:1] * 32.0 + tags[1:2]).astype(jnp.int32) - 1
    for ex, ut in ((0, ut0), (1, ut1)):
        ids = lax.broadcasted_iota(jnp.int32, (128, 128), 0) + (ex * 512 + t * 128)
        hit = jnp.where(ids == jnp.broadcast_to(spot, (128, 128)), 1.0, 0.0).astype(BF16)
        for f in range(4):
            part = nt(arrived[f * 512 : f * 512 + 512, :], hit)
            total = (part + ut[f * 512 : f * 512 + 512, :].astype(F32)).astype(BF16)
            for k in range(8):
                lhs[ex * 256 + f * 64 : ex * 256 + f * 64 + 64, k * 128 : k * 128 + 128] = total[
                    k * 64 : k * 64 + 64
                ]
    for c in range(4):
        wide[:, c * 256 : c * 256 + 256] = nn(lhs[...], rhs[:, c * 256 : c * 256 + 256])

    for f in range(4):
        for column in range(8):
            ref = (ya, yb)[column % 2]
            values = [
                wide[
                    ex * 256 + f * 64 + i * 8 : ex * 256 + f * 64 + i * 8 + 8,
                    column * 128 : column * 128 + 128,
                ]
                for ex in range(2)
                for i in range(8)
            ]
            results = halve(values, 12, 7)
            for o in range(12):
                value = results[o]
                if o < 2:
                    value = value * x_low
                if o >= 10:
                    value = value * x_high
                at = (f * 12 + o) * 176 + 24 + (column // 2) * 8 + t * 32
                ref[pl.ds(pl.multiple_of(at, 8), 8), :] = value

    @pl.when(t == 3)
    def _():
        def along_y(ref, base, count):
            total = None
            for tap in range(8):
                term = TAPS[tap] * ref[pl.ds(base + 5 + tap, count, stride=2), :]
                total = term if total is None else total + term
            low = total[0:8] * y_low
            high = total[count - 8 : count] * y_high
            return low, total[8 : count - 8], high

        def first(q, carry):
            low, middle, high = along_y(ya, q * 176, 80)
            edge_a[pl.ds(pl.multiple_of(q * 16, 16), 8), :] = low
            edge_a[pl.ds(pl.multiple_of(q * 16 + 8, 8), 8), :] = high
            main_a[pl.ds(pl.multiple_of(q * 64, 64), 64), :] = middle
            low, middle, high = along_y(yb, q * 176, 80)
            base = pl.multiple_of(q * 80, 16)
            mb[pl.ds(base, 8), :] = low
            mb[pl.ds(base + 8, 64), :] = middle
            mb[pl.ds(base + 72, 8), :] = high
            pbz[pl.ds(pl.multiple_of(q * 16, 16), 16), :] = jnp.concatenate(
                [low, high], axis=0
            ).astype(BF16)
            pbz[pl.ds(pl.multiple_of(768 + q * 64, 64), 64), :] = middle.astype(BF16)
            return carry

        lax.fori_loop(0, 48, first, 0)

        def along_x(v, carry):
            for f in range(4):
                values = [
                    mb[pl.ds(pl.multiple_of((f * 12 + o) * 80 + v * 8, 8), 8), :]
                    for o in range(12)
                ]
                results = halve(values, 10, 7)
                for o in range(10):
                    value = results[o]
                    if o < 3:
                        value = value * x_low
                    if o >= 7:
                        value = value * x_high
                    at = (f * 10 + o) * 112 + 16 + v * 8
                    yc[pl.ds(pl.multiple_of(at, 8), 8), :] = value
            return carry

        lax.fori_loop(0, 10, along_x, 0)

        def second(q, carry):
            low, middle, high = along_y(yc, q * 112, 48)
            edge_c[pl.ds(pl.multiple_of(q * 16, 16), 8), :] = low
            edge_c[pl.ds(pl.multiple_of(q * 16 + 8, 8), 8), :] = high
            main_c[pl.ds(pl.multiple_of(q * 32, 32), 32), :] = middle
            pcz[pl.ds(pl.multiple_of(q * 16, 16), 16), :] = jnp.concatenate(
                [low, high], axis=0
            ).astype(BF16)
            pcz[pl.ds(pl.multiple_of(640 + q * 32, 32), 32), :] = middle.astype(BF16)
            return carry

        lax.fori_loop(0, 40, second, 0)
        row = lax.broadcasted_iota(jnp.int32, (16, 128), 0)
        lane = lax.broadcasted_iota(jnp.int32, (16, 128), 1)
        pick = lambda count, first_lane: jnp.where(
            (row < count) & (lane == row + first_lane), 1.0, 0.0
        ).astype(BF16)
        for ref, at_mid, at_coarse in ((to_low, 64, 68), (to_high, 66, 71)):
            ref[:, 0:3840] = nt(pick(2, at_mid), pbz[...])[0:8].astype(BF16)
            ref[:, 3840:5760] = nt(pick(3, at_coarse), pcz[...])[0:8].astype(BF16)


def filters(coords, uniform_t, arrived):
    whole = lambda *shape: pl.BlockSpec(shape, lambda t: (0,) * len(shape))
    smem = pl.BlockSpec(memory_space=pltpu.SMEM)
    iz = coords[2]
    place = jnp.where(iz == 0, 0, jnp.where(iz == 3, 2, 1))
    depth = lax.dynamic_index_in_dim(jnp.asarray(depth_tables()), place, 0, keepdims=False)
    return pl.pallas_call(
        filter_kernel,
        grid=(4,),
        out_shape=[
            jax.ShapeDtypeStruct((48 * 64, 128), F32),
            jax.ShapeDtypeStruct((48 * 16, 128), F32),
            jax.ShapeDtypeStruct((40 * 32, 128), F32),
            jax.ShapeDtypeStruct((40 * 16, 128), F32),
            jax.ShapeDtypeStruct((8, 5760), BF16),
            jax.ShapeDtypeStruct((8, 5760), BF16),
        ],
        in_specs=[
            smem,
            pl.BlockSpec((2048, 128), lambda t: (0, t)),
            pl.BlockSpec((2048, 128), lambda t: (0, t + 4)),
        ]
        + [whole(PAYLOAD, 128)] * 6
        + [whole(512, 512), whole(512, 512), whole(256, 256)],
        out_specs=[
            whole(48 * 64, 128),
            whole(48 * 16, 128),
            whole(40 * 32, 128),
            whole(40 * 16, 128),
            whole(8, 5760),
            whole(8, 5760),
        ],
        scratch_shapes=[
            pltpu.VMEM((2048, 128), F32),
            pltpu.VMEM((2048, 128), BF16),
            pltpu.VMEM((1024, 1024), BF16),
            pltpu.VMEM((512, 1024), BF16),
            pltpu.VMEM((512, 1024), F32),
            pltpu.VMEM((48 * 176, 128), F32),
            pltpu.VMEM((48 * 176, 128), F32),
            pltpu.VMEM((48 * 80, 128), F32),
            pltpu.VMEM((40 * 112, 128), F32),
            pltpu.VMEM((3840, 128), BF16),
            pltpu.VMEM((1920, 128), BF16),
        ],
        compiler_params=pltpu.CompilerParams(vmem_limit_bytes=56 * MIB),
        name="filters",
    )(
        coords,
        uniform_t,
        uniform_t,
        *arrived,
        jnp.asarray(interp_table()),
        jnp.asarray(point_order()),
        depth,
    )


def depth_spread(first_lane_high, count):
    table = np.zeros((16, 128))
    for r in range(count):
        table[r, r] = 1.0
        table[8 + r, first_lane_high + r] = 1.0
    return bf16_of(table)


def y_edges_kernel(edge_a, edge_c, from_low, from_high, spread_a, spread_c,
                   to_low, to_high, sa, sc):
    lanes = jnp.concatenate([from_low[:, 0:768], from_high[:, 0:768]], axis=0)
    sa[...] = edge_a[...] + tn(lanes, spread_a[...])
    lanes = jnp.concatenate([from_low[:, 3840:4480], from_high[:, 3840:4480]], axis=0)
    sc[...] = edge_c[...] + tn(lanes, spread_c[...])
    for ref, ra, rc in ((to_low, 6, 5), (to_high, 8, 8)):
        for r in range(2):
            ref[r * 48 : r * 48 + 48, :] = sa[pl.ds(ra + r, 48, stride=16), :].astype(BF16)
        tail = [sc[pl.ds(rc + r, 40, stride=16), :] for r in range(3)] + [jnp.zeros((8, 128), F32)]
        ref[96:224, :] = jnp.concatenate(tail, axis=0).astype(BF16)


def vmem_call(kernel, out_shape, scratch, name, *operands, **options):
    vmem = pl.BlockSpec(memory_space=pltpu.VMEM)
    single = not isinstance(out_shape, list)
    return pl.pallas_call(
        kernel,
        out_shape=out_shape,
        in_specs=[vmem] * len(operands),
        out_specs=vmem if single else [vmem] * len(out_shape),
        scratch_shapes=scratch,
        compiler_params=pltpu.CompilerParams(vmem_limit_bytes=32 * MIB),
        name=name,
        **options,
    )(*operands)


def x_edges_kernel(main_a, main_c, zl, zh, yl, yh, spread_a, spread_c,
                   sa, sc, to_low, to_high, fl, fh):
    lanes = jnp.concatenate([zl[:, 768:3840], zh[:, 768:3840]], axis=0)
    sa[...] = main_a[...] + tn(lanes, spread_a[...])
    lanes = jnp.concatenate([zl[:, 4480:5760], zh[:, 4480:5760]], axis=0)
    sc[...] = main_c[...] + tn(lanes, spread_c[...])
    fl[...] = yl[...].astype(F32)
    fh[...] = yh[...].astype(F32)
    for r in range(2):
        sa[pl.ds(r, 48, stride=64), :] += fl[r * 48 : r * 48 + 48, :]
        sa[pl.ds(62 + r, 48, stride=64), :] += fh[r * 48 : r * 48 + 48, :]
    for r in range(3):
        sc[pl.ds(r, 40, stride=32), :] += fl[96 + r * 40 : 136 + r * 40, :]
        sc[pl.ds(29 + r, 40, stride=32), :] += fh[96 + r * 40 : 136 + r * 40, :]
    for ref, xa, xc in ((to_low, 0, 0), (to_high, 10, 7)):
        for f in range(4):
            ref[f * 128 : f * 128 + 128, :] = sa[
                (f * 12 + xa) * 64 : (f * 12 + xa) * 64 + 128, :
            ].astype(BF16)
            ref[512 + f * 96 : 608 + f * 96, :] = sc[
                (f * 10 + xc) * 32 : (f * 10 + xc) * 32 + 96, :
            ].astype(BF16)


def final_kernel(sa, sc, xl, xh, mid, coarse):
    for f in range(4):
        for x in range(8):
            base = (f * 12 + x + 2) * 64
            value = sa[base : base + 64, :]
            if x < 2:
                value = value + xl[f * 128 + x * 64 : f * 128 + x * 64 + 64, :].astype(F32)
            if x >= 6:
                at = f * 128 + (x - 6) * 64
                value = value + xh[at : at + 64, :].astype(F32)
            mid[f, x] = value
        for x in range(4):
            base = (f * 10 + x + 3) * 32
            value = sc[base : base + 32, :]
            if x < 3:
                at = 512 + f * 96 + x * 32
                value = value + xl[at : at + 32, :].astype(F32)
            if x >= 1:
                at = 512 + f * 96 + (x - 1) * 32
                value = value + xh[at : at + 32, :].astype(F32)
            coarse[f, x] = value[:, 0:64]


def shifted(x, axis, by):
    size = lax.axis_size(axis)
    return lax.ppermute(x, axis, [(i, (i + by) % size) for i in range(size)])


def local_views(fields, home_slot):
    fields_rows = fields.reshape(1024, 4, 4, 128).transpose(0, 2, 1, 3).reshape(16384, 128)
    return fields_rows, home_slot.reshape(8, 128), home_slot.reshape(1, 1024)


def body(fields, jacobian, home_slot):
    ix, iy, iz = (lax.axis_index(axis) for axis in ("gx", "gy", "gz"))
    me = (ix * lax.axis_size("gy") + iy) * lax.axis_size("gz") + iz
    coords = jnp.stack([ix, iy, iz, me]).astype(jnp.int32)
    fields_rows, home_tile, home_row = local_views(fields, home_slot)
    payloads = pack(coords, home_tile, jacobian, fields_rows)
    arrived = [shifted(p, axis, by) for p, (axis, by) in zip(payloads, SHIFTS)]
    uniform_t = own_elements(coords, home_slot, home_row, fields_rows, jacobian)
    main_a, edge_a, main_c, edge_c, z_low, z_high = filters(coords, uniform_t, arrived)
    from_z_low = shifted(z_high, "gz", 1)
    from_z_high = shifted(z_low, "gz", -1)
    spread_a = jnp.asarray(depth_spread(126, 2))
    spread_c = jnp.asarray(depth_spread(61, 3))
    y_low, y_high = vmem_call(
        y_edges_kernel,
        [jax.ShapeDtypeStruct((224, 128), BF16)] * 2,
        [pltpu.VMEM((768, 128), F32), pltpu.VMEM((640, 128), F32)],
        "y_edges",
        edge_a, edge_c, from_z_low, from_z_high, spread_a, spread_c,
    )
    from_y_low = shifted(y_high, "gy", 1)
    from_y_high = shifted(y_low, "gy", -1)
    sum_a, sum_c, x_low, x_high = vmem_call(
        x_edges_kernel,
        [
            jax.ShapeDtypeStruct((48 * 64, 128), F32),
            jax.ShapeDtypeStruct((40 * 32, 128), F32),
            jax.ShapeDtypeStruct((896, 128), BF16),
            jax.ShapeDtypeStruct((896, 128), BF16),
        ],
        [pltpu.VMEM((224, 128), F32), pltpu.VMEM((224, 128), F32)],
        "x_edges",
        main_a, main_c, from_z_low, from_z_high, from_y_low, from_y_high, spread_a, spread_c,
    )
    from_x_low = shifted(x_high, "gx", 1)
    from_x_high = shifted(x_low, "gx", -1)
    mid, coarse = vmem_call(
        final_kernel,
        [
            jax.ShapeDtypeStruct((4, 8, 64, 128), F32),
            jax.ShapeDtypeStruct((4, 4, 32, 64), F32),
        ],
        [],
        "final",
        sum_a, sum_c, from_x_low, from_x_high,
    )
    return mid, coarse


def solution(mesh):
    placed = (P(("gx", "gy", "gz"), None, None), P(("gx", "gy", "gz"), None), P(("gx", "gy", "gz")))
    return jax.shard_map(
        body,
        mesh=mesh,
        in_specs=placed,
        out_specs=(P(None, "gx", "gy", "gz"), P(None, "gx", "gy", "gz")),
        check_vma=False,
    )
```

```python
import jax
import jax.numpy as jnp
import numpy as np
from jax import lax
from jax.experimental import pallas as pl
from jax.experimental.pallas import tpu as pltpu
from jax.sharding import PartitionSpec as P

F32 = jnp.float32
BF16 = jnp.bfloat16
MIB = 1024 * 1024

GLL_NODES = np.array(
    [
        -1.0,
        -0.8717401485096066,
        -0.5917001814331423,
        -0.2092992179024789,
        0.2092992179024789,
        0.5917001814331423,
        0.8717401485096066,
        1.0,
    ]
)

SHIFTS = (("gx", 1), ("gx", -1), ("gy", 1), ("gy", -1), ("gz", 1), ("gz", -1))
STEPS = (16, -16, 4, -4, 1, -1)
PAYLOAD = 336


def gll_basis():
    targets = -1.0 + (2.0 * np.arange(8) + 1.0) / 8.0
    table = np.ones((8, 8))
    for node in range(8):
        for other in range(8):
            if other != node:
                table[:, node] *= (targets - GLL_NODES[other]) / (
                    GLL_NODES[node] - GLL_NODES[other]
                )
    return table


def plain_sinc(points):
    return np.sin(np.pi * points) / (np.pi * points)


def lanczos_taps():
    offsets = np.arange(8) - 3.5
    values = plain_sinc(offsets / 2.0) * plain_sinc(offsets / 4.0)
    return values / np.sum(values)


TAPS = [float(v) for v in lanczos_taps()]


def bf16_of(table):
    return np.asarray(table, np.float32).astype(jnp.bfloat16)


def interp_table():
    basis = gll_basis()
    table = np.einsum("ia,jb,kc->kijabc", basis, basis, basis).reshape(512, 512)
    return bf16_of(table)


def point_order():
    table = np.zeros((8, 8, 8, 8, 8, 8))
    for i in range(8):
        for j in range(8):
            for k in range(8):
                table[k, i, j, i, j, k] = 1.0
    return bf16_of(table.reshape(512, 512))


def depth_tables():
    taps = lanczos_taps()
    low = taps.astype(np.float32).astype(jnp.bfloat16).astype(np.float64)
    first = np.zeros((256, 132))
    for column in range(132):
        for tap in range(8):
            z = 2 * (column - 2) - 3 + tap
            if 0 <= z < 256:
                first[z, column] = low[tap]
    second = np.zeros((132, 70))
    for column in range(70):
        for tap in range(8):
            z = 2 * (column - 3) - 3 + tap + 2
            if 0 <= z < 132:
                second[z, column] = taps[tap]
    out = []
    for place in range(3):
        mid = first.copy()
        if place == 0:
            mid[:, :2] = 0.0
        if place == 2:
            mid[:, 130:] = 0.0
        both = mid @ second
        if place == 0:
            both[:, :3] = 0.0
        if place == 2:
            both[:, 67:] = 0.0
        columns = np.zeros((256, 256))
        columns[:, :128] = mid[:, 2:130]
        columns[:, 128:192] = both[:, 3:67]
        columns[:, 192:194] = mid[:, :2]
        columns[:, 194:196] = mid[:, 130:]
        columns[:, 196:199] = both[:, :3]
        columns[:, 199:202] = both[:, 67:]
        out.append(columns.reshape(32, 8, 256).transpose(1, 0, 2).reshape(256, 256))
    return bf16_of(np.stack(out))


def nt(a, b):
    return lax.dot_general(a, b, (((1,), (1,)), ((), ())), preferred_element_type=F32)


def nn(a, b):
    return lax.dot_general(a, b, (((1,), (0,)), ((), ())), preferred_element_type=F32)


def tn(a, b):
    return lax.dot_general(a, b, (((0,), (0,)), ((), ())), preferred_element_type=F32)


def pack_kernel(coords, home, jac_hbm, fields, *rest):
    outs = rest[:6]
    spots, picker, jac, index_v, index_s, sem_jac, sem_index, sem_rows = rest[6:]
    copy_jac = pltpu.make_async_copy(jac_hbm, jac, sem_jac)
    copy_jac.start()
    me = coords[3]
    slots = home[...]
    diff = (slots >> 10) - me
    tag = (slots & 1023) + 1
    masks = jnp.concatenate([jnp.where(diff == step, 1.0, 0.0) for step in STEPS], axis=0)
    upper = jnp.where(
        lax.broadcasted_iota(jnp.int32, (128, 128), 0)
        <= lax.broadcasted_iota(jnp.int32, (128, 128), 1),
        1.0,
        0.0,
    ).astype(BF16)
    counts = nn(masks.astype(BF16), upper)
    spots[...] = jnp.where(diff == 0, tag - 1, 1024)
    row = lax.broadcasted_iota(jnp.int32, (8, 128), 0)
    slot_id = lax.broadcasted_iota(jnp.int32, (16, 128), 0).astype(F32)
    for d in range(6):
        count = counts[d * 8 : d * 8 + 8]
        total = jnp.broadcast_to(count[:, 127:128], (8, 128))
        rank = count - 1.0
        for r in range(7):
            rank = rank + jnp.where(row > r, jnp.broadcast_to(total[r : r + 1], (8, 128)), 0.0)
        rank = jnp.where(masks[d * 8 : d * 8 + 8] > 0.5, rank, -1.0)
        for r in range(8):
            hit = jnp.broadcast_to(rank[r : r + 1], (16, 128)) == slot_id
            picker[d * 16 : d * 16 + 16, r * 128 : r * 128 + 128] = jnp.where(
                hit, 1.0, 0.0
            ).astype(BF16)
    picker[96:128, :] = jnp.zeros((32, 1024), BF16)
    lane = lax.broadcasted_iota(jnp.int32, (8, 128), 1)
    pieces = []
    for r in range(8):
        own_tag = jnp.broadcast_to(tag[r : r + 1], (8, 128))
        elem = lane + r * 128
        value = jnp.where(
            row == 0,
            elem >> 5,
            jnp.where(row == 1, elem & 31, jnp.where(row == 2, own_tag >> 5, own_tag & 31)),
        )
        pieces.append(value.astype(F32).astype(BF16))
    values = jnp.concatenate(pieces, axis=1)
    found = nt(values, picker[...])
    index = found[0:1] * 32.0 + found[1:2]
    index_v[...] = jnp.broadcast_to(index, (8, 128)).astype(jnp.int32)
    copy_index = pltpu.make_async_copy(index_v, index_s, sem_index)
    copy_index.start()
    copy_index.wait()
    copies = []
    for d in range(6):
        for s in range(16):
            start = pl.multiple_of(index_s[0, d * 16 + s] * 16, 16)
            copy = pltpu.make_async_copy(
                fields.at[pl.ds(start, 16)], outs[d].at[pl.ds(s * 16, 16)], sem_rows.at[d]
            )
            copy.start()
    copy_jac.wait()
    jac_rows = nn(picker[...], jac[...]).astype(BF16)
    tag_lane = lax.broadcasted_iota(jnp.int32, (16, 128), 1)
    tag_row = lax.broadcasted_iota(jnp.int32, (16, 128), 0)
    tag_hi = jnp.broadcast_to(found[2:3], (16, 128))
    tag_lo = jnp.broadcast_to(found[3:4], (16, 128))
    both = jnp.where(tag_row == 0, tag_hi, jnp.where(tag_row == 1, tag_lo, 0.0))
    for d in range(6):
        for c in range(4):
            outs[d][256 + c * 16 : 272 + c * 16, :] = jac_rows[
                d * 16 : d * 16 + 16, c * 128 : c * 128 + 128
            ]
        outs[d][320:336, :] = jnp.where((tag_lane >> 4) == d, both, 0.0).astype(BF16)
    for d in range(6):
        pltpu.make_async_copy(
            fields.at[pl.ds(0, 256)], outs[d].at[pl.ds(0, 256)], sem_rows.at[d]
        ).wait()


def pack(coords, home, jac, fields_rows):
    vmem = pl.BlockSpec(memory_space=pltpu.VMEM)
    hbm = pl.BlockSpec(memory_space=pltpu.HBM)
    return pl.pallas_call(
        pack_kernel,
        out_shape=[jax.ShapeDtypeStruct((PAYLOAD, 128), BF16)] * 6
        + [jax.ShapeDtypeStruct((8, 128), jnp.int32)],
        in_specs=[pl.BlockSpec(memory_space=pltpu.SMEM), vmem, hbm, hbm],
        out_specs=[vmem] * 7,
        scratch_shapes=[
            pltpu.VMEM((128, 1024), BF16),
            pltpu.VMEM((1024, 512), BF16),
            pltpu.VMEM((8, 128), jnp.int32),
            pltpu.SMEM((8, 128), jnp.int32),
            pltpu.SemaphoreType.DMA,
            pltpu.SemaphoreType.DMA,
            pltpu.SemaphoreType.DMA((6,)),
        ],
        compiler_params=pltpu.CompilerParams(vmem_limit_bytes=60 * MIB),
        name="pack",
    )(coords, home, jac, fields_rows)


def own_kernel(spot_s, spot_v, fields, jac, table, order, out, rows, jac_t):
    def clear(e, carry):
        rows[pl.ds(pl.multiple_of(e * 512, 512), 512), :] = jnp.zeros((512, 128), F32)
        return carry

    lax.fori_loop(0, 32, clear, 0)

    def place(e, carry):
        for u in range(16):
            spot = spot_s[e >> 3, (e & 7) * 16 + u]
            rows[pl.ds(pl.multiple_of(spot * 16, 16), 16), :] = fields[
                pl.ds(pl.multiple_of(e * 256 + u * 16, 16), 16), :
            ].astype(F32)
        return carry

    lax.fori_loop(0, 64, place, 0)
    ordered = nt(order[...], jac[...]).astype(BF16)
    for c in range(4):
        ids = lax.broadcasted_iota(jnp.int32, (256, 128), 0) + c * 256
        hit = jnp.concatenate(
            [
                jnp.where(
                    ids == jnp.broadcast_to(spot_v[r : r + 1, :], (256, 128)), 1.0, 0.0
                ).astype(BF16)
                for r in range(8)
            ],
            axis=1,
        )
        jac_t[:, c * 256 : c * 256 + 256] = nt(ordered, hit)

    for n in range(4):
        for f in range(4):
            pieces = [
                rows[pl.ds(n * 4096 + c * 4 + f, 256, stride=16), :].astype(BF16)
                for c in range(4)
            ]
            values = nt(table[...], jnp.concatenate(pieces, axis=1))
            out[f * 512 : f * 512 + 512, n * 256 : n * 256 + 256] = (
                values * jac_t[:, n * 256 : n * 256 + 256]
            ).astype(BF16)


def own_elements(spots, fields_rows, jac):
    vmem = pl.BlockSpec(memory_space=pltpu.VMEM)
    return pl.pallas_call(
        own_kernel,
        out_shape=jax.ShapeDtypeStruct((2048, 1024), BF16),
        in_specs=[pl.BlockSpec(memory_space=pltpu.SMEM)] + [vmem] * 5,
        out_specs=vmem,
        scratch_shapes=[
            pltpu.VMEM((1025 * 16, 128), F32),
            pltpu.VMEM((512, 1024), F32),
        ],
        compiler_params=pltpu.CompilerParams(vmem_limit_bytes=28 * MIB),
        cost_estimate=pl.CostEstimate(
            flops=6_000_000_000, bytes_accessed=10_000_000, transcendentals=0
        ),
        name="own_elements",
    )(
        spots,
        spots,
        fields_rows,
        jac,
        jnp.asarray(interp_table()),
        jnp.asarray(point_order()),
    )


def halve(values, outputs, shift):
    results = []
    for o in range(outputs):
        total = None
        for tap in range(8):
            at = 2 * o + tap - shift
            if 0 <= at < len(values):
                term = TAPS[tap] * values[at]
                total = term if total is None else total + term
        results.append(total)
    return results


def filter_kernel(
    coords, uniform, a0, a1, a2, a3, a4, a5, table, order, depths,
    main_a, edge_a, main_c, edge_c, to_low, to_high,
    raw, arrived, depth, wide, ya, yb, mb, yc, pbz, pcz, sem,
):
    arrays = (a0, a1, a2, a3, a4, a5)
    one = lambda flag: jnp.where(flag, 1.0, 0.0)
    x_low = one(coords[0] > 0)
    x_high = one(coords[0] < 7)
    y_low = one(coords[1] > 0)
    y_high = one(coords[1] < 3)

    spot_z = coords[2]
    place = jnp.where(spot_z == 0, 0, jnp.where(spot_z == 3, 2, 1))
    copy = pltpu.make_async_copy(depths.at[place], depth, sem)
    copy.start()
    raw[1536:2048, :] = jnp.zeros((512, 128), F32)
    for d in range(6):
        raw[d * 256 : d * 256 + 256, :] = arrays[d][0:256, :].astype(F32)
    jac = jnp.concatenate(
        [
            jnp.concatenate(
                [arrays[d][256 + c * 16 : 272 + c * 16, :] for c in range(4)], axis=1
            )
            for d in range(6)
        ]
        + [jnp.zeros((32, 512), BF16)],
        axis=0,
    )
    jac_t = nt(order[...], jac)
    for f in range(4):
        pieces = [
            raw[pl.ds(c * 4 + f, 128, stride=16), :].astype(BF16) for c in range(4)
        ]
        values = nt(table[...], jnp.concatenate(pieces, axis=1))
        arrived[f * 512 : f * 512 + 512, :] = (values * jac_t).astype(BF16)
    def pads(q, carry):
        zero = jnp.zeros((24, 128), F32)
        base = pl.multiple_of(q * 176, 8)
        for ref in (ya, yb):
            ref[pl.ds(base, 24), :] = zero
            ref[pl.ds(base + 152, 24), :] = zero
        return carry

    lax.fori_loop(0, 48, pads, 0)

    def more_pads(q, carry):
        zero = jnp.zeros((16, 128), F32)
        base = pl.multiple_of(q * 112, 8)
        yc[pl.ds(base, 16), :] = zero
        yc[pl.ds(base + 96, 16), :] = zero
        return carry

    lax.fori_loop(0, 40, more_pads, 0)
    copy.wait()

    tags = jnp.zeros((8, 128), F32)
    for d in range(6):
        tags = tags + arrays[d][320:336, :].astype(F32)[0:8]
    spot = (tags[0:1] * 32.0 + tags[1:2]).astype(jnp.int32) - 1
    def quarter(t, carry):
        row = lax.broadcasted_iota(jnp.int32, (256, 128), 0)
        ids = jnp.where(row < 128, row, row + 384) + t * 128
        hit = jnp.where(ids == jnp.broadcast_to(spot, (256, 128)), 1.0, 0.0).astype(BF16)
        lane = lax.broadcasted_iota(jnp.int32, (64, 128), 1)
        odd = (lane & 32) != 0
        upper = (lane & 64) != 0
        for f in range(4):
            both = nt(arrived[f * 512 : f * 512 + 512, :], hit)
            pieces = [[], [], [], []]
            for ex in range(2):
                part = both[:, ex * 128 : ex * 128 + 128]
                own = uniform[
                    f * 512 : f * 512 + 512,
                    pl.ds(pl.multiple_of(ex * 512 + t * 128, 128), 128),
                ]
                total = part + own.astype(F32)
                regrouped = []
                for h in range(2):
                    v = [total[(h * 4 + k) * 64 : (h * 4 + k) * 64 + 64] for k in range(4)]
                    for a, b in ((0, 1), (2, 3)):
                        v[a], v[b] = (
                            jnp.where(odd, pltpu.roll(v[b], 32, 1), v[a]),
                            jnp.where(odd, v[b], pltpu.roll(v[a], 96, 1)),
                        )
                    for a, b in ((0, 2), (1, 3)):
                        v[a], v[b] = (
                            jnp.where(upper, pltpu.roll(v[b], 64, 1), v[a]),
                            jnp.where(upper, v[b], pltpu.roll(v[a], 64, 1)),
                        )
                    regrouped.append(v)
                for e in range(4):
                    pieces[e].append(
                        jnp.concatenate([regrouped[0][e], regrouped[1][e]], axis=1).astype(BF16)
                    )
            operand = jnp.concatenate([p for e in range(4) for p in pieces[e]], axis=0)
            wide[f * 512 : f * 512 + 512, :] = nn(operand, depth[...])

        for f in range(4):
            for column in range(8):
                ref = (ya, yb)[column % 2]
                values = [
                    wide[
                        f * 512 + (column // 2) * 128 + ex * 64 + i * 8 : f * 512
                        + (column // 2) * 128 + ex * 64 + i * 8 + 8,
                        (column % 2) * 128 : (column % 2) * 128 + 128,
                    ]
                    for ex in range(2)
                    for i in range(8)
                ]
                results = halve(values, 12, 7)
                for o in range(12):
                    value = results[o]
                    if o < 2:
                        value = value * x_low
                    if o >= 10:
                        value = value * x_high
                    at = (f * 12 + o) * 176 + 24 + (column // 2) * 8 + t * 32
                    ref[pl.ds(pl.multiple_of(at, 8), 8), :] = value
        return carry

    lax.fori_loop(0, 4, quarter, 0)

    def along_y(ref, base, count):
        total = None
        for tap in range(8):
            term = TAPS[tap] * ref[pl.ds(base + 5 + tap, count, stride=2), :]
            total = term if total is None else total + term
        low = total[0:8] * y_low
        high = total[count - 8 : count] * y_high
        return low, total[8 : count - 8], high

    def first(q, carry):
        low, middle, high = along_y(ya, q * 176, 80)
        edge_a[pl.ds(pl.multiple_of(q * 16, 16), 8), :] = low
        edge_a[pl.ds(pl.multiple_of(q * 16 + 8, 8), 8), :] = high
        main_a[pl.ds(pl.multiple_of(q * 64, 64), 64), :] = middle
        low, middle, high = along_y(yb, q * 176, 80)
        base = pl.multiple_of(q * 80, 16)
        mb[pl.ds(base, 8), :] = low
        mb[pl.ds(base + 8, 64), :] = middle
        mb[pl.ds(base + 72, 8), :] = high
        pbz[pl.ds(pl.multiple_of(q * 16, 16), 16), :] = jnp.concatenate(
            [low, high], axis=0
        ).astype(BF16)
        pbz[pl.ds(pl.multiple_of(768 + q * 64, 64), 64), :] = middle.astype(BF16)
        return carry

    lax.fori_loop(0, 48, first, 0)

    def along_x(v, carry):
        for f in range(4):
            values = [
                mb[pl.ds(pl.multiple_of((f * 12 + o) * 80 + v * 8, 8), 8), :]
                for o in range(12)
            ]
            results = halve(values, 10, 7)
            for o in range(10):
                value = results[o]
                if o < 3:
                    value = value * x_low
                if o >= 7:
                    value = value * x_high
                at = (f * 10 + o) * 112 + 16 + v * 8
                yc[pl.ds(pl.multiple_of(at, 8), 8), :] = value
        return carry

    lax.fori_loop(0, 10, along_x, 0)

    def second(q, carry):
        low, middle, high = along_y(yc, q * 112, 48)
        edge_c[pl.ds(pl.multiple_of(q * 16, 16), 8), :] = low
        edge_c[pl.ds(pl.multiple_of(q * 16 + 8, 8), 8), :] = high
        main_c[pl.ds(pl.multiple_of(q * 32, 32), 32), :] = middle
        pcz[pl.ds(pl.multiple_of(q * 16, 16), 16), :] = jnp.concatenate(
            [low, high], axis=0
        ).astype(BF16)
        pcz[pl.ds(pl.multiple_of(640 + q * 32, 32), 32), :] = middle.astype(BF16)
        return carry

    lax.fori_loop(0, 40, second, 0)
    row = lax.broadcasted_iota(jnp.int32, (16, 128), 0)
    lane = lax.broadcasted_iota(jnp.int32, (16, 128), 1)
    pick = lambda count, first_lane: jnp.where(
        (row < count) & (lane == row + first_lane), 1.0, 0.0
    ).astype(BF16)
    for ref, at_mid, at_coarse in ((to_low, 64, 68), (to_high, 66, 71)):
        ref[:, 0:3840] = nt(pick(2, at_mid), pbz[...])[0:8].astype(BF16)
        ref[:, 3840:5760] = nt(pick(3, at_coarse), pcz[...])[0:8].astype(BF16)


def filters(coords, uniform_t, arrived):
    vmem = pl.BlockSpec(memory_space=pltpu.VMEM)
    return pl.pallas_call(
        filter_kernel,
        out_shape=[
            jax.ShapeDtypeStruct((48 * 64, 128), F32),
            jax.ShapeDtypeStruct((48 * 16, 128), F32),
            jax.ShapeDtypeStruct((40 * 32, 128), F32),
            jax.ShapeDtypeStruct((40 * 16, 128), F32),
            jax.ShapeDtypeStruct((8, 5760), BF16),
            jax.ShapeDtypeStruct((8, 5760), BF16),
        ],
        in_specs=[pl.BlockSpec(memory_space=pltpu.SMEM)]
        + [vmem] * 9
        + [pl.BlockSpec(memory_space=pltpu.HBM)],
        out_specs=[vmem] * 6,
        scratch_shapes=[
            pltpu.VMEM((2048, 128), F32),
            pltpu.VMEM((2048, 128), BF16),
            pltpu.VMEM((256, 256), BF16),
            pltpu.VMEM((2048, 256), F32),
            pltpu.VMEM((48 * 176, 128), F32),
            pltpu.VMEM((48 * 176, 128), F32),
            pltpu.VMEM((48 * 80, 128), F32),
            pltpu.VMEM((40 * 112, 128), F32),
            pltpu.VMEM((3840, 128), BF16),
            pltpu.VMEM((1920, 128), BF16),
            pltpu.SemaphoreType.DMA,
        ],
        compiler_params=pltpu.CompilerParams(vmem_limit_bytes=32 * MIB),
        name="filters",
    )(
        coords,
        uniform_t,
        *arrived,
        jnp.asarray(interp_table()),
        jnp.asarray(point_order()),
        jnp.asarray(depth_tables()),
    )


def depth_spread(first_lane_high, count):
    table = np.zeros((16, 128))
    for r in range(count):
        table[r, r] = 1.0
        table[8 + r, first_lane_high + r] = 1.0
    return bf16_of(table)


def y_edges_kernel(edge_a, edge_c, from_low, from_high, spread_a, spread_c,
                   to_low, to_high, sa, sc):
    lanes = jnp.concatenate([from_low[:, 0:768], from_high[:, 0:768]], axis=0)
    sa[...] = edge_a[...] + tn(lanes, spread_a[...])
    lanes = jnp.concatenate([from_low[:, 3840:4480], from_high[:, 3840:4480]], axis=0)
    sc[...] = edge_c[...] + tn(lanes, spread_c[...])
    for ref, ra, rc in ((to_low, 6, 5), (to_high, 8, 8)):
        for r in range(2):
            ref[r * 48 : r * 48 + 48, :] = sa[pl.ds(ra + r, 48, stride=16), :].astype(BF16)
        tail = [sc[pl.ds(rc + r, 40, stride=16), :] for r in range(3)] + [jnp.zeros((8, 128), F32)]
        ref[96:224, :] = jnp.concatenate(tail, axis=0).astype(BF16)


def vmem_call(kernel, out_shape, scratch, name, *operands, **options):
    vmem = pl.BlockSpec(memory_space=pltpu.VMEM)
    single = not isinstance(out_shape, list)
    return pl.pallas_call(
        kernel,
        out_shape=out_shape,
        in_specs=[vmem] * len(operands),
        out_specs=vmem if single else [vmem] * len(out_shape),
        scratch_shapes=scratch,
        compiler_params=pltpu.CompilerParams(vmem_limit_bytes=12 * MIB),
        name=name,
        **options,
    )(*operands)


def x_edges_kernel(main_a, main_c, zl, zh, yl, yh, spread_a, spread_c,
                   sa, sc, to_low, to_high, fl, fh):
    lanes = jnp.concatenate([zl[:, 768:3840], zh[:, 768:3840]], axis=0)
    sa[...] = main_a[...] + tn(lanes, spread_a[...])
    lanes = jnp.concatenate([zl[:, 4480:5760], zh[:, 4480:5760]], axis=0)
    sc[...] = main_c[...] + tn(lanes, spread_c[...])
    fl[...] = yl[...].astype(F32)
    fh[...] = yh[...].astype(F32)
    for r in range(2):
        sa[pl.ds(r, 48, stride=64), :] += fl[r * 48 : r * 48 + 48, :]
        sa[pl.ds(62 + r, 48, stride=64), :] += fh[r * 48 : r * 48 + 48, :]
    for r in range(3):
        sc[pl.ds(r, 40, stride=32), :] += fl[96 + r * 40 : 136 + r * 40, :]
        sc[pl.ds(29 + r, 40, stride=32), :] += fh[96 + r * 40 : 136 + r * 40, :]
    for ref, xa, xc in ((to_low, 0, 0), (to_high, 10, 7)):
        for f in range(4):
            ref[f * 128 : f * 128 + 128, :] = sa[
                (f * 12 + xa) * 64 : (f * 12 + xa) * 64 + 128, :
            ].astype(BF16)
            ref[512 + f * 96 : 608 + f * 96, :] = sc[
                (f * 10 + xc) * 32 : (f * 10 + xc) * 32 + 96, :
            ].astype(BF16)


def final_kernel(sa, sc, xl, xh, mid, coarse):
    for f in range(4):
        for x in range(8):
            base = (f * 12 + x + 2) * 64
            value = sa[base : base + 64, :]
            if x < 2:
                value = value + xl[f * 128 + x * 64 : f * 128 + x * 64 + 64, :].astype(F32)
            if x >= 6:
                at = f * 128 + (x - 6) * 64
                value = value + xh[at : at + 64, :].astype(F32)
            mid[f, x] = value
        for x in range(4):
            base = (f * 10 + x + 3) * 32
            value = sc[base : base + 32, :]
            if x < 3:
                at = 512 + f * 96 + x * 32
                value = value + xl[at : at + 32, :].astype(F32)
            if x >= 1:
                at = 512 + f * 96 + (x - 1) * 32
                value = value + xh[at : at + 32, :].astype(F32)
            coarse[f, x] = value[:, 0:64]


def shifted(x, axis, by):
    size = lax.axis_size(axis)
    return lax.ppermute(x, axis, [(i, (i + by) % size) for i in range(size)])


def local_views(fields, home_slot):
    fields_rows = fields.reshape(1024, 4, 4, 128).transpose(0, 2, 1, 3).reshape(16384, 128)
    return fields_rows, home_slot.reshape(8, 128)


def body(fields, jacobian, home_slot):
    ix, iy, iz = (lax.axis_index(axis) for axis in ("gx", "gy", "gz"))
    me = (ix * lax.axis_size("gy") + iy) * lax.axis_size("gz") + iz
    coords = jnp.stack([ix, iy, iz, me]).astype(jnp.int32)
    fields_rows, home_tile = local_views(fields, home_slot)
    *payloads, spots = pack(coords, home_tile, jacobian, fields_rows)
    arrived = [shifted(p, axis, by) for p, (axis, by) in zip(payloads, SHIFTS)]
    uniform_t = own_elements(spots, fields_rows, jacobian)
    main_a, edge_a, main_c, edge_c, z_low, z_high = filters(coords, uniform_t, arrived)
    from_z_low = shifted(z_high, "gz", 1)
    from_z_high = shifted(z_low, "gz", -1)
    spread_a = jnp.asarray(depth_spread(126, 2))
    spread_c = jnp.asarray(depth_spread(61, 3))
    y_low, y_high = vmem_call(
        y_edges_kernel,
        [jax.ShapeDtypeStruct((224, 128), BF16)] * 2,
        [pltpu.VMEM((768, 128), F32), pltpu.VMEM((640, 128), F32)],
        "y_edges",
        edge_a, edge_c, from_z_low, from_z_high, spread_a, spread_c,
    )
    from_y_low = shifted(y_high, "gy", 1)
    from_y_high = shifted(y_low, "gy", -1)
    sum_a, sum_c, x_low, x_high = vmem_call(
        x_edges_kernel,
        [
            jax.ShapeDtypeStruct((48 * 64, 128), F32),
            jax.ShapeDtypeStruct((40 * 32, 128), F32),
            jax.ShapeDtypeStruct((896, 128), BF16),
            jax.ShapeDtypeStruct((896, 128), BF16),
        ],
        [pltpu.VMEM((224, 128), F32), pltpu.VMEM((224, 128), F32)],
        "x_edges",
        main_a, main_c, from_z_low, from_z_high, from_y_low, from_y_high, spread_a, spread_c,
    )
    from_x_low = shifted(x_high, "gx", 1)
    from_x_high = shifted(x_low, "gx", -1)
    mid, coarse = vmem_call(
        final_kernel,
        [
            jax.ShapeDtypeStruct((4, 8, 64, 128), F32),
            jax.ShapeDtypeStruct((4, 4, 32, 64), F32),
        ],
        [],
        "final",
        sum_a, sum_c, from_x_low, from_x_high,
    )
    return mid, coarse


def solution(mesh):
    placed = (P(("gx", "gy", "gz"), None, None), P(("gx", "gy", "gz"), None), P(("gx", "gy", "gz")))
    return jax.shard_map(
        body,
        mesh=mesh,
        in_specs=placed,
        out_specs=(P(None, "gx", "gy", "gz"), P(None, "gx", "gy", "gz")),
        check_vma=False,
    )
```

```python
import jax
import jax.numpy as jnp
import numpy as np
from jax import lax
from jax.experimental import pallas as pl
from jax.experimental.pallas import tpu as pltpu
from jax.sharding import PartitionSpec as P

F32 = jnp.float32
BF16 = jnp.bfloat16
MIB = 1024 * 1024

GLL_NODES = np.array(
    [
        -1.0,
        -0.8717401485096066,
        -0.5917001814331423,
        -0.2092992179024789,
        0.2092992179024789,
        0.5917001814331423,
        0.8717401485096066,
        1.0,
    ]
)

SHIFTS = (("gx", 1), ("gx", -1), ("gy", 1), ("gy", -1), ("gz", 1), ("gz", -1))
STEPS = (16, -16, 4, -4, 1, -1)
PAYLOAD = 336


def gll_basis():
    targets = -1.0 + (2.0 * np.arange(8) + 1.0) / 8.0
    table = np.ones((8, 8))
    for node in range(8):
        for other in range(8):
            if other != node:
                table[:, node] *= (targets - GLL_NODES[other]) / (
                    GLL_NODES[node] - GLL_NODES[other]
                )
    return table


def plain_sinc(points):
    return np.sin(np.pi * points) / (np.pi * points)


def lanczos_taps():
    offsets = np.arange(8) - 3.5
    values = plain_sinc(offsets / 2.0) * plain_sinc(offsets / 4.0)
    return values / np.sum(values)


TAPS = [float(v) for v in lanczos_taps()]


def bf16_of(table):
    return np.asarray(table, np.float32).astype(jnp.bfloat16)


def interp_table():
    basis = gll_basis()
    table = np.einsum("ia,jb,kc->kijabc", basis, basis, basis).reshape(512, 512)
    return bf16_of(table)


def point_order():
    table = np.zeros((8, 8, 8, 8, 8, 8))
    for i in range(8):
        for j in range(8):
            for k in range(8):
                table[k, i, j, i, j, k] = 1.0
    return bf16_of(table.reshape(512, 512))


def depth_tables():
    taps = lanczos_taps()
    low = taps.astype(np.float32).astype(jnp.bfloat16).astype(np.float64)
    first = np.zeros((256, 132))
    for column in range(132):
        for tap in range(8):
            z = 2 * (column - 2) - 3 + tap
            if 0 <= z < 256:
                first[z, column] = low[tap]
    second = np.zeros((132, 70))
    for column in range(70):
        for tap in range(8):
            z = 2 * (column - 3) - 3 + tap + 2
            if 0 <= z < 132:
                second[z, column] = taps[tap]
    out = []
    for place in range(3):
        mid = first.copy()
        if place == 0:
            mid[:, :2] = 0.0
        if place == 2:
            mid[:, 130:] = 0.0
        both = mid @ second
        if place == 0:
            both[:, :3] = 0.0
        if place == 2:
            both[:, 67:] = 0.0
        columns = np.zeros((256, 256))
        columns[:, :128] = mid[:, 2:130]
        columns[:, 128:192] = both[:, 3:67]
        columns[:, 192:194] = mid[:, :2]
        columns[:, 194:196] = mid[:, 130:]
        columns[:, 196:199] = both[:, :3]
        columns[:, 199:202] = both[:, 67:]
        out.append(columns.reshape(32, 8, 256).transpose(1, 0, 2).reshape(256, 256))
    return bf16_of(np.stack(out))


def nt(a, b):
    return lax.dot_general(a, b, (((1,), (1,)), ((), ())), preferred_element_type=F32)


def nn(a, b):
    return lax.dot_general(a, b, (((1,), (0,)), ((), ())), preferred_element_type=F32)


def tn(a, b):
    return lax.dot_general(a, b, (((0,), (0,)), ((), ())), preferred_element_type=F32)


def pack_kernel(coords, home, jac_hbm, fields, *rest):
    outs = rest[:6]
    spots, picker, jac, index_v, index_s, sem_jac, sem_index, sem_rows = rest[6:]
    copy_jac = pltpu.make_async_copy(jac_hbm, jac, sem_jac)
    copy_jac.start()
    me = coords[3]
    slots = home[...]
    diff = (slots >> 10) - me
    tag = (slots & 1023) + 1
    masks = jnp.concatenate([jnp.where(diff == step, 1.0, 0.0) for step in STEPS], axis=0)
    upper = jnp.where(
        lax.broadcasted_iota(jnp.int32, (128, 128), 0)
        <= lax.broadcasted_iota(jnp.int32, (128, 128), 1),
        1.0,
        0.0,
    ).astype(BF16)
    counts = nn(masks.astype(BF16), upper)
    spots[...] = jnp.where(diff == 0, tag - 1, 1024)
    row = lax.broadcasted_iota(jnp.int32, (8, 128), 0)
    slot_id = lax.broadcasted_iota(jnp.int32, (16, 128), 0).astype(F32)
    for d in range(6):
        count = counts[d * 8 : d * 8 + 8]
        total = jnp.broadcast_to(count[:, 127:128], (8, 128))
        rank = count - 1.0
        for r in range(7):
            rank = rank + jnp.where(row > r, jnp.broadcast_to(total[r : r + 1], (8, 128)), 0.0)
        rank = jnp.where(masks[d * 8 : d * 8 + 8] > 0.5, rank, -1.0)
        for r in range(8):
            hit = jnp.broadcast_to(rank[r : r + 1], (16, 128)) == slot_id
            picker[d * 16 : d * 16 + 16, r * 128 : r * 128 + 128] = jnp.where(
                hit, 1.0, 0.0
            ).astype(BF16)
    picker[96:128, :] = jnp.zeros((32, 1024), BF16)
    lane = lax.broadcasted_iota(jnp.int32, (8, 128), 1)
    pieces = []
    for r in range(8):
        own_tag = jnp.broadcast_to(tag[r : r + 1], (8, 128))
        elem = lane + r * 128
        value = jnp.where(
            row == 0,
            elem >> 5,
            jnp.where(row == 1, elem & 31, jnp.where(row == 2, own_tag >> 5, own_tag & 31)),
        )
        pieces.append(value.astype(F32).astype(BF16))
    values = jnp.concatenate(pieces, axis=1)
    found = nt(values, picker[...])
    index = found[0:1] * 32.0 + found[1:2]
    index_v[...] = jnp.broadcast_to(index, (8, 128)).astype(jnp.int32)
    copy_index = pltpu.make_async_copy(index_v, index_s, sem_index)
    copy_index.start()
    copy_index.wait()
    copies = []
    for d in range(6):
        for s in range(16):
            start = pl.multiple_of(index_s[0, d * 16 + s] * 16, 16)
            copy = pltpu.make_async_copy(
                fields.at[pl.ds(start, 16)], outs[d].at[pl.ds(s * 16, 16)], sem_rows.at[d]
            )
            copy.start()
    copy_jac.wait()
    jac_rows = nn(picker[...], jac[...]).astype(BF16)
    tag_lane = lax.broadcasted_iota(jnp.int32, (16, 128), 1)
    tag_row = lax.broadcasted_iota(jnp.int32, (16, 128), 0)
    tag_hi = jnp.broadcast_to(found[2:3], (16, 128))
    tag_lo = jnp.broadcast_to(found[3:4], (16, 128))
    both = jnp.where(tag_row == 0, tag_hi, jnp.where(tag_row == 1, tag_lo, 0.0))
    for d in range(6):
        for c in range(4):
            outs[d][256 + c * 16 : 272 + c * 16, :] = jac_rows[
                d * 16 : d * 16 + 16, c * 128 : c * 128 + 128
            ]
        outs[d][320:336, :] = jnp.where((tag_lane >> 4) == d, both, 0.0).astype(BF16)
    for d in range(6):
        pltpu.make_async_copy(
            fields.at[pl.ds(0, 256)], outs[d].at[pl.ds(0, 256)], sem_rows.at[d]
        ).wait()


def pack(coords, home, jac, fields_rows):
    vmem = pl.BlockSpec(memory_space=pltpu.VMEM)
    hbm = pl.BlockSpec(memory_space=pltpu.HBM)
    return pl.pallas_call(
        pack_kernel,
        out_shape=[jax.ShapeDtypeStruct((PAYLOAD, 128), BF16)] * 6
        + [jax.ShapeDtypeStruct((8, 128), jnp.int32)],
        in_specs=[pl.BlockSpec(memory_space=pltpu.SMEM), vmem, hbm, hbm],
        out_specs=[vmem] * 7,
        scratch_shapes=[
            pltpu.VMEM((128, 1024), BF16),
            pltpu.VMEM((1024, 512), BF16),
            pltpu.VMEM((8, 128), jnp.int32),
            pltpu.SMEM((8, 128), jnp.int32),
            pltpu.SemaphoreType.DMA,
            pltpu.SemaphoreType.DMA,
            pltpu.SemaphoreType.DMA((6,)),
        ],
        compiler_params=pltpu.CompilerParams(vmem_limit_bytes=60 * MIB),
        name="pack",
    )(coords, home, jac, fields_rows)


def local_call(kernel, outs, specs, operands, name, out_specs=None, scratch=(),
               aliases=None, flops=0, limit=16):
    vmem = pl.BlockSpec(memory_space=pltpu.VMEM)
    return pl.pallas_call(
        kernel,
        out_shape=list(outs),
        in_specs=specs,
        out_specs=out_specs or [vmem] * len(outs),
        scratch_shapes=list(scratch),
        input_output_aliases=aliases or {},
        compiler_params=pltpu.CompilerParams(vmem_limit_bytes=limit * MIB),
        cost_estimate=pl.CostEstimate(
            flops=flops, bytes_accessed=1_000_000, transcendentals=0
        ),
        name=name,
    )(*operands)


def jacobian_kernel(spots, jac, order, jac_t):
    ordered = nt(order[...], jac[...]).astype(BF16)
    for c in range(4):
        ids = lax.broadcasted_iota(jnp.int32, (256, 128), 0) + c * 256
        hit = jnp.concatenate(
            [
                jnp.where(
                    ids == jnp.broadcast_to(spots[r : r + 1, :], (256, 128)), 1.0, 0.0
                ).astype(BF16)
                for r in range(8)
            ],
            axis=1,
        )
        jac_t[:, c * 256 : c * 256 + 256] = nt(ordered, hit)


def place_kernel(spots, fields, rows):
    def place(e, carry):
        targets = [spots[e * 32 + u] for u in range(32)]
        values = [fields[e * 32 + u] for u in range(32)]
        for u in range(32):
            rows[targets[u]] = values[u].astype(F32)
        return carry

    lax.fori_loop(0, 32, place, 0)


def arrive_kernel(a0, a1, a2, a3, a4, a5, order, jac_in, rows_in, jac_t, rows,
                  staged, spot_v, spot_s, sem, sem_rows):
    arrays = (a0, a1, a2, a3, a4, a5)
    tags = jnp.zeros((8, 128), F32)
    for d in range(6):
        tags = tags + arrays[d][320:336, :].astype(F32)[0:8]
    spot = (tags[0:1] * 32.0 + tags[1:2]).astype(jnp.int32) - 1
    spare = lax.broadcasted_iota(jnp.int32, (1, 128), 1) + 1024
    spot_v[...] = jnp.broadcast_to(jnp.where(spot < 0, spare, spot), (8, 128))
    copy = pltpu.make_async_copy(spot_v, spot_s, sem)
    copy.start()
    jac = jnp.concatenate(
        [
            jnp.concatenate(
                [arrays[d][256 + c * 16 : 272 + c * 16, :] for c in range(4)], axis=1
            )
            for d in range(6)
        ]
        + [jnp.zeros((32, 512), BF16)],
        axis=0,
    )
    ordered = nt(order[...], jac).astype(BF16)
    for c in range(4):
        ids = lax.broadcasted_iota(jnp.int32, (256, 128), 0) + c * 256
        hit = jnp.where(ids == jnp.broadcast_to(spot, (256, 128)), 1.0, 0.0).astype(BF16)
        jac_t[:, c * 256 : c * 256 + 256] = jac_in[:, c * 256 : c * 256 + 256] + nt(ordered, hit)
    for d in range(6):
        for e in range(16):
            staged[d * 16 + e] = arrays[d][e * 16 : e * 16 + 16, :].astype(F32)
    copy.wait()
    for e in range(96):
        pltpu.make_async_copy(staged.at[e], rows.at[spot_s[0, e]], sem_rows).start()
    pltpu.make_async_copy(staged, rows.at[pl.ds(0, 96)], sem_rows).wait()


def fields_kernel(rows, jac_t, table, u0, u1, u2, u3):
    for f, out in enumerate((u0, u1, u2, u3)):
        for n in range(4):
            pieces = [
                rows[pl.ds(n * 4096 + c * 4 + f, 256, stride=16), :].astype(BF16)
                for c in range(4)
            ]
            values = nt(table[...], jnp.concatenate(pieces, axis=1))
            out[:, n * 256 : n * 256 + 256] = (
                values * jac_t[:, n * 256 : n * 256 + 256]
            ).astype(BF16)


def own_elements(spots, fields_elems, jac):
    vmem = pl.BlockSpec(memory_space=pltpu.VMEM)
    smem = pl.BlockSpec(memory_space=pltpu.SMEM)
    order = jnp.asarray(point_order())
    [jac_t] = local_call(
        jacobian_kernel,
        [jax.ShapeDtypeStruct((512, 1024), F32)],
        [vmem] * 3,
        [spots, jac, order],
        "jacobians",
        flops=2_000_000_000,
    )
    [rows] = local_call(
        place_kernel,
        [jax.ShapeDtypeStruct((1152, 16, 128), F32)],
        [smem, vmem],
        [spots.reshape(1024), fields_elems],
        "place",
        flops=2_000_000_000,
    )
    return rows, jac_t


def all_elements(rows, jac_t, arrived):
    vmem = pl.BlockSpec(memory_space=pltpu.VMEM)
    anywhere = pl.BlockSpec(memory_space=pl.ANY)
    jac_t, rows = local_call(
        arrive_kernel,
        [
            jax.ShapeDtypeStruct((512, 1024), F32),
            jax.ShapeDtypeStruct((1152, 16, 128), F32),
        ],
        [vmem] * 8 + [anywhere],
        [*arrived, jnp.asarray(point_order()), jac_t, rows],
        "arrive",
        out_specs=[vmem, anywhere],
        scratch=[
            pltpu.VMEM((96, 16, 128), F32),
            pltpu.VMEM((8, 128), jnp.int32),
            pltpu.SMEM((8, 128), jnp.int32),
            pltpu.SemaphoreType.DMA,
            pltpu.SemaphoreType.DMA,
        ],
        aliases={8: 1},
    )
    return local_call(
        fields_kernel,
        [jax.ShapeDtypeStruct((512, 1024), BF16)] * 4,
        [vmem] * 3,
        [rows.reshape(1152 * 16, 128), jac_t, jnp.asarray(interp_table())],
        "fields",
        limit=24,
    )


def halve(values, outputs, shift):
    results = []
    for o in range(outputs):
        total = None
        for tap in range(4):
            pair = [
                values[at]
                for at in (2 * o + tap - shift, 2 * o + 7 - tap - shift)
                if 0 <= at < len(values)
            ]
            if pair:
                term = TAPS[tap] * (pair[0] + pair[1] if len(pair) == 2 else pair[0])
                total = term if total is None else total + term
        results.append(total)
    return results


def along_y(ref, base, count, y_low, y_high):
    total = None
    for tap in range(4):
        pair = (
            ref[pl.ds(base + 5 + tap, count, stride=2), :]
            + ref[pl.ds(base + 12 - tap, count, stride=2), :]
        )
        total = TAPS[tap] * pair if total is None else total + TAPS[tap] * pair
    low = total[0:8] * y_low
    high = total[count - 8 : count] * y_high
    return low, total[8 : count - 8], high


def first_y_kernel(coords, ya, main_a, edge_a):
    y_low = jnp.where(coords[1] > 0, 1.0, 0.0)
    y_high = jnp.where(coords[1] < 3, 1.0, 0.0)

    def first(q, carry):
        low, middle, high = along_y(ya, q * 176, 80, y_low, y_high)
        edge_a[pl.ds(pl.multiple_of(q * 16, 16), 8), :] = low
        edge_a[pl.ds(pl.multiple_of(q * 16 + 8, 8), 8), :] = high
        main_a[pl.ds(pl.multiple_of(q * 64, 64), 64), :] = middle
        return carry

    lax.fori_loop(0, 48, first, 0)


def filter_kernel(
    coords, u0, u1, u2, u3, depths,
    ya, main_c, edge_c, to_low, to_high,
    depth, wide, yb, mb, yc, pbz, pcz, sem,
):
    one = lambda flag: jnp.where(flag, 1.0, 0.0)
    x_low = one(coords[0] > 0)
    x_high = one(coords[0] < 7)
    y_low = one(coords[1] > 0)
    y_high = one(coords[1] < 3)

    spot_z = coords[2]
    place = jnp.where(spot_z == 0, 0, jnp.where(spot_z == 3, 2, 1))
    copy = pltpu.make_async_copy(depths.at[place], depth, sem)
    copy.start()
    def pads(q, carry):
        zero = jnp.zeros((24, 128), F32)
        base = pl.multiple_of(q * 176, 8)
        for ref in (ya, yb):
            ref[pl.ds(base, 24), :] = zero
            ref[pl.ds(base + 152, 24), :] = zero
        return carry

    lax.fori_loop(0, 48, pads, 0)

    def more_pads(q, carry):
        zero = jnp.zeros((16, 128), F32)
        base = pl.multiple_of(q * 112, 8)
        yc[pl.ds(base, 16), :] = zero
        yc[pl.ds(base + 96, 16), :] = zero
        return carry

    lax.fori_loop(0, 40, more_pads, 0)
    copy.wait()

    def quarter(t, carry):
        lane = lax.broadcasted_iota(jnp.int32, (64, 128), 1)
        odd = (lane & 32) != 0
        upper = (lane & 64) != 0
        for f in range(4):
            pieces = [[], [], [], []]
            for ex in range(2):
                total = (u0, u1, u2, u3)[f][
                    :, pl.ds(pl.multiple_of(ex * 512 + t * 128, 128), 128)
                ]
                regrouped = []
                for h in range(2):
                    v = [total[(h * 4 + k) * 64 : (h * 4 + k) * 64 + 64] for k in range(4)]
                    for a, b in ((0, 1), (2, 3)):
                        v[a], v[b] = (
                            jnp.where(odd, pltpu.roll(v[b], 32, 1), v[a]),
                            jnp.where(odd, v[b], pltpu.roll(v[a], 96, 1)),
                        )
                    for a, b in ((0, 2), (1, 3)):
                        v[a], v[b] = (
                            jnp.where(upper, pltpu.roll(v[b], 64, 1), v[a]),
                            jnp.where(upper, v[b], pltpu.roll(v[a], 64, 1)),
                        )
                    regrouped.append(v)
                for e in range(4):
                    pieces[e].append(
                        jnp.concatenate([regrouped[0][e], regrouped[1][e]], axis=1)
                    )
            operand = jnp.concatenate([p for e in range(4) for p in pieces[e]], axis=0)
            wide[f * 512 : f * 512 + 512, :] = nn(operand, depth[...])

        for f in range(4):
            for column in range(8):
                ref = (ya, yb)[column % 2]
                values = [
                    wide[
                        f * 512 + (column // 2) * 128 + ex * 64 + i * 8 : f * 512
                        + (column // 2) * 128 + ex * 64 + i * 8 + 8,
                        (column % 2) * 128 : (column % 2) * 128 + 128,
                    ]
                    for ex in range(2)
                    for i in range(8)
                ]
                results = halve(values, 12, 7)
                for o in range(12):
                    value = results[o]
                    if o < 2:
                        value = value * x_low
                    if o >= 10:
                        value = value * x_high
                    at = (f * 12 + o) * 176 + 24 + (column // 2) * 8 + t * 32
                    ref[pl.ds(pl.multiple_of(at, 8), 8), :] = value
        return carry

    lax.fori_loop(0, 4, quarter, 0)

    def first(q, carry):
        low, middle, high = along_y(yb, q * 176, 80, y_low, y_high)
        base = pl.multiple_of(q * 80, 16)
        mb[pl.ds(base, 8), :] = low
        mb[pl.ds(base + 8, 64), :] = middle
        mb[pl.ds(base + 72, 8), :] = high
        pbz[pl.ds(pl.multiple_of(q * 16, 16), 16), :] = jnp.concatenate(
            [low, high], axis=0
        ).astype(BF16)
        pbz[pl.ds(pl.multiple_of(768 + q * 64, 64), 64), :] = middle.astype(BF16)
        return carry

    lax.fori_loop(0, 48, first, 0)

    def along_x(v, carry):
        for f in range(4):
            values = [
                mb[pl.ds(pl.multiple_of((f * 12 + o) * 80 + v * 8, 8), 8), :]
                for o in range(12)
            ]
            results = halve(values, 10, 7)
            for o in range(10):
                value = results[o]
                if o < 3:
                    value = value * x_low
                if o >= 7:
                    value = value * x_high
                at = (f * 10 + o) * 112 + 16 + v * 8
                yc[pl.ds(pl.multiple_of(at, 8), 8), :] = value
        return carry

    lax.fori_loop(0, 10, along_x, 0)

    def second(q, carry):
        low, middle, high = along_y(yc, q * 112, 48, y_low, y_high)
        edge_c[pl.ds(pl.multiple_of(q * 16, 16), 8), :] = low
        edge_c[pl.ds(pl.multiple_of(q * 16 + 8, 8), 8), :] = high
        main_c[pl.ds(pl.multiple_of(q * 32, 32), 32), :] = middle
        pcz[pl.ds(pl.multiple_of(q * 16, 16), 16), :] = jnp.concatenate(
            [low, high], axis=0
        ).astype(BF16)
        pcz[pl.ds(pl.multiple_of(640 + q * 32, 32), 32), :] = middle.astype(BF16)
        return carry

    lax.fori_loop(0, 40, second, 0)
    row = lax.broadcasted_iota(jnp.int32, (16, 128), 0)
    lane = lax.broadcasted_iota(jnp.int32, (16, 128), 1)

    def pick(count, low_lane, high_lane):
        low = (row < count) & (lane == row + low_lane)
        high = (row >= 8) & (row < 8 + count) & (lane == row - 8 + high_lane)
        return jnp.where(low | high, 1.0, 0.0).astype(BF16)

    mid = nt(pick(2, 64, 66), pbz[...])
    coarse = nt(pick(3, 68, 71), pcz[...])
    for ref, at in ((to_low, 0), (to_high, 8)):
        ref[:, 0:3840] = mid[at : at + 8].astype(BF16)
        ref[:, 3840:5760] = coarse[at : at + 8].astype(BF16)


def filters(coords, uniform_t):
    vmem = pl.BlockSpec(memory_space=pltpu.VMEM)
    smem = pl.BlockSpec(memory_space=pltpu.SMEM)
    return local_call(
        filter_kernel,
        [
            jax.ShapeDtypeStruct((48 * 176, 128), F32),
            jax.ShapeDtypeStruct((40 * 32, 128), F32),
            jax.ShapeDtypeStruct((40 * 16, 128), F32),
            jax.ShapeDtypeStruct((8, 5760), BF16),
            jax.ShapeDtypeStruct((8, 5760), BF16),
        ],
        [smem] + [vmem] * 4 + [pl.BlockSpec(memory_space=pltpu.HBM)],
        [coords, *uniform_t, jnp.asarray(depth_tables())],
        "filters",
        scratch=[
            pltpu.VMEM((256, 256), BF16),
            pltpu.VMEM((2048, 256), F32),
            pltpu.VMEM((48 * 176, 128), F32),
            pltpu.VMEM((48 * 80, 128), F32),
            pltpu.VMEM((40 * 112, 128), F32),
            pltpu.VMEM((3840, 128), BF16),
            pltpu.VMEM((1920, 128), BF16),
            pltpu.SemaphoreType.DMA,
        ],
        limit=32,
    )


def first_y(coords, ya):
    vmem = pl.BlockSpec(memory_space=pltpu.VMEM)
    return local_call(
        first_y_kernel,
        [jax.ShapeDtypeStruct((48 * 64, 128), F32), jax.ShapeDtypeStruct((48 * 16, 128), F32)],
        [pl.BlockSpec(memory_space=pltpu.SMEM), vmem],
        [coords, ya],
        "first_y",
        flops=2_000_000_000,
    )


def depth_spread(first_lane_high, count):
    table = np.zeros((16, 128))
    for r in range(count):
        table[r, r] = 1.0
        table[8 + r, first_lane_high + r] = 1.0
    return bf16_of(table)


def y_edges_kernel(edge_a, edge_c, from_low, from_high, spread_a, spread_c,
                   to_low, to_high, sa, sc):
    lanes = jnp.concatenate([from_low[:, 0:768], from_high[:, 0:768]], axis=0)
    sa[...] = edge_a[...] + tn(lanes, spread_a[...])
    lanes = jnp.concatenate([from_low[:, 3840:4480], from_high[:, 3840:4480]], axis=0)
    sc[...] = edge_c[...] + tn(lanes, spread_c[...])
    for ref, ra, rc in ((to_low, 6, 5), (to_high, 8, 8)):
        for r in range(2):
            ref[r * 48 : r * 48 + 48, :] = sa[pl.ds(ra + r, 48, stride=16), :].astype(BF16)
        tail = [sc[pl.ds(rc + r, 40, stride=16), :] for r in range(3)] + [jnp.zeros((8, 128), F32)]
        ref[96:224, :] = jnp.concatenate(tail, axis=0).astype(BF16)


def vmem_call(kernel, out_shape, scratch, name, *operands, **options):
    vmem = pl.BlockSpec(memory_space=pltpu.VMEM)
    single = not isinstance(out_shape, list)
    return pl.pallas_call(
        kernel,
        out_shape=out_shape,
        in_specs=[vmem] * len(operands),
        out_specs=vmem if single else [vmem] * len(out_shape),
        scratch_shapes=scratch,
        compiler_params=pltpu.CompilerParams(vmem_limit_bytes=12 * MIB),
        name=name,
        **options,
    )(*operands)


def z_main_kernel(main_a, main_c, zl, zh, spread_a, spread_c, sa, sc):
    lanes = jnp.concatenate([zl[:, 768:3840], zh[:, 768:3840]], axis=0)
    sa[...] = main_a[...] + tn(lanes, spread_a[...])
    lanes = jnp.concatenate([zl[:, 4480:5760], zh[:, 4480:5760]], axis=0)
    sc[...] = main_c[...] + tn(lanes, spread_c[...])


def x_edges_kernel(sa_in, sc_in, yl, yh, sa, sc, to_low, to_high, fl, fh):
    sa[...] = sa_in[...]
    sc[...] = sc_in[...]
    fl[...] = yl[...].astype(F32)
    fh[...] = yh[...].astype(F32)
    for r in range(2):
        sa[pl.ds(r, 48, stride=64), :] += fl[r * 48 : r * 48 + 48, :]
        sa[pl.ds(62 + r, 48, stride=64), :] += fh[r * 48 : r * 48 + 48, :]
    for r in range(3):
        sc[pl.ds(r, 40, stride=32), :] += fl[96 + r * 40 : 136 + r * 40, :]
        sc[pl.ds(29 + r, 40, stride=32), :] += fh[96 + r * 40 : 136 + r * 40, :]
    for ref, xa, xc in ((to_low, 0, 0), (to_high, 10, 7)):
        for f in range(4):
            ref[f * 128 : f * 128 + 128, :] = sa[
                (f * 12 + xa) * 64 : (f * 12 + xa) * 64 + 128, :
            ].astype(BF16)
            ref[512 + f * 96 : 608 + f * 96, :] = sc[
                (f * 10 + xc) * 32 : (f * 10 + xc) * 32 + 96, :
            ].astype(BF16)


def final_kernel(sa, sc, xl, xh, mid, coarse):
    for f in range(4):
        for x in range(8):
            base = (f * 12 + x + 2) * 64
            value = sa[base : base + 64, :]
            if x < 2:
                value = value + xl[f * 128 + x * 64 : f * 128 + x * 64 + 64, :].astype(F32)
            if x >= 6:
                at = f * 128 + (x - 6) * 64
                value = value + xh[at : at + 64, :].astype(F32)
            mid[f, x] = value
        for x in range(4):
            base = (f * 10 + x + 3) * 32
            value = sc[base : base + 32, :]
            if x < 3:
                at = 512 + f * 96 + x * 32
                value = value + xl[at : at + 32, :].astype(F32)
            if x >= 1:
                at = 512 + f * 96 + (x - 1) * 32
                value = value + xh[at : at + 32, :].astype(F32)
            coarse[f, x] = value[:, 0:64]


def shifted(x, axis, by):
    size = lax.axis_size(axis)
    return lax.ppermute(x, axis, [(i, (i + by) % size) for i in range(size)])


def local_views(fields, home_slot):
    fields_rows = fields.reshape(1024, 4, 4, 128).transpose(0, 2, 1, 3).reshape(16384, 128)
    return fields_rows, fields_rows.reshape(1024, 16, 128), home_slot.reshape(8, 128)


def body(fields, jacobian, home_slot):
    ix, iy, iz = (lax.axis_index(axis) for axis in ("gx", "gy", "gz"))
    me = (ix * lax.axis_size("gy") + iy) * lax.axis_size("gz") + iz
    coords = jnp.stack([ix, iy, iz, me]).astype(jnp.int32)
    fields_rows, fields_elems, home_tile = local_views(fields, home_slot)
    *payloads, spots = pack(coords, home_tile, jacobian, fields_rows)
    arrived = [shifted(p, *move) for p, move in zip(payloads, SHIFTS)]
    rows, jac_t = own_elements(spots, fields_elems, jacobian)
    uniform_t = all_elements(rows, jac_t, arrived)
    ya, main_c, edge_c, z_low, z_high = filters(coords, uniform_t)
    from_z_low = shifted(z_high, "gz", 1)
    from_z_high = shifted(z_low, "gz", -1)
    main_a, edge_a = first_y(coords, ya)
    spread_a = jnp.asarray(depth_spread(126, 2))
    spread_c = jnp.asarray(depth_spread(61, 3))
    y_low, y_high = vmem_call(
        y_edges_kernel,
        [jax.ShapeDtypeStruct((224, 128), BF16)] * 2,
        [pltpu.VMEM((768, 128), F32), pltpu.VMEM((640, 128), F32)],
        "y_edges",
        edge_a, edge_c, from_z_low, from_z_high, spread_a, spread_c,
    )
    from_y_low = shifted(y_high, "gy", 1)
    from_y_high = shifted(y_low, "gy", -1)
    vmem = pl.BlockSpec(memory_space=pltpu.VMEM)
    shapes = [
        jax.ShapeDtypeStruct((48 * 64, 128), F32),
        jax.ShapeDtypeStruct((40 * 32, 128), F32),
    ]
    sum_a, sum_c = local_call(
        z_main_kernel,
        shapes,
        [vmem] * 6,
        [main_a, main_c, from_z_low, from_z_high, spread_a, spread_c],
        "z_main",
        flops=2_000_000_000,
    )
    sum_a, sum_c, x_low, x_high = local_call(
        x_edges_kernel,
        shapes + [jax.ShapeDtypeStruct((896, 128), BF16)] * 2,
        [vmem] * 4,
        [sum_a, sum_c, from_y_low, from_y_high],
        "x_edges",
        scratch=[pltpu.VMEM((224, 128), F32), pltpu.VMEM((224, 128), F32)],
    )
    from_x_low = shifted(x_high, "gx", 1)
    from_x_high = shifted(x_low, "gx", -1)
    mid, coarse = vmem_call(
        final_kernel,
        [
            jax.ShapeDtypeStruct((4, 8, 64, 128), F32),
            jax.ShapeDtypeStruct((4, 4, 32, 64), F32),
        ],
        [],
        "final",
        sum_a, sum_c, from_x_low, from_x_high,
    )
    return mid, coarse


def solution(mesh):
    placed = (P(("gx", "gy", "gz"), None, None), P(("gx", "gy", "gz"), None), P(("gx", "gy", "gz")))
    return jax.shard_map(
        body,
        mesh=mesh,
        in_specs=placed,
        out_specs=(P(None, "gx", "gy", "gz"), P(None, "gx", "gy", "gz")),
        check_vma=False,
    )
```

```python
import jax
import jax.numpy as jnp
import numpy as np
from jax import lax
from jax.experimental import pallas as pl
from jax.experimental.pallas import tpu as pltpu
from jax.sharding import PartitionSpec as P

F32 = jnp.float32
BF16 = jnp.bfloat16
MIB = 1024 * 1024

GLL_NODES = np.array(
    [
        -1.0,
        -0.8717401485096066,
        -0.5917001814331423,
        -0.2092992179024789,
        0.2092992179024789,
        0.5917001814331423,
        0.8717401485096066,
        1.0,
    ]
)

SHIFTS = (("gx", 1), ("gx", -1), ("gy", 1), ("gy", -1), ("gz", 1), ("gz", -1))
STEPS = (16, -16, 4, -4, 1, -1)
PAYLOAD = 336


def gll_basis():
    targets = -1.0 + (2.0 * np.arange(8) + 1.0) / 8.0
    table = np.ones((8, 8))
    for node in range(8):
        for other in range(8):
            if other != node:
                table[:, node] *= (targets - GLL_NODES[other]) / (
                    GLL_NODES[node] - GLL_NODES[other]
                )
    return table


def plain_sinc(points):
    return np.sin(np.pi * points) / (np.pi * points)


def lanczos_taps():
    offsets = np.arange(8) - 3.5
    values = plain_sinc(offsets / 2.0) * plain_sinc(offsets / 4.0)
    return values / np.sum(values)


TAPS = [float(v) for v in lanczos_taps()]


def bf16_of(table):
    return np.asarray(table, np.float32).astype(jnp.bfloat16)


def interp_table():
    basis = gll_basis()
    table = np.einsum("ia,jb,kc->kijabc", basis, basis, basis).reshape(512, 512)
    return bf16_of(table)


def point_order():
    table = np.zeros((8, 8, 8, 8, 8, 8))
    for i in range(8):
        for j in range(8):
            for k in range(8):
                table[k, i, j, i, j, k] = 1.0
    return bf16_of(table.reshape(512, 512))


def depth_tables():
    taps = lanczos_taps()
    low = taps.astype(np.float32).astype(jnp.bfloat16).astype(np.float64)
    first = np.zeros((256, 132))
    for column in range(132):
        for tap in range(8):
            z = 2 * (column - 2) - 3 + tap
            if 0 <= z < 256:
                first[z, column] = low[tap]
    second = np.zeros((132, 70))
    for column in range(70):
        for tap in range(8):
            z = 2 * (column - 3) - 3 + tap + 2
            if 0 <= z < 132:
                second[z, column] = taps[tap]
    out = []
    for place in range(3):
        mid = first.copy()
        if place == 0:
            mid[:, :2] = 0.0
        if place == 2:
            mid[:, 130:] = 0.0
        both = mid @ second
        if place == 0:
            both[:, :3] = 0.0
        if place == 2:
            both[:, 67:] = 0.0
        columns = np.zeros((256, 256))
        columns[:, :128] = mid[:, 2:130]
        columns[:, 128:192] = both[:, 3:67]
        columns[:, 192:194] = mid[:, :2]
        columns[:, 194:196] = mid[:, 130:]
        columns[:, 196:199] = both[:, :3]
        columns[:, 199:202] = both[:, 67:]
        out.append(columns.reshape(32, 8, 256).transpose(1, 0, 2).reshape(256, 256))
    return bf16_of(np.stack(out))


def nt(a, b):
    return lax.dot_general(a, b, (((1,), (1,)), ((), ())), preferred_element_type=F32)


def nn(a, b):
    return lax.dot_general(a, b, (((1,), (0,)), ((), ())), preferred_element_type=F32)


def tn(a, b):
    return lax.dot_general(a, b, (((0,), (0,)), ((), ())), preferred_element_type=F32)


def brick_place():
    return tuple(lax.axis_index(axis) for axis in ("gx", "gy", "gz"))


def pack_kernel(home, jac_hbm, fields, *rest):
    outs = rest[:6]
    spots, picker, jac, index_v, index_s, sem_jac, sem_index, sem_rows = rest[6:]
    copy_jac = pltpu.make_async_copy(jac_hbm, jac, sem_jac)
    copy_jac.start()
    ix, iy, iz = brick_place()
    me = (ix * 4 + iy) * 4 + iz
    slots = home[...]
    diff = (slots >> 10) - me
    tag = (slots & 1023) + 1
    masks = jnp.concatenate([jnp.where(diff == step, 1.0, 0.0) for step in STEPS], axis=0)
    upper = jnp.where(
        lax.broadcasted_iota(jnp.int32, (128, 128), 0)
        <= lax.broadcasted_iota(jnp.int32, (128, 128), 1),
        1.0,
        0.0,
    ).astype(BF16)
    counts = nn(masks.astype(BF16), upper)
    spots[...] = jnp.where(diff == 0, tag - 1, 1024)
    row = lax.broadcasted_iota(jnp.int32, (8, 128), 0)
    slot_id = lax.broadcasted_iota(jnp.int32, (16, 128), 0).astype(F32)
    for d in range(6):
        count = counts[d * 8 : d * 8 + 8]
        total = jnp.broadcast_to(count[:, 127:128], (8, 128))
        rank = count - 1.0
        for r in range(7):
            rank = rank + jnp.where(row > r, jnp.broadcast_to(total[r : r + 1], (8, 128)), 0.0)
        rank = jnp.where(masks[d * 8 : d * 8 + 8] > 0.5, rank, -1.0)
        for r in range(8):
            hit = jnp.broadcast_to(rank[r : r + 1], (16, 128)) == slot_id
            picker[d * 16 : d * 16 + 16, r * 128 : r * 128 + 128] = jnp.where(
                hit, 1.0, 0.0
            ).astype(BF16)
    picker[96:128, :] = jnp.zeros((32, 1024), BF16)
    lane = lax.broadcasted_iota(jnp.int32, (8, 128), 1)
    pieces = []
    for r in range(8):
        own_tag = jnp.broadcast_to(tag[r : r + 1], (8, 128))
        elem = lane + r * 128
        value = jnp.where(
            row == 0,
            elem >> 5,
            jnp.where(row == 1, elem & 31, jnp.where(row == 2, own_tag >> 5, own_tag & 31)),
        )
        pieces.append(value.astype(F32).astype(BF16))
    values = jnp.concatenate(pieces, axis=1)
    found = nt(values, picker[...])
    index = found[0:1] * 32.0 + found[1:2]
    index_v[...] = jnp.broadcast_to(index, (8, 128)).astype(jnp.int32)
    copy_index = pltpu.make_async_copy(index_v, index_s, sem_index)
    copy_index.start()
    copy_index.wait()
    copies = []
    for d in range(6):
        for s in range(16):
            start = pl.multiple_of(index_s[0, d * 16 + s] * 16, 16)
            copy = pltpu.make_async_copy(
                fields.at[pl.ds(start, 16)], outs[d].at[pl.ds(s * 16, 16)], sem_rows.at[d]
            )
            copy.start()
    copy_jac.wait()
    jac_rows = nn(picker[...], jac[...]).astype(BF16)
    tag_lane = lax.broadcasted_iota(jnp.int32, (16, 128), 1)
    tag_row = lax.broadcasted_iota(jnp.int32, (16, 128), 0)
    tag_hi = jnp.broadcast_to(found[2:3], (16, 128))
    tag_lo = jnp.broadcast_to(found[3:4], (16, 128))
    both = jnp.where(tag_row == 0, tag_hi, jnp.where(tag_row == 1, tag_lo, 0.0))
    for d in range(6):
        for c in range(4):
            outs[d][256 + c * 16 : 272 + c * 16, :] = jac_rows[
                d * 16 : d * 16 + 16, c * 128 : c * 128 + 128
            ]
        outs[d][320:336, :] = jnp.where((tag_lane >> 4) == d, both, 0.0).astype(BF16)
    for d in range(6):
        pltpu.make_async_copy(
            fields.at[pl.ds(0, 256)], outs[d].at[pl.ds(0, 256)], sem_rows.at[d]
        ).wait()


def pack(home, jac, fields_rows):
    vmem = pl.BlockSpec(memory_space=pltpu.VMEM)
    hbm = pl.BlockSpec(memory_space=pltpu.HBM)
    return pl.pallas_call(
        pack_kernel,
        out_shape=[jax.ShapeDtypeStruct((PAYLOAD, 128), BF16)] * 6
        + [jax.ShapeDtypeStruct((8, 128), jnp.int32)],
        in_specs=[vmem, hbm, hbm],
        out_specs=[vmem] * 7,
        scratch_shapes=[
            pltpu.VMEM((128, 1024), BF16),
            pltpu.VMEM((1024, 512), BF16),
            pltpu.VMEM((8, 128), jnp.int32),
            pltpu.SMEM((8, 128), jnp.int32),
            pltpu.SemaphoreType.DMA,
            pltpu.SemaphoreType.DMA,
            pltpu.SemaphoreType.DMA((6,)),
        ],
        compiler_params=pltpu.CompilerParams(vmem_limit_bytes=60 * MIB),
        name="pack",
    )(home, jac, fields_rows)


def local_call(kernel, outs, specs, operands, name, out_specs=None, scratch=(),
               aliases=None, flops=0, limit=16):
    vmem = pl.BlockSpec(memory_space=pltpu.VMEM)
    return pl.pallas_call(
        kernel,
        out_shape=list(outs),
        in_specs=specs,
        out_specs=out_specs or [vmem] * len(outs),
        scratch_shapes=list(scratch),
        input_output_aliases=aliases or {},
        compiler_params=pltpu.CompilerParams(vmem_limit_bytes=limit * MIB),
        cost_estimate=pl.CostEstimate(
            flops=flops, bytes_accessed=1_000_000, transcendentals=0
        ),
        name=name,
    )(*operands)


def jacobian_kernel(spots, jac, order, first_arrived, jac_t):
    ordered = nt(order[...], jac[...]).astype(BF16)
    for c in range(4):
        ids = lax.broadcasted_iota(jnp.int32, (256, 128), 0) + c * 256
        hit = jnp.concatenate(
            [
                jnp.where(
                    ids == jnp.broadcast_to(spots[r : r + 1, :], (256, 128)), 1.0, 0.0
                ).astype(BF16)
                for r in range(8)
            ],
            axis=1,
        )
        jac_t[:, c * 256 : c * 256 + 256] = nt(ordered, hit)


def place_kernel(spots, fields, _, rows):
    def place(e, carry):
        targets = [spots[e * 32 + u] for u in range(32)]
        values = [fields[e * 32 + u] for u in range(32)]
        for u in range(32):
            rows[targets[u]] = values[u].astype(F32)
        return carry

    lax.fori_loop(0, 32, place, 0)


def brick_kernel(a0, a1, a2, a3, a4, a5, order, table, jac_in, rows, u0, u1, u2, u3, _,
                 jac_t, spot_v, spot_s, sem):
    arrays = (a0, a1, a2, a3, a4, a5)
    tags = jnp.zeros((8, 128), F32)
    for d in range(6):
        tags = tags + arrays[d][320:336, :].astype(F32)[0:8]
    spot = (tags[0:1] * 32.0 + tags[1:2]).astype(jnp.int32) - 1
    spot_v[...] = jnp.broadcast_to(jnp.where(spot < 0, 1024, spot), (8, 128))
    copy = pltpu.make_async_copy(spot_v, spot_s, sem)
    copy.start()
    jac = jnp.concatenate(
        [
            jnp.concatenate(
                [arrays[d][256 + c * 16 : 272 + c * 16, :] for c in range(4)], axis=1
            )
            for d in range(6)
        ]
        + [jnp.zeros((32, 512), BF16)],
        axis=0,
    )
    ordered = nt(order[...], jac).astype(BF16)
    for c in range(4):
        ids = lax.broadcasted_iota(jnp.int32, (256, 128), 0) + c * 256
        hit = jnp.where(ids == jnp.broadcast_to(spot, (256, 128)), 1.0, 0.0).astype(BF16)
        jac_t[:, c * 256 : c * 256 + 256] = jac_in[:, c * 256 : c * 256 + 256] + nt(ordered, hit)
    copy.wait()
    for d in range(6):
        for e in range(16):
            rows[spot_s[0, d * 16 + e]] = arrays[d][e * 16 : e * 16 + 16, :].astype(F32)
    flat = rows.reshape(1040 * 16, 128)
    for f, out in enumerate((u0, u1, u2, u3)):
        for n in range(4):
            pieces = [
                flat[pl.ds(n * 4096 + c * 4 + f, 256, stride=16), :].astype(BF16)
                for c in range(4)
            ]
            values = nt(table[...], jnp.concatenate(pieces, axis=1))
            out[:, n * 256 : n * 256 + 256] = (
                values * jac_t[:, n * 256 : n * 256 + 256]
            ).astype(BF16)


def own_elements(spots, fields_elems, jac, first_arrived):
    vmem = pl.BlockSpec(memory_space=pltpu.VMEM)
    smem = pl.BlockSpec(memory_space=pltpu.SMEM)
    order = jnp.asarray(point_order())
    [jac_t] = local_call(
        jacobian_kernel,
        [jax.ShapeDtypeStruct((512, 1024), F32)],
        [vmem] * 3 + [pl.BlockSpec(memory_space=pl.ANY)],
        [spots, jac, order, first_arrived],
        "jacobians",
        flops=2_000_000_000,
    )
    [rows] = local_call(
        place_kernel,
        [jax.ShapeDtypeStruct((1040, 16, 128), F32)],
        [smem, vmem, pl.BlockSpec(memory_space=pl.ANY)],
        [spots.reshape(1024), fields_elems, jac_t],
        "place",
        flops=2_000_000_000,
    )
    return rows, jac_t


def all_elements(rows, jac_t, arrived):
    vmem = pl.BlockSpec(memory_space=pltpu.VMEM)
    return local_call(
        brick_kernel,
        [jax.ShapeDtypeStruct((512, 1024), BF16)] * 4
        + [jax.ShapeDtypeStruct((1040, 16, 128), F32)],
        [vmem] * 10,
        [*arrived, jnp.asarray(point_order()), jnp.asarray(interp_table()), jac_t, rows],
        "brick",
        scratch=[
            pltpu.VMEM((512, 1024), F32),
            pltpu.VMEM((8, 128), jnp.int32),
            pltpu.SMEM((8, 128), jnp.int32),
            pltpu.SemaphoreType.DMA,
        ],
        aliases={9: 4},
        limit=36,
    )[:4]


def halve(values, outputs, shift):
    results = []
    for o in range(outputs):
        total = None
        for tap in range(4):
            pair = [
                values[at]
                for at in (2 * o + tap - shift, 2 * o + 7 - tap - shift)
                if 0 <= at < len(values)
            ]
            if pair:
                term = TAPS[tap] * (pair[0] + pair[1] if len(pair) == 2 else pair[0])
                total = term if total is None else total + term
        results.append(total)
    return results


def along_y(ref, base, count, y_low, y_high):
    total = None
    for tap in range(4):
        pair = (
            ref[pl.ds(base + 5 + tap, count, stride=2), :]
            + ref[pl.ds(base + 12 - tap, count, stride=2), :]
        )
        total = TAPS[tap] * pair if total is None else total + TAPS[tap] * pair
    low = total[0:8] * y_low
    high = total[count - 8 : count] * y_high
    return low, total[8 : count - 8], high


def inner_sides():
    ix, iy, _ = brick_place()
    return tuple(jnp.where(flag, 1.0, 0.0) for flag in (ix > 0, ix < 7, iy > 0, iy < 3))


def clear_pads(ref, count, size, width):
    def pads(q, carry):
        zero = jnp.zeros((width, 128), F32)
        base = pl.multiple_of(q * size, 8)
        ref[pl.ds(base, width), :] = zero
        ref[pl.ds(base + size - width, width), :] = zero
        return carry

    lax.fori_loop(0, count, pads, 0)


def along_x(values, outputs, edge, x_low, x_high):
    results = halve(values, outputs, 7)
    return [
        r * x_low if o < edge else r * x_high if o >= outputs - edge else r
        for o, r in enumerate(results)
    ]


def first_x(wide, base, f, e, t, ref, x_low, x_high):
    values = [
        wide[pl.ds(pl.multiple_of(base + e * 128 + x * 8, 8), 8), :] for x in range(16)
    ]
    for o, value in enumerate(along_x(values, 12, 2, x_low, x_high)):
        at = (f * 12 + o) * 176 + 24 + e * 8 + t * 32
        ref[pl.ds(pl.multiple_of(at, 8), 8), :] = value


def first_a_kernel(wide, main_a, edge_a, ya):
    x_low, x_high, y_low, y_high = inner_sides()
    clear_pads(ya, 48, 176, 24)

    def quarter(t, carry):
        for f in range(4):
            for e in range(4):
                first_x(wide, t * 2048 + f * 512, f, e, t, ya, x_low, x_high)
        return carry

    lax.fori_loop(0, 4, quarter, 0)

    def first(q, carry):
        low, middle, high = along_y(ya, q * 176, 80, y_low, y_high)
        edge_a[pl.ds(pl.multiple_of(q * 16, 16), 8), :] = low
        edge_a[pl.ds(pl.multiple_of(q * 16 + 8, 8), 8), :] = high
        main_a[pl.ds(pl.multiple_of(q * 64, 64), 64), :] = middle
        return carry

    lax.fori_loop(0, 48, first, 0)


def filter_kernel(u0, u1, u2, u3, depths, wide_a, main_c, edge_c, to_low, to_high,
                  depth, wide_b, yb, mb, yc, pbz, pcz, sem):
    x_low, x_high, y_low, y_high = inner_sides()
    _, _, iz = brick_place()
    place = jnp.where(iz == 0, 0, jnp.where(iz == 3, 2, 1))
    copy = pltpu.make_async_copy(depths.at[place], depth, sem)
    copy.start()
    clear_pads(yb, 48, 176, 24)
    clear_pads(yc, 40, 112, 16)
    copy.wait()

    def quarter(t, carry):
        lane = lax.broadcasted_iota(jnp.int32, (64, 128), 1)
        odd = (lane & 32) != 0
        upper = (lane & 64) != 0
        for f in range(4):
            pieces = [[], [], [], []]
            for ex in range(2):
                total = (u0, u1, u2, u3)[f][
                    :, pl.ds(pl.multiple_of(ex * 512 + t * 128, 128), 128)
                ]
                regrouped = []
                for h in range(2):
                    v = [total[(h * 4 + k) * 64 : (h * 4 + k) * 64 + 64] for k in range(4)]
                    for a, b in ((0, 1), (2, 3)):
                        v[a], v[b] = (
                            jnp.where(odd, pltpu.roll(v[b], 32, 1), v[a]),
                            jnp.where(odd, v[b], pltpu.roll(v[a], 96, 1)),
                        )
                    for a, b in ((0, 2), (1, 3)):
                        v[a], v[b] = (
                            jnp.where(upper, pltpu.roll(v[b], 64, 1), v[a]),
                            jnp.where(upper, v[b], pltpu.roll(v[a], 64, 1)),
                        )
                    regrouped.append(v)
                for e in range(4):
                    pieces[e].append(
                        jnp.concatenate([regrouped[0][e], regrouped[1][e]], axis=1)
                    )
            operand = jnp.concatenate([p for e in range(4) for p in pieces[e]], axis=0)
            both = nn(operand, depth[...])
            wide_a[pl.ds(pl.multiple_of(t * 2048 + f * 512, 512), 512), :] = both[:, 0:128]
            wide_b[f * 512 : f * 512 + 512, :] = both[:, 128:256]
        for f in range(4):
            for e in range(4):
                first_x(wide_b, f * 512, f, e, t, yb, x_low, x_high)
        return carry

    lax.fori_loop(0, 4, quarter, 0)

    def first(q, carry):
        low, middle, high = along_y(yb, q * 176, 80, y_low, y_high)
        base = pl.multiple_of(q * 80, 16)
        mb[pl.ds(base, 8), :] = low
        mb[pl.ds(base + 8, 64), :] = middle
        mb[pl.ds(base + 72, 8), :] = high
        pbz[pl.ds(pl.multiple_of(q * 16, 16), 16), :] = jnp.concatenate(
            [low, high], axis=0
        ).astype(BF16)
        pbz[pl.ds(pl.multiple_of(768 + q * 64, 64), 64), :] = middle.astype(BF16)
        return carry

    lax.fori_loop(0, 48, first, 0)

    def second_x(v, carry):
        for f in range(4):
            values = [
                mb[pl.ds(pl.multiple_of((f * 12 + o) * 80 + v * 8, 8), 8), :] for o in range(12)
            ]
            for o, value in enumerate(along_x(values, 10, 3, x_low, x_high)):
                at = (f * 10 + o) * 112 + 16 + v * 8
                yc[pl.ds(pl.multiple_of(at, 8), 8), :] = value
        return carry

    lax.fori_loop(0, 10, second_x, 0)

    def second(q, carry):
        low, middle, high = along_y(yc, q * 112, 48, y_low, y_high)
        edge_c[pl.ds(pl.multiple_of(q * 16, 16), 8), :] = low
        edge_c[pl.ds(pl.multiple_of(q * 16 + 8, 8), 8), :] = high
        main_c[pl.ds(pl.multiple_of(q * 32, 32), 32), :] = middle
        pcz[pl.ds(pl.multiple_of(q * 16, 16), 16), :] = jnp.concatenate(
            [low, high], axis=0
        ).astype(BF16)
        pcz[pl.ds(pl.multiple_of(640 + q * 32, 32), 32), :] = middle.astype(BF16)
        return carry

    lax.fori_loop(0, 40, second, 0)
    row = lax.broadcasted_iota(jnp.int32, (16, 128), 0)
    lane = lax.broadcasted_iota(jnp.int32, (16, 128), 1)

    def pick(count, low_lane, high_lane):
        low = (row < count) & (lane == row + low_lane)
        high = (row >= 8) & (row < 8 + count) & (lane == row - 8 + high_lane)
        return jnp.where(low | high, 1.0, 0.0).astype(BF16)

    mid = nt(pick(2, 64, 66), pbz[...])
    coarse = nt(pick(3, 68, 71), pcz[...])
    for ref, at in ((to_low, 0), (to_high, 8)):
        ref[:, 0:3840] = mid[at : at + 4].astype(BF16)
        ref[:, 3840:5760] = coarse[at : at + 4].astype(BF16)


def filters(uniform_t):
    vmem = pl.BlockSpec(memory_space=pltpu.VMEM)
    return local_call(
        filter_kernel,
        [
            jax.ShapeDtypeStruct((8192, 128), F32),
            jax.ShapeDtypeStruct((40 * 32, 128), F32),
            jax.ShapeDtypeStruct((40 * 16, 128), F32),
            jax.ShapeDtypeStruct((4, 5760), BF16),
            jax.ShapeDtypeStruct((4, 5760), BF16),
        ],
        [vmem] * 4 + [pl.BlockSpec(memory_space=pltpu.HBM)],
        [*uniform_t, jnp.asarray(depth_tables())],
        "filters",
        scratch=[
            pltpu.VMEM((256, 256), BF16),
            pltpu.VMEM((2048, 128), F32),
            pltpu.VMEM((48 * 176, 128), F32),
            pltpu.VMEM((48 * 80, 128), F32),
            pltpu.VMEM((40 * 112, 128), F32),
            pltpu.VMEM((3840, 128), BF16),
            pltpu.VMEM((1920, 128), BF16),
            pltpu.SemaphoreType.DMA,
        ],
        limit=32,
    )


def first_a(wide):
    return local_call(
        first_a_kernel,
        [jax.ShapeDtypeStruct((48 * 64, 128), F32), jax.ShapeDtypeStruct((48 * 16, 128), F32)],
        [pl.BlockSpec(memory_space=pltpu.VMEM)],
        [wide],
        "first_a",
        scratch=[pltpu.VMEM((48 * 176, 128), F32)],
        flops=3_000_000_000,
    )


def depth_spread(first_lane_high, count):
    table = np.zeros((8, 128))
    for r in range(count):
        table[r, r] = 1.0
        table[4 + r, first_lane_high + r] = 1.0
    return bf16_of(table)


def y_edges_kernel(edge_a, edge_c, from_low, from_high, spread_a, spread_c,
                   to_low, to_high, sa, sc):
    lanes = jnp.concatenate([from_low[:, 0:768], from_high[:, 0:768]], axis=0)
    sa[...] = edge_a[...] + tn(lanes, spread_a[...])
    lanes = jnp.concatenate([from_low[:, 3840:4480], from_high[:, 3840:4480]], axis=0)
    sc[...] = edge_c[...] + tn(lanes, spread_c[...])
    for ref, ra, rc in ((to_low, 6, 5), (to_high, 8, 8)):
        for r in range(2):
            ref[r * 48 : r * 48 + 48, :] = sa[pl.ds(ra + r, 48, stride=16), :].astype(BF16)
        tail = [sc[pl.ds(rc + r, 40, stride=16), :] for r in range(3)] + [jnp.zeros((8, 128), F32)]
        ref[96:224, :] = jnp.concatenate(tail, axis=0).astype(BF16)


def vmem_call(kernel, out_shape, scratch, name, *operands, **options):
    vmem = pl.BlockSpec(memory_space=pltpu.VMEM)
    single = not isinstance(out_shape, list)
    return pl.pallas_call(
        kernel,
        out_shape=out_shape,
        in_specs=[vmem] * len(operands),
        out_specs=vmem if single else [vmem] * len(out_shape),
        scratch_shapes=scratch,
        compiler_params=pltpu.CompilerParams(vmem_limit_bytes=12 * MIB),
        name=name,
        **options,
    )(*operands)


def z_main_kernel(main_a, main_c, zl, zh, spread_a, spread_c, sa, sc):
    lanes = jnp.concatenate([zl[:, 768:3840], zh[:, 768:3840]], axis=0)
    sa[...] = main_a[...] + tn(lanes, spread_a[...])
    lanes = jnp.concatenate([zl[:, 4480:5760], zh[:, 4480:5760]], axis=0)
    sc[...] = main_c[...] + tn(lanes, spread_c[...])


def x_edges_kernel(sa_in, sc_in, yl, yh, sa, sc, to_low, to_high, fl, fh):
    sa[...] = sa_in[...]
    sc[...] = sc_in[...]
    fl[...] = yl[...].astype(F32)
    fh[...] = yh[...].astype(F32)
    for r in range(2):
        sa[pl.ds(r, 48, stride=64), :] += fl[r * 48 : r * 48 + 48, :]
        sa[pl.ds(62 + r, 48, stride=64), :] += fh[r * 48 : r * 48 + 48, :]
    for r in range(3):
        sc[pl.ds(r, 40, stride=32), :] += fl[96 + r * 40 : 136 + r * 40, :]
        sc[pl.ds(29 + r, 40, stride=32), :] += fh[96 + r * 40 : 136 + r * 40, :]
    for ref, xa, xc in ((to_low, 0, 0), (to_high, 10, 7)):
        for f in range(4):
            ref[f * 128 : f * 128 + 128, :] = sa[
                (f * 12 + xa) * 64 : (f * 12 + xa) * 64 + 128, :
            ].astype(BF16)
        for pair in range(2):
            left, right = (
                sc[(f * 10 + xc) * 32 : (f * 10 + xc) * 32 + 96, :]
                for f in (2 * pair, 2 * pair + 1)
            )
            lane = lax.broadcasted_iota(jnp.int32, (96, 128), 1)
            ref[512 + pair * 96 : 608 + pair * 96, :] = jnp.where(
                lane < 64, left, pltpu.roll(right, 64, 1)
            ).astype(BF16)


def inside_kernel(sa, mid, sems):
    copies = [
        pltpu.make_async_copy(
            sa.at[pl.ds(f * 12 + 4, 4)], mid.at[f].at[pl.ds(2, 4)], sems.at[f]
        )
        for f in range(4)
    ]
    for copy in copies:
        copy.start()
    for copy in copies:
        copy.wait()


def final_kernel(sa, sc, xl, xh, _, coarse, mid, planes, sems):
    copies = []
    for side, ref in enumerate((xl, xh)):
        for f in range(4):
            for x in range(2):
                plane = f * 12 + 2 + side * 6 + x
                at = f * 128 + x * 64
                planes[side * 4 + f, x] = sa[plane] + ref[at : at + 64, :].astype(F32)
            copy = pltpu.make_async_copy(
                planes.at[side * 4 + f],
                mid.at[f].at[pl.ds(side * 6, 2)],
                sems.at[side * 4 + f],
            )
            copy.start()
            copies.append(copy)
    for f in range(4):
        half = f % 2 * 64
        for x in range(4):
            base = (f * 10 + x + 3) * 32
            value = sc[base : base + 32, :][:, 0:64]
            start = 512 + f // 2 * 96 + x * 32
            if x < 3:
                value = value + xl[start : start + 32, :].astype(F32)[:, half : half + 64]
            if x >= 1:
                value = value + xh[start - 32 : start, :].astype(F32)[:, half : half + 64]
            coarse[f, x] = value
    for copy in copies:
        copy.wait()


def shifted(x, axis, by):
    size = lax.axis_size(axis)
    return lax.ppermute(x, axis, [(i, (i + by) % size) for i in range(size)])


def local_views(fields, home_slot):
    fields_rows = fields.reshape(1024, 4, 4, 128).transpose(0, 2, 1, 3).reshape(16384, 128)
    return fields_rows, fields_rows.reshape(1024, 16, 128), home_slot.reshape(8, 128)


def body(fields, jacobian, home_slot):
    fields_rows, fields_elems, home_tile = local_views(fields, home_slot)
    *payloads, spots = pack(home_tile, jacobian, fields_rows)
    arrived = [shifted(p, *move) for p, move in zip(payloads, SHIFTS)]
    rows, jac_t = own_elements(spots, fields_elems, jacobian, arrived[0])
    uniform_t = all_elements(rows, jac_t, arrived)
    wide_a, main_c, edge_c, z_low, z_high = filters(uniform_t)
    from_z_low = shifted(z_high, "gz", 1)
    from_z_high = shifted(z_low, "gz", -1)
    main_a, edge_a = first_a(wide_a)
    spread_a = jnp.asarray(depth_spread(126, 2))
    spread_c = jnp.asarray(depth_spread(61, 3))
    y_low, y_high = vmem_call(
        y_edges_kernel,
        [jax.ShapeDtypeStruct((224, 128), BF16)] * 2,
        [pltpu.VMEM((768, 128), F32), pltpu.VMEM((640, 128), F32)],
        "y_edges",
        edge_a, edge_c, from_z_low, from_z_high, spread_a, spread_c,
    )
    from_y_low = shifted(y_high, "gy", 1)
    from_y_high = shifted(y_low, "gy", -1)
    vmem = pl.BlockSpec(memory_space=pltpu.VMEM)
    shapes = [
        jax.ShapeDtypeStruct((48 * 64, 128), F32),
        jax.ShapeDtypeStruct((40 * 32, 128), F32),
    ]
    sum_a, sum_c = local_call(
        z_main_kernel,
        shapes,
        [vmem] * 6,
        [main_a, main_c, from_z_low, from_z_high, spread_a, spread_c],
        "z_main",
        flops=2_000_000_000,
    )
    sum_a, sum_c, x_low, x_high = local_call(
        x_edges_kernel,
        shapes + [jax.ShapeDtypeStruct((704, 128), BF16)] * 2,
        [vmem] * 4,
        [sum_a, sum_c, from_y_low, from_y_high],
        "x_edges",
        scratch=[pltpu.VMEM((224, 128), F32), pltpu.VMEM((224, 128), F32)],
    )
    from_x_low = shifted(x_high, "gx", 1)
    from_x_high = shifted(x_low, "gx", -1)
    hbm = pl.BlockSpec(memory_space=pltpu.HBM)
    planes = sum_a.reshape(48, 64, 128)
    mid_shape = jax.ShapeDtypeStruct((4, 8, 64, 128), F32)
    [mid] = local_call(
        inside_kernel,
        [mid_shape],
        [vmem],
        [planes],
        "inside",
        out_specs=[hbm],
        scratch=[pltpu.SemaphoreType.DMA((4,))],
        flops=2_000_000_000,
    )
    coarse, mid = local_call(
        final_kernel,
        [jax.ShapeDtypeStruct((4, 4, 32, 64), F32), mid_shape],
        [vmem] * 4 + [hbm],
        [planes, sum_c, from_x_low, from_x_high, mid],
        "final",
        out_specs=[vmem, hbm],
        scratch=[pltpu.VMEM((8, 2, 64, 128), F32), pltpu.SemaphoreType.DMA((8,))],
        aliases={4: 1},
    )
    return mid, coarse


def solution(mesh):
    placed = (P(("gx", "gy", "gz"), None, None), P(("gx", "gy", "gz"), None), P(("gx", "gy", "gz")))
    return jax.shard_map(
        body,
        mesh=mesh,
        in_specs=placed,
        out_specs=(P(None, "gx", "gy", "gz"), P(None, "gx", "gy", "gz")),
        check_vma=False,
    )
```

```python
import jax
import jax.numpy as jnp
import numpy as np
from jax import lax
from jax.experimental import pallas as pl
from jax.experimental.pallas import tpu as pltpu
from jax.sharding import PartitionSpec as P

F32 = jnp.float32
BF16 = jnp.bfloat16
MIB = 1024 * 1024

GLL_NODES = np.array(
    [
        -1.0,
        -0.8717401485096066,
        -0.5917001814331423,
        -0.2092992179024789,
        0.2092992179024789,
        0.5917001814331423,
        0.8717401485096066,
        1.0,
    ]
)

SHIFTS = (("gx", 1), ("gx", -1), ("gy", 1), ("gy", -1), ("gz", 1), ("gz", -1))
STEPS = (16, -16, 4, -4, 1, -1)
PAYLOAD = 336


def gll_basis():
    targets = -1.0 + (2.0 * np.arange(8) + 1.0) / 8.0
    table = np.ones((8, 8))
    for node in range(8):
        for other in range(8):
            if other != node:
                table[:, node] *= (targets - GLL_NODES[other]) / (
                    GLL_NODES[node] - GLL_NODES[other]
                )
    return table


def plain_sinc(points):
    return np.sin(np.pi * points) / (np.pi * points)


def lanczos_taps():
    offsets = np.arange(8) - 3.5
    values = plain_sinc(offsets / 2.0) * plain_sinc(offsets / 4.0)
    return values / np.sum(values)


TAPS = [float(v) for v in lanczos_taps()]


def bf16_of(table):
    return np.asarray(table, np.float32).astype(jnp.bfloat16)


def interp_table():
    basis = gll_basis()
    table = np.einsum("ia,jb,kc->kijabc", basis, basis, basis).reshape(512, 512)
    return bf16_of(table)


def point_order():
    table = np.zeros((8, 8, 8, 8, 8, 8))
    for i in range(8):
        for j in range(8):
            for k in range(8):
                table[k, i, j, i, j, k] = 1.0
    return bf16_of(table.reshape(512, 512))


def depth_tables():
    taps = lanczos_taps()
    low = taps.astype(np.float32).astype(jnp.bfloat16).astype(np.float64)
    first = np.zeros((256, 132))
    for column in range(132):
        for tap in range(8):
            z = 2 * (column - 2) - 3 + tap
            if 0 <= z < 256:
                first[z, column] = low[tap]
    second = np.zeros((132, 70))
    for column in range(70):
        for tap in range(8):
            z = 2 * (column - 3) - 3 + tap + 2
            if 0 <= z < 132:
                second[z, column] = taps[tap]
    out = []
    for place in range(3):
        mid = first.copy()
        if place == 0:
            mid[:, :2] = 0.0
        if place == 2:
            mid[:, 130:] = 0.0
        both = mid @ second
        if place == 0:
            both[:, :3] = 0.0
        if place == 2:
            both[:, 67:] = 0.0
        columns = np.zeros((256, 256))
        columns[:, :128] = mid[:, 2:130]
        columns[:, 128:192] = both[:, 3:67]
        columns[:, 192:194] = mid[:, :2]
        columns[:, 194:196] = mid[:, 130:]
        columns[:, 196:199] = both[:, :3]
        columns[:, 199:202] = both[:, 67:]
        out.append(columns.reshape(32, 8, 256).transpose(1, 0, 2).reshape(256, 256))
    return bf16_of(np.stack(out))


def nt(a, b):
    return lax.dot_general(a, b, (((1,), (1,)), ((), ())), preferred_element_type=F32)


def nn(a, b):
    return lax.dot_general(a, b, (((1,), (0,)), ((), ())), preferred_element_type=F32)


def tn(a, b):
    return lax.dot_general(a, b, (((0,), (0,)), ((), ())), preferred_element_type=F32)


def brick_place():
    return tuple(lax.axis_index(axis) for axis in ("gx", "gy", "gz"))


def pack_kernel(home, jac_hbm, fields, *rest):
    outs = rest[:6]
    spots, picker, jac, index_v, index_s, sem_jac, sem_index, sem_rows = rest[6:]
    copy_jac = pltpu.make_async_copy(jac_hbm, jac, sem_jac)
    copy_jac.start()
    ix, iy, iz = brick_place()
    me = (ix * 4 + iy) * 4 + iz
    slots = home[...]
    diff = (slots >> 10) - me
    tag = (slots & 1023) + 1
    masks = jnp.concatenate([jnp.where(diff == step, 1.0, 0.0) for step in STEPS], axis=0)
    upper = jnp.where(
        lax.broadcasted_iota(jnp.int32, (128, 128), 0)
        <= lax.broadcasted_iota(jnp.int32, (128, 128), 1),
        1.0,
        0.0,
    ).astype(BF16)
    counts = nn(masks.astype(BF16), upper)
    spots[...] = jnp.where(diff == 0, tag - 1, 1024)
    row = lax.broadcasted_iota(jnp.int32, (8, 128), 0)
    slot_id = lax.broadcasted_iota(jnp.int32, (16, 128), 0).astype(F32)
    for d in range(6):
        count = counts[d * 8 : d * 8 + 8]
        total = jnp.broadcast_to(count[:, 127:128], (8, 128))
        rank = count - 1.0
        for r in range(7):
            rank = rank + jnp.where(row > r, jnp.broadcast_to(total[r : r + 1], (8, 128)), 0.0)
        rank = jnp.where(masks[d * 8 : d * 8 + 8] > 0.5, rank, -1.0)
        for r in range(8):
            hit = jnp.broadcast_to(rank[r : r + 1], (16, 128)) == slot_id
            picker[d * 16 : d * 16 + 16, r * 128 : r * 128 + 128] = jnp.where(
                hit, 1.0, 0.0
            ).astype(BF16)
    picker[96:128, :] = jnp.zeros((32, 1024), BF16)
    lane = lax.broadcasted_iota(jnp.int32, (8, 128), 1)
    pieces = []
    for r in range(8):
        own_tag = jnp.broadcast_to(tag[r : r + 1], (8, 128))
        elem = lane + r * 128
        value = jnp.where(
            row == 0,
            elem >> 5,
            jnp.where(row == 1, elem & 31, jnp.where(row == 2, own_tag >> 5, own_tag & 31)),
        )
        pieces.append(value.astype(F32).astype(BF16))
    values = jnp.concatenate(pieces, axis=1)
    found = nt(values, picker[...])
    index = found[0:1] * 32.0 + found[1:2]
    index_v[...] = jnp.broadcast_to(index, (8, 128)).astype(jnp.int32)
    copy_index = pltpu.make_async_copy(index_v, index_s, sem_index)
    copy_index.start()
    copy_index.wait()
    copies = []
    for d in range(6):
        for s in range(16):
            start = pl.multiple_of(index_s[0, d * 16 + s] * 16, 16)
            copy = pltpu.make_async_copy(
                fields.at[pl.ds(start, 16)], outs[d].at[pl.ds(s * 16, 16)], sem_rows.at[d]
            )
            copy.start()
    copy_jac.wait()
    jac_rows = nn(picker[...], jac[...]).astype(BF16)
    tag_lane = lax.broadcasted_iota(jnp.int32, (16, 128), 1)
    tag_row = lax.broadcasted_iota(jnp.int32, (16, 128), 0)
    tag_hi = jnp.broadcast_to(found[2:3], (16, 128))
    tag_lo = jnp.broadcast_to(found[3:4], (16, 128))
    both = jnp.where(tag_row == 0, tag_hi, jnp.where(tag_row == 1, tag_lo, 0.0))
    for d in range(6):
        for c in range(4):
            outs[d][256 + c * 16 : 272 + c * 16, :] = jac_rows[
                d * 16 : d * 16 + 16, c * 128 : c * 128 + 128
            ]
        outs[d][320:336, :] = jnp.where((tag_lane >> 4) == d, both, 0.0).astype(BF16)
    for d in range(6):
        pltpu.make_async_copy(
            fields.at[pl.ds(0, 256)], outs[d].at[pl.ds(0, 256)], sem_rows.at[d]
        ).wait()


def pack(home, jac, fields_rows):
    vmem = pl.BlockSpec(memory_space=pltpu.VMEM)
    hbm = pl.BlockSpec(memory_space=pltpu.HBM)
    return pl.pallas_call(
        pack_kernel,
        out_shape=[jax.ShapeDtypeStruct((PAYLOAD, 128), BF16)] * 6
        + [jax.ShapeDtypeStruct((8, 128), jnp.int32)],
        in_specs=[vmem, hbm, hbm],
        out_specs=[vmem] * 7,
        scratch_shapes=[
            pltpu.VMEM((128, 1024), BF16),
            pltpu.VMEM((1024, 512), BF16),
            pltpu.VMEM((8, 128), jnp.int32),
            pltpu.SMEM((8, 128), jnp.int32),
            pltpu.SemaphoreType.DMA,
            pltpu.SemaphoreType.DMA,
            pltpu.SemaphoreType.DMA((6,)),
        ],
        compiler_params=pltpu.CompilerParams(vmem_limit_bytes=53 * MIB),
        name="pack",
    )(home, jac, fields_rows)


def local_call(kernel, outs, specs, operands, name, out_specs=None, scratch=(),
               aliases=None, flops=0, limit=16):
    vmem = pl.BlockSpec(memory_space=pltpu.VMEM)
    return pl.pallas_call(
        kernel,
        out_shape=list(outs),
        in_specs=specs,
        out_specs=out_specs or [vmem] * len(outs),
        scratch_shapes=list(scratch),
        input_output_aliases=aliases or {},
        compiler_params=pltpu.CompilerParams(vmem_limit_bytes=limit * MIB),
        cost_estimate=pl.CostEstimate(
            flops=flops, bytes_accessed=1_000_000, transcendentals=0
        ),
        name=name,
    )(*operands)


def jacobian_kernel(spots, jac, order, first_arrived, jac_t):
    ordered = nt(order[...], jac[...]).astype(BF16)
    for c in range(4):
        ids = lax.broadcasted_iota(jnp.int32, (256, 128), 0) + c * 256
        hit = jnp.concatenate(
            [
                jnp.where(
                    ids == jnp.broadcast_to(spots[r : r + 1, :], (256, 128)), 1.0, 0.0
                ).astype(BF16)
                for r in range(8)
            ],
            axis=1,
        )
        jac_t[:, c * 256 : c * 256 + 256] = nt(ordered, hit)


def place_kernel(spots, fields, _, rows):
    def place(e, carry):
        targets = [spots[e * 32 + u] for u in range(32)]
        values = [fields[e * 32 + u] for u in range(32)]
        for u in range(32):
            rows[targets[u]] = values[u].astype(F32)
        return carry

    lax.fori_loop(0, 32, place, 0)


def brick_kernel(a0, a1, a2, a3, a4, a5, order, table, jac_in, rows, u0, u1, u2, u3, _,
                 jac_t, spot_v, spot_s, sem):
    arrays = (a0, a1, a2, a3, a4, a5)
    tags = jnp.zeros((8, 128), F32)
    for d in range(6):
        tags = tags + arrays[d][320:336, :].astype(F32)[0:8]
    spot = (tags[0:1] * 32.0 + tags[1:2]).astype(jnp.int32) - 1
    spot_v[...] = jnp.broadcast_to(jnp.where(spot < 0, 1024, spot), (8, 128))
    copy = pltpu.make_async_copy(spot_v, spot_s, sem)
    copy.start()
    jac = jnp.concatenate(
        [
            jnp.concatenate(
                [arrays[d][256 + c * 16 : 272 + c * 16, :] for c in range(4)], axis=1
            )
            for d in range(6)
        ]
        + [jnp.zeros((32, 512), BF16)],
        axis=0,
    )
    ordered = nt(order[...], jac).astype(BF16)
    for c in range(4):
        ids = lax.broadcasted_iota(jnp.int32, (256, 128), 0) + c * 256
        hit = jnp.where(ids == jnp.broadcast_to(spot, (256, 128)), 1.0, 0.0).astype(BF16)
        jac_t[:, c * 256 : c * 256 + 256] = jac_in[:, c * 256 : c * 256 + 256] + nt(ordered, hit)
    copy.wait()
    for d in range(6):
        for e in range(16):
            rows[spot_s[0, d * 16 + e]] = arrays[d][e * 16 : e * 16 + 16, :].astype(F32)
    flat = rows.reshape(1040 * 16, 128)
    for f, out in enumerate((u0, u1, u2, u3)):
        for n in range(4):
            pieces = [
                flat[pl.ds(n * 4096 + c * 4 + f, 256, stride=16), :].astype(BF16)
                for c in range(4)
            ]
            values = nt(table[...], jnp.concatenate(pieces, axis=1))
            out[:, n * 256 : n * 256 + 256] = (
                values * jac_t[:, n * 256 : n * 256 + 256]
            ).astype(BF16)


def own_elements(spots, fields_elems, jac, first_arrived):
    vmem = pl.BlockSpec(memory_space=pltpu.VMEM)
    smem = pl.BlockSpec(memory_space=pltpu.SMEM)
    order = jnp.asarray(point_order())
    [jac_t] = local_call(
        jacobian_kernel,
        [jax.ShapeDtypeStruct((512, 1024), F32)],
        [vmem] * 3 + [pl.BlockSpec(memory_space=pl.ANY)],
        [spots, jac, order, first_arrived],
        "jacobians",
        flops=2_000_000_000,
    )
    [rows] = local_call(
        place_kernel,
        [jax.ShapeDtypeStruct((1040, 16, 128), F32)],
        [smem, vmem, pl.BlockSpec(memory_space=pl.ANY)],
        [spots.reshape(1024), fields_elems, jac_t],
        "place",
        flops=2_000_000_000,
    )
    return rows, jac_t


def all_elements(rows, jac_t, arrived):
    vmem = pl.BlockSpec(memory_space=pltpu.VMEM)
    return local_call(
        brick_kernel,
        [jax.ShapeDtypeStruct((512, 1024), BF16)] * 4
        + [jax.ShapeDtypeStruct((1040, 16, 128), F32)],
        [vmem] * 10,
        [*arrived, jnp.asarray(point_order()), jnp.asarray(interp_table()), jac_t, rows],
        "brick",
        scratch=[
            pltpu.VMEM((512, 1024), F32),
            pltpu.VMEM((8, 128), jnp.int32),
            pltpu.SMEM((8, 128), jnp.int32),
            pltpu.SemaphoreType.DMA,
        ],
        aliases={9: 4},
        limit=36,
    )[:4]


def halve(values, outputs, shift):
    results = []
    for o in range(outputs):
        total = None
        for tap in range(4):
            pair = [
                values[at]
                for at in (2 * o + tap - shift, 2 * o + 7 - tap - shift)
                if 0 <= at < len(values)
            ]
            if pair:
                term = TAPS[tap] * (pair[0] + pair[1] if len(pair) == 2 else pair[0])
                total = term if total is None else total + term
        results.append(total)
    return results


def along_y(ref, base, count, y_low, y_high):
    total = None
    for tap in range(4):
        pair = (
            ref[pl.ds(base + 5 + tap, count, stride=2), :]
            + ref[pl.ds(base + 12 - tap, count, stride=2), :]
        )
        total = TAPS[tap] * pair if total is None else total + TAPS[tap] * pair
    low = total[0:8] * y_low
    high = total[count - 8 : count] * y_high
    return low, total[8 : count - 8], high


def inner_sides():
    ix, iy, _ = brick_place()
    return tuple(jnp.where(flag, 1.0, 0.0) for flag in (ix > 0, ix < 7, iy > 0, iy < 3))


def clear_pads(ref, count, size, width):
    def pads(q, carry):
        zero = jnp.zeros((width, 128), F32)
        base = pl.multiple_of(q * size, 8)
        ref[pl.ds(base, width), :] = zero
        ref[pl.ds(base + size - width, width), :] = zero
        return carry

    lax.fori_loop(0, count, pads, 0, unroll=4)


def along_x(values, outputs, edge, x_low, x_high):
    results = halve(values, outputs, 7)
    return [
        r * x_low if o < edge else r * x_high if o >= outputs - edge else r
        for o, r in enumerate(results)
    ]


def first_x(wide, base, f, e, t, ref, x_low, x_high):
    values = [
        wide[pl.ds(pl.multiple_of(base + e * 128 + x * 8, 8), 8), :] for x in range(16)
    ]
    for o, value in enumerate(along_x(values, 12, 2, x_low, x_high)):
        at = (f * 12 + o) * 176 + 24 + e * 8 + t * 32
        ref[pl.ds(pl.multiple_of(at, 8), 8), :] = value


def first_a_kernel(wide, main_a, edge_a, ya):
    x_low, x_high, y_low, y_high = inner_sides()
    clear_pads(ya, 48, 176, 24)

    def quarter(t, carry):
        for f in range(4):
            for e in range(4):
                first_x(wide, t * 2048 + f * 512, f, e, t, ya, x_low, x_high)
        return carry

    lax.fori_loop(0, 4, quarter, 0)

    def first(q, carry):
        low, middle, high = along_y(ya, q * 176, 80, y_low, y_high)
        edge_a[pl.ds(pl.multiple_of(q * 16, 16), 8), :] = low
        edge_a[pl.ds(pl.multiple_of(q * 16 + 8, 8), 8), :] = high
        main_a[pl.ds(pl.multiple_of(q * 64, 64), 64), :] = middle
        return carry

    lax.fori_loop(0, 48, first, 0, unroll=4)


def filter_kernel(u0, u1, u2, u3, depths, wide_a, main_c, edge_c, to_low, to_high,
                  depth, wide_b, yb, mb, yc, pbz, pcz, sem):
    x_low, x_high, y_low, y_high = inner_sides()
    _, _, iz = brick_place()
    place = jnp.where(iz == 0, 0, jnp.where(iz == 3, 2, 1))
    copy = pltpu.make_async_copy(depths.at[place], depth, sem)
    copy.start()
    clear_pads(yb, 48, 176, 24)
    clear_pads(yc, 40, 112, 16)
    copy.wait()

    def quarter(t, carry):
        lane = lax.broadcasted_iota(jnp.int32, (64, 128), 1)
        odd = (lane & 32) != 0
        upper = (lane & 64) != 0
        for f in range(4):
            pieces = [[], [], [], []]
            for ex in range(2):
                total = (u0, u1, u2, u3)[f][
                    :, pl.ds(pl.multiple_of(ex * 512 + t * 128, 128), 128)
                ]
                regrouped = []
                for h in range(2):
                    v = [total[(h * 4 + k) * 64 : (h * 4 + k) * 64 + 64] for k in range(4)]
                    for a, b in ((0, 1), (2, 3)):
                        v[a], v[b] = (
                            jnp.where(odd, pltpu.roll(v[b], 32, 1), v[a]),
                            jnp.where(odd, v[b], pltpu.roll(v[a], 96, 1)),
                        )
                    for a, b in ((0, 2), (1, 3)):
                        v[a], v[b] = (
                            jnp.where(upper, pltpu.roll(v[b], 64, 1), v[a]),
                            jnp.where(upper, v[b], pltpu.roll(v[a], 64, 1)),
                        )
                    regrouped.append(v)
                for e in range(4):
                    pieces[e].append(
                        jnp.concatenate([regrouped[0][e], regrouped[1][e]], axis=1)
                    )
            operand = jnp.concatenate([p for e in range(4) for p in pieces[e]], axis=0)
            both = nn(operand, depth[...])
            wide_a[pl.ds(pl.multiple_of(t * 2048 + f * 512, 512), 512), :] = both[:, 0:128]
            wide_b[f * 512 : f * 512 + 512, :] = both[:, 128:256]
        for f in range(4):
            for e in range(4):
                first_x(wide_b, f * 512, f, e, t, yb, x_low, x_high)
        return carry

    lax.fori_loop(0, 4, quarter, 0)

    def first(q, carry):
        low, middle, high = along_y(yb, q * 176, 80, y_low, y_high)
        base = pl.multiple_of(q * 80, 16)
        mb[pl.ds(base, 8), :] = low
        mb[pl.ds(base + 8, 64), :] = middle
        mb[pl.ds(base + 72, 8), :] = high
        pbz[pl.ds(pl.multiple_of(q * 16, 16), 16), :] = jnp.concatenate(
            [low, high], axis=0
        ).astype(BF16)
        pbz[pl.ds(pl.multiple_of(768 + q * 64, 64), 64), :] = middle.astype(BF16)
        return carry

    lax.fori_loop(0, 48, first, 0, unroll=4)

    def second_x(v, carry):
        for f in range(4):
            values = [
                mb[pl.ds(pl.multiple_of((f * 12 + o) * 80 + v * 8, 8), 8), :] for o in range(12)
            ]
            for o, value in enumerate(along_x(values, 10, 3, x_low, x_high)):
                at = (f * 10 + o) * 112 + 16 + v * 8
                yc[pl.ds(pl.multiple_of(at, 8), 8), :] = value
        return carry

    lax.fori_loop(0, 10, second_x, 0, unroll=2)

    def second(q, carry):
        low, middle, high = along_y(yc, q * 112, 48, y_low, y_high)
        edge_c[pl.ds(pl.multiple_of(q * 16, 16), 8), :] = low
        edge_c[pl.ds(pl.multiple_of(q * 16 + 8, 8), 8), :] = high
        main_c[pl.ds(pl.multiple_of(q * 32, 32), 32), :] = middle
        pcz[pl.ds(pl.multiple_of(q * 16, 16), 16), :] = jnp.concatenate(
            [low, high], axis=0
        ).astype(BF16)
        pcz[pl.ds(pl.multiple_of(640 + q * 32, 32), 32), :] = middle.astype(BF16)
        return carry

    lax.fori_loop(0, 40, second, 0, unroll=4)
    row = lax.broadcasted_iota(jnp.int32, (16, 128), 0)
    lane = lax.broadcasted_iota(jnp.int32, (16, 128), 1)

    def pick(count, low_lane, high_lane):
        low = (row < count) & (lane == row + low_lane)
        high = (row >= 8) & (row < 8 + count) & (lane == row - 8 + high_lane)
        return jnp.where(low | high, 1.0, 0.0).astype(BF16)

    mid = nt(pick(2, 64, 66), pbz[...])
    coarse = nt(pick(3, 68, 71), pcz[...])
    for ref, at in ((to_low, 0), (to_high, 8)):
        ref[:, 0:3840] = mid[at : at + 4].astype(BF16)
        ref[:, 3840:5760] = coarse[at : at + 4].astype(BF16)


def filters(uniform_t):
    vmem = pl.BlockSpec(memory_space=pltpu.VMEM)
    return local_call(
        filter_kernel,
        [
            jax.ShapeDtypeStruct((8192, 128), F32),
            jax.ShapeDtypeStruct((40 * 32, 128), F32),
            jax.ShapeDtypeStruct((40 * 16, 128), F32),
            jax.ShapeDtypeStruct((4, 5760), BF16),
            jax.ShapeDtypeStruct((4, 5760), BF16),
        ],
        [vmem] * 4 + [pl.BlockSpec(memory_space=pltpu.HBM)],
        [*uniform_t, jnp.asarray(depth_tables())],
        "filters",
        scratch=[
            pltpu.VMEM((256, 256), BF16),
            pltpu.VMEM((2048, 128), F32),
            pltpu.VMEM((48 * 176, 128), F32),
            pltpu.VMEM((48 * 80, 128), F32),
            pltpu.VMEM((40 * 112, 128), F32),
            pltpu.VMEM((3840, 128), BF16),
            pltpu.VMEM((1920, 128), BF16),
            pltpu.SemaphoreType.DMA,
        ],
        limit=32,
    )


def first_a(wide):
    return local_call(
        first_a_kernel,
        [jax.ShapeDtypeStruct((48 * 64, 128), F32), jax.ShapeDtypeStruct((48 * 16, 128), F32)],
        [pl.BlockSpec(memory_space=pltpu.VMEM)],
        [wide],
        "first_a",
        scratch=[pltpu.VMEM((48 * 176, 128), F32)],
        flops=3_000_000_000,
    )


def depth_spread(first_lane_high, count):
    table = np.zeros((8, 128))
    for r in range(count):
        table[r, r] = 1.0
        table[4 + r, first_lane_high + r] = 1.0
    return bf16_of(table)


def y_edges_kernel(edge_a, edge_c, from_low, from_high, spread_a, spread_c,
                   to_low, to_high, sa, sc):
    lanes = jnp.concatenate([from_low[:, 0:768], from_high[:, 0:768]], axis=0)
    sa[...] = edge_a[...] + tn(lanes, spread_a[...])
    lanes = jnp.concatenate([from_low[:, 3840:4480], from_high[:, 3840:4480]], axis=0)
    sc[...] = edge_c[...] + tn(lanes, spread_c[...])
    for ref, ra, rc in ((to_low, 6, 5), (to_high, 8, 8)):
        for r in range(2):
            ref[r * 48 : r * 48 + 48, :] = sa[pl.ds(ra + r, 48, stride=16), :].astype(BF16)
        tail = [sc[pl.ds(rc + r, 40, stride=16), :] for r in range(3)] + [jnp.zeros((8, 128), F32)]
        ref[96:224, :] = jnp.concatenate(tail, axis=0).astype(BF16)


def vmem_call(kernel, out_shape, scratch, name, *operands, **options):
    vmem = pl.BlockSpec(memory_space=pltpu.VMEM)
    single = not isinstance(out_shape, list)
    return pl.pallas_call(
        kernel,
        out_shape=out_shape,
        in_specs=[vmem] * len(operands),
        out_specs=vmem if single else [vmem] * len(out_shape),
        scratch_shapes=scratch,
        compiler_params=pltpu.CompilerParams(vmem_limit_bytes=12 * MIB),
        name=name,
        **options,
    )(*operands)


def z_main_kernel(main_a, main_c, zl, zh, spread_a, spread_c, sa, sc):
    lanes = jnp.concatenate([zl[:, 768:3840], zh[:, 768:3840]], axis=0)
    sa[...] = main_a[...] + tn(lanes, spread_a[...])
    lanes = jnp.concatenate([zl[:, 4480:5760], zh[:, 4480:5760]], axis=0)
    sc[...] = main_c[...] + tn(lanes, spread_c[...])


def x_edges_kernel(sa_in, sc_in, yl, yh, sa, sc, to_low, to_high, fl, fh):
    sa[...] = sa_in[...]
    sc[...] = sc_in[...]
    fl[...] = yl[...].astype(F32)
    fh[...] = yh[...].astype(F32)
    for r in range(2):
        sa[pl.ds(r, 48, stride=64), :] += fl[r * 48 : r * 48 + 48, :]
        sa[pl.ds(62 + r, 48, stride=64), :] += fh[r * 48 : r * 48 + 48, :]
    for r in range(3):
        sc[pl.ds(r, 40, stride=32), :] += fl[96 + r * 40 : 136 + r * 40, :]
        sc[pl.ds(29 + r, 40, stride=32), :] += fh[96 + r * 40 : 136 + r * 40, :]
    for ref, xa, xc in ((to_low, 0, 0), (to_high, 10, 7)):
        for f in range(4):
            ref[f * 128 : f * 128 + 128, :] = sa[
                (f * 12 + xa) * 64 : (f * 12 + xa) * 64 + 128, :
            ].astype(BF16)
        for pair in range(2):
            left, right = (
                sc[(f * 10 + xc) * 32 : (f * 10 + xc) * 32 + 96, :]
                for f in (2 * pair, 2 * pair + 1)
            )
            lane = lax.broadcasted_iota(jnp.int32, (96, 128), 1)
            ref[512 + pair * 96 : 608 + pair * 96, :] = jnp.where(
                lane < 64, left, pltpu.roll(right, 64, 1)
            ).astype(BF16)


def inside_kernel(sa, mid, sems):
    copies = [
        pltpu.make_async_copy(
            sa.at[pl.ds(f * 12 + 4, 4)], mid.at[f].at[pl.ds(2, 4)], sems.at[f]
        )
        for f in range(4)
    ]
    for copy in copies:
        copy.start()
    for copy in copies:
        copy.wait()


def final_kernel(sa, sc, xl, xh, _, coarse, mid, planes, small, sems):
    copies = []
    for side, ref in enumerate((xl, xh)):
        for f in range(4):
            for x in range(2):
                plane = f * 12 + 2 + side * 6 + x
                at = f * 128 + x * 64
                planes[side * 4 + f, x] = sa[plane] + ref[at : at + 64, :].astype(F32)
            copy = pltpu.make_async_copy(
                planes.at[side * 4 + f],
                mid.at[f].at[pl.ds(side * 6, 2)],
                sems.at[side * 4 + f],
            )
            copy.start()
            copies.append(copy)
    for f in range(4):
        half = f % 2 * 64
        for x in range(4):
            base = (f * 10 + x + 3) * 32
            value = sc[base : base + 32, :][:, 0:64]
            start = 512 + f // 2 * 96 + x * 32
            if x < 3:
                value = value + xl[start : start + 32, :].astype(F32)[:, half : half + 64]
            if x >= 1:
                value = value + xh[start - 32 : start, :].astype(F32)[:, half : half + 64]
            small[f, x] = value
    copy = pltpu.make_async_copy(small, coarse, sems.at[8])
    copy.start()
    for copy in copies + [copy]:
        copy.wait()


def shifted(x, axis, by):
    size = lax.axis_size(axis)
    return lax.ppermute(x, axis, [(i, (i + by) % size) for i in range(size)])


def local_views(fields, home_slot):
    fields_rows = fields.reshape(1024, 4, 4, 128).transpose(0, 2, 1, 3).reshape(16384, 128)
    return fields_rows, fields_rows.reshape(1024, 16, 128), home_slot.reshape(8, 128)


def body(fields, jacobian, home_slot):
    fields_rows, fields_elems, home_tile = local_views(fields, home_slot)
    *payloads, spots = pack(home_tile, jacobian, fields_rows)
    arrived = [shifted(p, *move) for p, move in zip(payloads, SHIFTS)]
    rows, jac_t = own_elements(spots, fields_elems, jacobian, arrived[0])
    uniform_t = all_elements(rows, jac_t, arrived)
    wide_a, main_c, edge_c, z_low, z_high = filters(uniform_t)
    from_z_low = shifted(z_high, "gz", 1)
    from_z_high = shifted(z_low, "gz", -1)
    main_a, edge_a = first_a(wide_a)
    spread_a = jnp.asarray(depth_spread(126, 2))
    spread_c = jnp.asarray(depth_spread(61, 3))
    y_low, y_high = vmem_call(
        y_edges_kernel,
        [jax.ShapeDtypeStruct((224, 128), BF16)] * 2,
        [pltpu.VMEM((768, 128), F32), pltpu.VMEM((640, 128), F32)],
        "y_edges",
        edge_a, edge_c, from_z_low, from_z_high, spread_a, spread_c,
    )
    from_y_low = shifted(y_high, "gy", 1)
    from_y_high = shifted(y_low, "gy", -1)
    vmem = pl.BlockSpec(memory_space=pltpu.VMEM)
    shapes = [
        jax.ShapeDtypeStruct((48 * 64, 128), F32),
        jax.ShapeDtypeStruct((40 * 32, 128), F32),
    ]
    sum_a, sum_c = local_call(
        z_main_kernel,
        shapes,
        [vmem] * 6,
        [main_a, main_c, from_z_low, from_z_high, spread_a, spread_c],
        "z_main",
        flops=2_000_000_000,
    )
    sum_a, sum_c, x_low, x_high = local_call(
        x_edges_kernel,
        shapes + [jax.ShapeDtypeStruct((704, 128), BF16)] * 2,
        [vmem] * 4,
        [sum_a, sum_c, from_y_low, from_y_high],
        "x_edges",
        scratch=[pltpu.VMEM((224, 128), F32), pltpu.VMEM((224, 128), F32)],
    )
    from_x_low = shifted(x_high, "gx", 1)
    from_x_high = shifted(x_low, "gx", -1)
    hbm = pl.BlockSpec(memory_space=pltpu.HBM)
    planes = sum_a.reshape(48, 64, 128)
    mid_shape = jax.ShapeDtypeStruct((4, 8, 64, 128), F32)
    [mid] = local_call(
        inside_kernel,
        [mid_shape],
        [vmem],
        [planes],
        "inside",
        out_specs=[hbm],
        scratch=[pltpu.SemaphoreType.DMA((4,))],
        flops=2_000_000_000,
    )
    coarse, mid = local_call(
        final_kernel,
        [jax.ShapeDtypeStruct((4, 4, 32, 64), F32), mid_shape],
        [vmem] * 4 + [hbm],
        [planes, sum_c, from_x_low, from_x_high, mid],
        "final",
        out_specs=[hbm, hbm],
        scratch=[
            pltpu.VMEM((8, 2, 64, 128), F32),
            pltpu.VMEM((4, 4, 32, 64), F32),
            pltpu.SemaphoreType.DMA((9,)),
        ],
        aliases={4: 1},
    )
    return mid, coarse


def solution(mesh):
    placed = (P(("gx", "gy", "gz"), None, None), P(("gx", "gy", "gz"), None), P(("gx", "gy", "gz")))
    return jax.shard_map(
        body,
        mesh=mesh,
        in_specs=placed,
        out_specs=(P(None, "gx", "gy", "gz"), P(None, "gx", "gy", "gz")),
        check_vma=False,
    )
```

```python
import jax
import jax.numpy as jnp
import numpy as np
from jax import lax
from jax.experimental import pallas as pl
from jax.experimental.pallas import tpu as pltpu
from jax.sharding import PartitionSpec as P

F32 = jnp.float32
BF16 = jnp.bfloat16
MIB = 1024 * 1024

GLL_NODES = np.array(
    [
        -1.0,
        -0.8717401485096066,
        -0.5917001814331423,
        -0.2092992179024789,
        0.2092992179024789,
        0.5917001814331423,
        0.8717401485096066,
        1.0,
    ]
)

SHIFTS = (('gz', 1), ('gz', -1), ('gy', 1), ('gy', -1), ('gx', 1), ('gx', -1))
STEPS = (1, -1, 4, -4, 16, -16)
PAYLOAD = 336


def gll_basis():
    targets = -1.0 + (2.0 * np.arange(8) + 1.0) / 8.0
    table = np.ones((8, 8))
    for node in range(8):
        for other in range(8):
            if other != node:
                table[:, node] *= (targets - GLL_NODES[other]) / (
                    GLL_NODES[node] - GLL_NODES[other]
                )
    return table


def plain_sinc(points):
    return np.sin(np.pi * points) / (np.pi * points)


def lanczos_taps():
    offsets = np.arange(8) - 3.5
    values = plain_sinc(offsets / 2.0) * plain_sinc(offsets / 4.0)
    return values / np.sum(values)


TAPS = [float(v) for v in lanczos_taps()]


def bf16_of(table):
    return np.asarray(table, np.float32).astype(jnp.bfloat16)


def interp_table():
    basis = gll_basis()
    table = np.einsum("ia,jb,kc->kijabc", basis, basis, basis).reshape(512, 512)
    return bf16_of(table)


def point_order():
    table = np.zeros((8, 8, 8, 8, 8, 8))
    for i in range(8):
        for j in range(8):
            for k in range(8):
                table[k, i, j, i, j, k] = 1.0
    return bf16_of(table.reshape(512, 512))


def depth_tables():
    taps = lanczos_taps()
    low = taps.astype(np.float32).astype(jnp.bfloat16).astype(np.float64)
    first = np.zeros((256, 132))
    for column in range(132):
        for tap in range(8):
            z = 2 * (column - 2) - 3 + tap
            if 0 <= z < 256:
                first[z, column] = low[tap]
    second = np.zeros((132, 70))
    for column in range(70):
        for tap in range(8):
            z = 2 * (column - 3) - 3 + tap + 2
            if 0 <= z < 132:
                second[z, column] = taps[tap]
    out = []
    for place in range(3):
        mid = first.copy()
        if place == 0:
            mid[:, :2] = 0.0
        if place == 2:
            mid[:, 130:] = 0.0
        both = mid @ second
        if place == 0:
            both[:, :3] = 0.0
        if place == 2:
            both[:, 67:] = 0.0
        columns = np.zeros((256, 256))
        columns[:, :128] = mid[:, 2:130]
        columns[:, 128:192] = both[:, 3:67]
        columns[:, 192:194] = mid[:, :2]
        columns[:, 194:196] = mid[:, 130:]
        columns[:, 196:199] = both[:, :3]
        columns[:, 199:202] = both[:, 67:]
        out.append(columns.reshape(32, 8, 256).transpose(1, 0, 2).reshape(256, 256))
    return bf16_of(np.stack(out))


def nt(a, b):
    return lax.dot_general(a, b, (((1,), (1,)), ((), ())), preferred_element_type=F32)


def nn(a, b):
    return lax.dot_general(a, b, (((1,), (0,)), ((), ())), preferred_element_type=F32)


def tn(a, b):
    return lax.dot_general(a, b, (((0,), (0,)), ((), ())), preferred_element_type=F32)


def brick_place():
    return tuple(lax.axis_index(axis) for axis in ("gx", "gy", "gz"))


def pack_kernel(home, jac_hbm, fields, *rest):
    outs = rest[:6]
    spots, picker, jac, index_v, index_s, sem_jac, sem_index, sem_rows = rest[6:]
    copy_jac = pltpu.make_async_copy(jac_hbm, jac, sem_jac)
    copy_jac.start()
    ix, iy, iz = brick_place()
    me = (ix * 4 + iy) * 4 + iz
    slots = home[...]
    diff = (slots >> 10) - me
    tag = (slots & 1023) + 1
    masks = jnp.concatenate([jnp.where(diff == step, 1.0, 0.0) for step in STEPS], axis=0)
    upper = jnp.where(
        lax.broadcasted_iota(jnp.int32, (128, 128), 0)
        <= lax.broadcasted_iota(jnp.int32, (128, 128), 1),
        1.0,
        0.0,
    ).astype(BF16)
    counts = nn(masks.astype(BF16), upper)
    spots[...] = jnp.where(diff == 0, tag - 1, 1024)
    row = lax.broadcasted_iota(jnp.int32, (8, 128), 0)
    slot_id = lax.broadcasted_iota(jnp.int32, (16, 128), 0).astype(F32)
    for d in range(6):
        count = counts[d * 8 : d * 8 + 8]
        total = jnp.broadcast_to(count[:, 127:128], (8, 128))
        rank = count - 1.0
        for r in range(7):
            rank = rank + jnp.where(row > r, jnp.broadcast_to(total[r : r + 1], (8, 128)), 0.0)
        rank = jnp.where(masks[d * 8 : d * 8 + 8] > 0.5, rank, -1.0)
        for r in range(8):
            hit = jnp.broadcast_to(rank[r : r + 1], (16, 128)) == slot_id
            picker[d * 16 : d * 16 + 16, r * 128 : r * 128 + 128] = jnp.where(
                hit, 1.0, 0.0
            ).astype(BF16)
    picker[96:128, :] = jnp.zeros((32, 1024), BF16)
    lane = lax.broadcasted_iota(jnp.int32, (8, 128), 1)
    pieces = []
    for r in range(8):
        own_tag = jnp.broadcast_to(tag[r : r + 1], (8, 128))
        elem = lane + r * 128
        value = jnp.where(
            row == 0,
            elem >> 5,
            jnp.where(row == 1, elem & 31, jnp.where(row == 2, own_tag >> 5, own_tag & 31)),
        )
        pieces.append(value.astype(F32).astype(BF16))
    values = jnp.concatenate(pieces, axis=1)
    found = nt(values, picker[...])
    index = found[0:1] * 32.0 + found[1:2]
    index_v[...] = jnp.broadcast_to(index, (8, 128)).astype(jnp.int32)
    copy_index = pltpu.make_async_copy(index_v, index_s, sem_index)
    copy_index.start()
    copy_index.wait()
    copies = []
    for d in range(6):
        for s in range(16):
            start = pl.multiple_of(index_s[0, d * 16 + s] * 16, 16)
            copy = pltpu.make_async_copy(
                fields.at[pl.ds(start, 16)], outs[d].at[pl.ds(s * 16, 16)], sem_rows.at[d]
            )
            copy.start()
    copy_jac.wait()
    jac_rows = nn(picker[...], jac[...]).astype(BF16)
    tag_lane = lax.broadcasted_iota(jnp.int32, (16, 128), 1)
    tag_row = lax.broadcasted_iota(jnp.int32, (16, 128), 0)
    tag_hi = jnp.broadcast_to(found[2:3], (16, 128))
    tag_lo = jnp.broadcast_to(found[3:4], (16, 128))
    both = jnp.where(tag_row == 0, tag_hi, jnp.where(tag_row == 1, tag_lo, 0.0))
    for d in range(6):
        for c in range(4):
            outs[d][256 + c * 16 : 272 + c * 16, :] = jac_rows[
                d * 16 : d * 16 + 16, c * 128 : c * 128 + 128
            ]
        outs[d][320:336, :] = jnp.where((tag_lane >> 4) == d, both, 0.0).astype(BF16)
    for d in range(6):
        pltpu.make_async_copy(
            fields.at[pl.ds(0, 256)], outs[d].at[pl.ds(0, 256)], sem_rows.at[d]
        ).wait()


def pack(home, jac, fields_rows):
    vmem = pl.BlockSpec(memory_space=pltpu.VMEM)
    hbm = pl.BlockSpec(memory_space=pltpu.HBM)
    return pl.pallas_call(
        pack_kernel,
        out_shape=[jax.ShapeDtypeStruct((PAYLOAD, 128), BF16)] * 6
        + [jax.ShapeDtypeStruct((8, 128), jnp.int32)],
        in_specs=[vmem, hbm, hbm],
        out_specs=[vmem] * 7,
        scratch_shapes=[
            pltpu.VMEM((128, 1024), BF16),
            pltpu.VMEM((1024, 512), BF16),
            pltpu.VMEM((8, 128), jnp.int32),
            pltpu.SMEM((8, 128), jnp.int32),
            pltpu.SemaphoreType.DMA,
            pltpu.SemaphoreType.DMA,
            pltpu.SemaphoreType.DMA((6,)),
        ],
        compiler_params=pltpu.CompilerParams(vmem_limit_bytes=53 * MIB),
        name="pack",
    )(home, jac, fields_rows)


def local_call(kernel, outs, specs, operands, name, out_specs=None, scratch=(),
               aliases=None, flops=0, limit=16):
    vmem = pl.BlockSpec(memory_space=pltpu.VMEM)
    return pl.pallas_call(
        kernel,
        out_shape=list(outs),
        in_specs=specs,
        out_specs=out_specs or [vmem] * len(outs),
        scratch_shapes=list(scratch),
        input_output_aliases=aliases or {},
        compiler_params=pltpu.CompilerParams(vmem_limit_bytes=limit * MIB),
        cost_estimate=pl.CostEstimate(
            flops=flops, bytes_accessed=1_000_000, transcendentals=0
        ),
        name=name,
    )(*operands)


def jacobian_kernel(spots, jac, order, first_arrived, jac_t):
    ordered = nt(order[...], jac[...]).astype(BF16)
    for c in range(4):
        ids = lax.broadcasted_iota(jnp.int32, (256, 128), 0) + c * 256
        hit = jnp.concatenate(
            [
                jnp.where(
                    ids == jnp.broadcast_to(spots[r : r + 1, :], (256, 128)), 1.0, 0.0
                ).astype(BF16)
                for r in range(8)
            ],
            axis=1,
        )
        jac_t[:, c * 256 : c * 256 + 256] = nt(ordered, hit)


def place_kernel(spots, fields, _, rows):
    def place(e, carry):
        targets = [spots[e * 32 + u] for u in range(32)]
        values = [fields[e * 32 + u] for u in range(32)]
        for u in range(32):
            rows[targets[u]] = values[u].astype(F32)
        return carry

    lax.fori_loop(0, 32, place, 0)


def regroup(values):
    lane = lax.broadcasted_iota(jnp.int32, values[0].shape, 1)
    v = list(values)
    for bit, pairs in ((32, ((0, 1), (2, 3))), (64, ((0, 2), (1, 3)))):
        mask = (lane & bit) != 0
        for a, b in pairs:
            v[a], v[b] = (
                jnp.where(mask, pltpu.roll(v[b], bit, 1), v[a]),
                jnp.where(mask, v[b], pltpu.roll(v[a], 128 - bit, 1)),
            )
    return v


def brick_kernel(a0, a1, a2, a3, a4, a5, order, table, jac_in, rows, lhs, _,
                 jac_t, spot_v, spot_s, sem):
    arrays = (a0, a1, a2, a3, a4, a5)
    tags = jnp.zeros((8, 128), F32)
    for d in range(6):
        tags = tags + arrays[d][320:336, :].astype(F32)[0:8]
    spot = (tags[0:1] * 32.0 + tags[1:2]).astype(jnp.int32) - 1
    spot_v[...] = jnp.broadcast_to(jnp.where(spot < 0, 1024, spot), (8, 128))
    copy = pltpu.make_async_copy(spot_v, spot_s, sem)
    copy.start()
    jac = jnp.concatenate(
        [
            jnp.concatenate(
                [arrays[d][256 + c * 16 : 272 + c * 16, :] for c in range(4)], axis=1
            )
            for d in range(6)
        ]
        + [jnp.zeros((32, 512), BF16)],
        axis=0,
    )
    ordered = nt(order[...], jac).astype(BF16)
    for c in range(4):
        ids = lax.broadcasted_iota(jnp.int32, (256, 128), 0) + c * 256
        hit = jnp.where(ids == jnp.broadcast_to(spot, (256, 128)), 1.0, 0.0).astype(BF16)
        jac_t[:, c * 256 : c * 256 + 256] = jac_in[:, c * 256 : c * 256 + 256] + nt(ordered, hit)
    copy.wait()
    for d in range(6):
        for e in range(16):
            rows[spot_s[0, d * 16 + e]] = arrays[d][e * 16 : e * 16 + 16, :].astype(F32)
    flat = rows.reshape(1040 * 16, 128)
    for n in range(4):
        for f in range(4):
            pieces = [
                flat[pl.ds(n * 4096 + c * 4 + f, 256, stride=16), :].astype(BF16)
                for c in range(4)
            ]
            values = nt(table[...], jnp.concatenate(pieces, axis=1))
            values = (values * jac_t[:, n * 256 : n * 256 + 256]).astype(BF16)
            for half in range(2):
                ex, t = n // 2, n % 2 * 2 + half
                part = values[:, half * 128 : half * 128 + 128]
                for h in range(2):
                    blocks = regroup([part[k * 64 : k * 64 + 64] for k in range(h * 4, h * 4 + 4)])
                    for e in range(4):
                        at = ((t * 4 + f) * 4 + e) * 128 + ex * 64
                        lhs[at : at + 64, h * 128 : h * 128 + 128] = blocks[e]


def own_elements(spots, fields_elems, jac, first_arrived):
    vmem = pl.BlockSpec(memory_space=pltpu.VMEM)
    smem = pl.BlockSpec(memory_space=pltpu.SMEM)
    order = jnp.asarray(point_order())
    [jac_t] = local_call(
        jacobian_kernel,
        [jax.ShapeDtypeStruct((512, 1024), F32)],
        [vmem] * 3 + [pl.BlockSpec(memory_space=pl.ANY)],
        [spots, jac, order, first_arrived],
        "jacobians",
        flops=2_000_000_000,
    )
    [rows] = local_call(
        place_kernel,
        [jax.ShapeDtypeStruct((1040, 16, 128), F32)],
        [smem, vmem, pl.BlockSpec(memory_space=pl.ANY)],
        [spots.reshape(1024), fields_elems, jac_t],
        "place",
        flops=2_000_000_000,
    )
    return rows, jac_t


def all_elements(rows, jac_t, arrived):
    vmem = pl.BlockSpec(memory_space=pltpu.VMEM)
    return local_call(
        brick_kernel,
        [
            jax.ShapeDtypeStruct((8192, 256), BF16),
            jax.ShapeDtypeStruct((1040, 16, 128), F32),
        ],
        [vmem] * 10,
        [*arrived, jnp.asarray(point_order()), jnp.asarray(interp_table()), jac_t, rows],
        "brick",
        scratch=[
            pltpu.VMEM((512, 1024), F32),
            pltpu.VMEM((8, 128), jnp.int32),
            pltpu.SMEM((8, 128), jnp.int32),
            pltpu.SemaphoreType.DMA,
        ],
        aliases={9: 1},
        limit=36,
    )[0]


def halve(values, outputs, shift):
    results = []
    for o in range(outputs):
        total = None
        for tap in range(4):
            pair = [
                values[at]
                for at in (2 * o + tap - shift, 2 * o + 7 - tap - shift)
                if 0 <= at < len(values)
            ]
            if pair:
                term = TAPS[tap] * (pair[0] + pair[1] if len(pair) == 2 else pair[0])
                total = term if total is None else total + term
        results.append(total)
    return results


def along_y(ref, base, count, y_low, y_high):
    total = None
    for tap in range(4):
        pair = (
            ref[pl.ds(base + 5 + tap, count, stride=2), :]
            + ref[pl.ds(base + 12 - tap, count, stride=2), :]
        )
        total = TAPS[tap] * pair if total is None else total + TAPS[tap] * pair
    low = total[0:8] * y_low
    high = total[count - 8 : count] * y_high
    return low, total[8 : count - 8], high


def inner_sides():
    ix, iy, _ = brick_place()
    return tuple(jnp.where(flag, 1.0, 0.0) for flag in (ix > 0, ix < 7, iy > 0, iy < 3))


def clear_pads(ref, count, size, width):
    def pads(q, carry):
        zero = jnp.zeros((width, 128), F32)
        base = pl.multiple_of(q * size, 8)
        ref[pl.ds(base, width), :] = zero
        ref[pl.ds(base + size - width, width), :] = zero
        return carry

    lax.fori_loop(0, count, pads, 0, unroll=4)


def along_x(values, outputs, edge, x_low, x_high):
    results = halve(values, outputs, 7)
    return [
        r * x_low if o < edge else r * x_high if o >= outputs - edge else r
        for o, r in enumerate(results)
    ]


def first_x(wide, base, f, e, t, ref, x_low, x_high):
    values = [
        wide[pl.ds(pl.multiple_of(base + e * 128 + x * 8, 8), 8), :] for x in range(16)
    ]
    for o, value in enumerate(along_x(values, 12, 2, x_low, x_high)):
        at = (f * 12 + o) * 176 + 24 + e * 8 + t * 32
        ref[pl.ds(pl.multiple_of(at, 8), 8), :] = value


def first_a_kernel(wide, main_a, edge_a, ya):
    x_low, x_high, y_low, y_high = inner_sides()
    clear_pads(ya, 48, 176, 24)

    def quarter(t, carry):
        for f in range(4):
            for e in range(4):
                first_x(wide, t * 2048 + f * 512, f, e, t, ya, x_low, x_high)
        return carry

    lax.fori_loop(0, 4, quarter, 0)

    def first(q, carry):
        low, middle, high = along_y(ya, q * 176, 80, y_low, y_high)
        edge_a[pl.ds(pl.multiple_of(q * 16, 16), 8), :] = low
        edge_a[pl.ds(pl.multiple_of(q * 16 + 8, 8), 8), :] = high
        main_a[pl.ds(pl.multiple_of(q * 64, 64), 64), :] = middle
        return carry

    lax.fori_loop(0, 48, first, 0, unroll=4)


def filter_kernel(lhs, depths, wide_a, main_c, edge_c, to_low, to_high,
                  depth, wide_b, yb, mb, yc, pbz, pcz, sem):
    x_low, x_high, y_low, y_high = inner_sides()
    _, _, iz = brick_place()
    place = jnp.where(iz == 0, 0, jnp.where(iz == 3, 2, 1))
    copy = pltpu.make_async_copy(depths.at[place], depth, sem)
    copy.start()
    clear_pads(yb, 48, 176, 24)
    clear_pads(yc, 40, 112, 16)
    copy.wait()

    def quarter(t, carry):
        for f in range(4):
            start = pl.multiple_of(t * 2048 + f * 512, 512)
            operand = lhs[pl.ds(start, 512), :]
            both = nn(operand, depth[...])
            wide_a[pl.ds(pl.multiple_of(t * 2048 + f * 512, 512), 512), :] = both[:, 0:128]
            wide_b[f * 512 : f * 512 + 512, :] = both[:, 128:256]
        for f in range(4):
            for e in range(4):
                first_x(wide_b, f * 512, f, e, t, yb, x_low, x_high)
        return carry

    lax.fori_loop(0, 4, quarter, 0)

    def first(q, carry):
        low, middle, high = along_y(yb, q * 176, 80, y_low, y_high)
        base = pl.multiple_of(q * 80, 16)
        mb[pl.ds(base, 8), :] = low
        mb[pl.ds(base + 8, 64), :] = middle
        mb[pl.ds(base + 72, 8), :] = high
        pbz[pl.ds(pl.multiple_of(q * 16, 16), 16), :] = jnp.concatenate(
            [low, high], axis=0
        ).astype(BF16)
        pbz[pl.ds(pl.multiple_of(768 + q * 64, 64), 64), :] = middle.astype(BF16)
        return carry

    lax.fori_loop(0, 48, first, 0, unroll=4)

    def second_x(v, carry):
        for f in range(4):
            values = [
                mb[pl.ds(pl.multiple_of((f * 12 + o) * 80 + v * 8, 8), 8), :] for o in range(12)
            ]
            for o, value in enumerate(along_x(values, 10, 3, x_low, x_high)):
                at = (f * 10 + o) * 112 + 16 + v * 8
                yc[pl.ds(pl.multiple_of(at, 8), 8), :] = value
        return carry

    lax.fori_loop(0, 10, second_x, 0, unroll=2)

    def second(q, carry):
        low, middle, high = along_y(yc, q * 112, 48, y_low, y_high)
        edge_c[pl.ds(pl.multiple_of(q * 16, 16), 8), :] = low
        edge_c[pl.ds(pl.multiple_of(q * 16 + 8, 8), 8), :] = high
        main_c[pl.ds(pl.multiple_of(q * 32, 32), 32), :] = middle
        pcz[pl.ds(pl.multiple_of(q * 16, 16), 16), :] = jnp.concatenate(
            [low, high], axis=0
        ).astype(BF16)
        pcz[pl.ds(pl.multiple_of(640 + q * 32, 32), 32), :] = middle.astype(BF16)
        return carry

    lax.fori_loop(0, 40, second, 0, unroll=4)
    row = lax.broadcasted_iota(jnp.int32, (16, 128), 0)
    lane = lax.broadcasted_iota(jnp.int32, (16, 128), 1)

    def pick(count, low_lane, high_lane):
        low = (row < count) & (lane == row + low_lane)
        high = (row >= 8) & (row < 8 + count) & (lane == row - 8 + high_lane)
        return jnp.where(low | high, 1.0, 0.0).astype(BF16)

    mid = nt(pick(2, 64, 66), pbz[...])
    coarse = nt(pick(3, 68, 71), pcz[...])
    for ref, at in ((to_low, 0), (to_high, 8)):
        ref[:, 0:3840] = mid[at : at + 4].astype(BF16)
        ref[:, 3840:5760] = coarse[at : at + 4].astype(BF16)


def filters(uniform):
    vmem = pl.BlockSpec(memory_space=pltpu.VMEM)
    return local_call(
        filter_kernel,
        [
            jax.ShapeDtypeStruct((8192, 128), F32),
            jax.ShapeDtypeStruct((40 * 32, 128), F32),
            jax.ShapeDtypeStruct((40 * 16, 128), F32),
            jax.ShapeDtypeStruct((4, 5760), BF16),
            jax.ShapeDtypeStruct((4, 5760), BF16),
        ],
        [vmem, pl.BlockSpec(memory_space=pltpu.HBM)],
        [uniform, jnp.asarray(depth_tables())],
        "filters",
        scratch=[
            pltpu.VMEM((256, 256), BF16),
            pltpu.VMEM((2048, 128), F32),
            pltpu.VMEM((48 * 176, 128), F32),
            pltpu.VMEM((48 * 80, 128), F32),
            pltpu.VMEM((40 * 112, 128), F32),
            pltpu.VMEM((3840, 128), BF16),
            pltpu.VMEM((1920, 128), BF16),
            pltpu.SemaphoreType.DMA,
        ],
        limit=32,
    )


def first_a(wide):
    return local_call(
        first_a_kernel,
        [jax.ShapeDtypeStruct((48 * 64, 128), F32), jax.ShapeDtypeStruct((48 * 16, 128), F32)],
        [pl.BlockSpec(memory_space=pltpu.VMEM)],
        [wide],
        "first_a",
        scratch=[pltpu.VMEM((48 * 176, 128), F32)],
        flops=3_000_000_000,
    )


def depth_spread(first_lane_high, count):
    table = np.zeros((8, 128))
    for r in range(count):
        table[r, r] = 1.0
        table[4 + r, first_lane_high + r] = 1.0
    return bf16_of(table)


def y_edges_kernel(edge_a, edge_c, from_low, from_high, spread_a, spread_c,
                   to_low, to_high, sa, sc):
    lanes = jnp.concatenate([from_low[:, 0:768], from_high[:, 0:768]], axis=0)
    sa[...] = edge_a[...] + tn(lanes, spread_a[...])
    lanes = jnp.concatenate([from_low[:, 3840:4480], from_high[:, 3840:4480]], axis=0)
    sc[...] = edge_c[...] + tn(lanes, spread_c[...])
    for ref, ra, rc in ((to_low, 6, 5), (to_high, 8, 8)):
        for r in range(2):
            ref[r * 48 : r * 48 + 48, :] = sa[pl.ds(ra + r, 48, stride=16), :].astype(BF16)
        tail = [sc[pl.ds(rc + r, 40, stride=16), :] for r in range(3)] + [jnp.zeros((8, 128), F32)]
        ref[96:224, :] = jnp.concatenate(tail, axis=0).astype(BF16)


def vmem_call(kernel, out_shape, scratch, name, *operands, **options):
    vmem = pl.BlockSpec(memory_space=pltpu.VMEM)
    single = not isinstance(out_shape, list)
    return pl.pallas_call(
        kernel,
        out_shape=out_shape,
        in_specs=[vmem] * len(operands),
        out_specs=vmem if single else [vmem] * len(out_shape),
        scratch_shapes=scratch,
        compiler_params=pltpu.CompilerParams(vmem_limit_bytes=12 * MIB),
        name=name,
        **options,
    )(*operands)


def z_main_kernel(main_a, main_c, zl, zh, spread_a, spread_c, sa, sc):
    lanes = jnp.concatenate([zl[:, 768:3840], zh[:, 768:3840]], axis=0)
    sa[...] = main_a[...] + tn(lanes, spread_a[...])
    lanes = jnp.concatenate([zl[:, 4480:5760], zh[:, 4480:5760]], axis=0)
    sc[...] = main_c[...] + tn(lanes, spread_c[...])


def x_edges_kernel(sa, sc, yl, yh, to_low, to_high, fl, fh, pa, pc):
    fl[...] = yl[...].astype(F32)
    fh[...] = yh[...].astype(F32)
    for ref, xa, xc in ((to_low, 0, 0), (to_high, 10, 7)):
        for f in range(4):
            first = f * 12 + xa
            pa[...] = sa[first * 64 : first * 64 + 128, :]
            for x in range(2):
                for r in range(2):
                    row = r * 48 + first + x
                    low, high = x * 64 + r, x * 64 + 62 + r
                    pa[low : low + 1, :] += fl[row : row + 1, :]
                    pa[high : high + 1, :] += fh[row : row + 1, :]
            ref[f * 128 : f * 128 + 128, :] = pa[...].astype(BF16)
            first = f * 10 + xc
            at = f % 2 * 96
            pc[at : at + 96, :] = sc[first * 32 : first * 32 + 96, :]
            for x in range(3):
                for r in range(3):
                    row = 96 + r * 40 + first + x
                    low, high = at + x * 32 + r, at + x * 32 + 29 + r
                    pc[low : low + 1, :] += fl[row : row + 1, :]
                    pc[high : high + 1, :] += fh[row : row + 1, :]
            if f % 2 == 1:
                lane = lax.broadcasted_iota(jnp.int32, (96, 128), 1)
                start = 512 + f // 2 * 96
                ref[start : start + 96, :] = jnp.where(
                    lane < 64, pc[0:96, :], pltpu.roll(pc[96:192, :], 64, 1)
                ).astype(BF16)


def inside_kernel(sa_in, sc_in, yl, yh, mid, sa, sc, fl, fh, sems):
    sa[...] = sa_in[...]
    sc[...] = sc_in[...]
    fl[...] = yl[...].astype(F32)
    fh[...] = yh[...].astype(F32)
    for r in range(2):
        sa[pl.ds(r, 48, stride=64), :] += fl[r * 48 : r * 48 + 48, :]
        sa[pl.ds(62 + r, 48, stride=64), :] += fh[r * 48 : r * 48 + 48, :]
    for r in range(3):
        sc[pl.ds(r, 40, stride=32), :] += fl[96 + r * 40 : 136 + r * 40, :]
        sc[pl.ds(29 + r, 40, stride=32), :] += fh[96 + r * 40 : 136 + r * 40, :]
    planes = sa.reshape(48, 64, 128)
    copies = [
        pltpu.make_async_copy(
            planes.at[pl.ds(f * 12 + 4, 4)], mid.at[f].at[pl.ds(2, 4)], sems.at[f]
        )
        for f in range(4)
    ]
    for copy in copies:
        copy.start()
    for copy in copies:
        copy.wait()


def final_kernel(sa, sc, xl, xh, _, coarse, mid, planes, small, sems):
    copies = []
    for side, ref in enumerate((xl, xh)):
        for f in range(4):
            for x in range(2):
                plane = f * 12 + 2 + side * 6 + x
                at = f * 128 + x * 64
                planes[side * 4 + f, x] = sa[plane] + ref[at : at + 64, :].astype(F32)
            copy = pltpu.make_async_copy(
                planes.at[side * 4 + f],
                mid.at[f].at[pl.ds(side * 6, 2)],
                sems.at[side * 4 + f],
            )
            copy.start()
            copies.append(copy)
    for f in range(4):
        half = f % 2 * 64
        for x in range(4):
            base = (f * 10 + x + 3) * 32
            value = sc[base : base + 32, :][:, 0:64]
            start = 512 + f // 2 * 96 + x * 32
            if x < 3:
                value = value + xl[start : start + 32, :].astype(F32)[:, half : half + 64]
            if x >= 1:
                value = value + xh[start - 32 : start, :].astype(F32)[:, half : half + 64]
            small[f, x] = value
    copy = pltpu.make_async_copy(small, coarse, sems.at[8])
    copy.start()
    for copy in copies + [copy]:
        copy.wait()


def shifted(x, axis, by):
    size = lax.axis_size(axis)
    return lax.ppermute(x, axis, [(i, (i + by) % size) for i in range(size)])


def local_views(fields, home_slot):
    fields_rows = fields.reshape(1024, 4, 4, 128).transpose(0, 2, 1, 3).reshape(16384, 128)
    return fields_rows, fields_rows.reshape(1024, 16, 128), home_slot.reshape(8, 128)


def body(fields, jacobian, home_slot):
    fields_rows, fields_elems, home_tile = local_views(fields, home_slot)
    *payloads, spots = pack(home_tile, jacobian, fields_rows)
    arrived = [shifted(p, *move) for p, move in zip(payloads, SHIFTS)]
    rows, jac_t = own_elements(spots, fields_elems, jacobian, arrived[0])
    uniform = all_elements(rows, jac_t, arrived)
    wide_a, main_c, edge_c, z_low, z_high = filters(uniform)
    from_z_low = shifted(z_high, "gz", 1)
    from_z_high = shifted(z_low, "gz", -1)
    main_a, edge_a = first_a(wide_a)
    spread_a = jnp.asarray(depth_spread(126, 2))
    spread_c = jnp.asarray(depth_spread(61, 3))
    y_low, y_high = vmem_call(
        y_edges_kernel,
        [jax.ShapeDtypeStruct((224, 128), BF16)] * 2,
        [pltpu.VMEM((768, 128), F32), pltpu.VMEM((640, 128), F32)],
        "y_edges",
        edge_a, edge_c, from_z_low, from_z_high, spread_a, spread_c,
    )
    from_y_low = shifted(y_high, "gy", 1)
    from_y_high = shifted(y_low, "gy", -1)
    vmem = pl.BlockSpec(memory_space=pltpu.VMEM)
    shapes = [
        jax.ShapeDtypeStruct((48 * 64, 128), F32),
        jax.ShapeDtypeStruct((40 * 32, 128), F32),
    ]
    sum_a, sum_c = local_call(
        z_main_kernel,
        shapes,
        [vmem] * 6,
        [main_a, main_c, from_z_low, from_z_high, spread_a, spread_c],
        "z_main",
        flops=2_000_000_000,
    )
    x_low, x_high = local_call(
        x_edges_kernel,
        [jax.ShapeDtypeStruct((704, 128), BF16)] * 2,
        [vmem] * 4,
        [sum_a, sum_c, from_y_low, from_y_high],
        "x_edges",
        scratch=[
            pltpu.VMEM((224, 128), F32),
            pltpu.VMEM((224, 128), F32),
            pltpu.VMEM((128, 128), F32),
            pltpu.VMEM((192, 128), F32),
        ],
    )
    from_x_low = shifted(x_high, "gx", 1)
    from_x_high = shifted(x_low, "gx", -1)
    hbm = pl.BlockSpec(memory_space=pltpu.HBM)
    mid_shape = jax.ShapeDtypeStruct((4, 8, 64, 128), F32)
    mid, sum_a, sum_c = local_call(
        inside_kernel,
        [mid_shape] + shapes,
        [vmem] * 4,
        [sum_a, sum_c, from_y_low, from_y_high],
        "inside",
        out_specs=[hbm, vmem, vmem],
        scratch=[
            pltpu.VMEM((224, 128), F32),
            pltpu.VMEM((224, 128), F32),
            pltpu.SemaphoreType.DMA((4,)),
        ],
        flops=2_000_000_000,
    )
    coarse, mid = local_call(
        final_kernel,
        [jax.ShapeDtypeStruct((4, 4, 32, 64), F32), mid_shape],
        [vmem] * 4 + [hbm],
        [sum_a.reshape(48, 64, 128), sum_c, from_x_low, from_x_high, mid],
        "final",
        out_specs=[hbm, hbm],
        scratch=[
            pltpu.VMEM((8, 2, 64, 128), F32),
            pltpu.VMEM((4, 4, 32, 64), F32),
            pltpu.SemaphoreType.DMA((9,)),
        ],
        aliases={4: 1},
    )
    return mid, coarse


def solution(mesh):
    placed = (P(("gx", "gy", "gz"), None, None), P(("gx", "gy", "gz"), None), P(("gx", "gy", "gz")))
    return jax.shard_map(
        body,
        mesh=mesh,
        in_specs=placed,
        out_specs=(P(None, "gx", "gy", "gz"), P(None, "gx", "gy", "gz")),
        check_vma=False,
    )
```

```python
import jax
import jax.numpy as jnp
import numpy as np
from jax import lax
from jax.experimental import pallas as pl
from jax.experimental.pallas import tpu as pltpu
from jax.sharding import PartitionSpec as P

F32 = jnp.float32
BF16 = jnp.bfloat16
MIB = 1024 * 1024

GLL_NODES = np.array(
    [
        -1.0,
        -0.8717401485096066,
        -0.5917001814331423,
        -0.2092992179024789,
        0.2092992179024789,
        0.5917001814331423,
        0.8717401485096066,
        1.0,
    ]
)

SHIFTS = (('gz', 1), ('gz', -1), ('gy', 1), ('gy', -1), ('gx', 1), ('gx', -1))
STEPS = (1, -1, 4, -4, 16, -16)
PAYLOAD = 336


def gll_basis():
    targets = -1.0 + (2.0 * np.arange(8) + 1.0) / 8.0
    table = np.ones((8, 8))
    for node in range(8):
        for other in range(8):
            if other != node:
                table[:, node] *= (targets - GLL_NODES[other]) / (
                    GLL_NODES[node] - GLL_NODES[other]
                )
    return table


def plain_sinc(points):
    return np.sin(np.pi * points) / (np.pi * points)


def lanczos_taps():
    offsets = np.arange(8) - 3.5
    values = plain_sinc(offsets / 2.0) * plain_sinc(offsets / 4.0)
    return values / np.sum(values)


TAPS = [float(v) for v in lanczos_taps()]


def bf16_of(table):
    return np.asarray(table, np.float32).astype(jnp.bfloat16)


def interp_table():
    basis = gll_basis()
    table = np.einsum("ia,jb,kc->kijabc", basis, basis, basis).reshape(512, 512)
    return bf16_of(table)


def point_order():
    table = np.zeros((8, 8, 8, 8, 8, 8))
    for i in range(8):
        for j in range(8):
            for k in range(8):
                table[k, i, j, i, j, k] = 1.0
    return bf16_of(table.reshape(512, 512))


def depth_tables():
    taps = lanczos_taps()
    low = taps.astype(np.float32).astype(jnp.bfloat16).astype(np.float64)
    first = np.zeros((256, 132))
    for column in range(132):
        for tap in range(8):
            z = 2 * (column - 2) - 3 + tap
            if 0 <= z < 256:
                first[z, column] = low[tap]
    second = np.zeros((132, 70))
    for column in range(70):
        for tap in range(8):
            z = 2 * (column - 3) - 3 + tap + 2
            if 0 <= z < 132:
                second[z, column] = taps[tap]
    out = []
    for place in range(3):
        mid = first.copy()
        if place == 0:
            mid[:, :2] = 0.0
        if place == 2:
            mid[:, 130:] = 0.0
        both = mid @ second
        if place == 0:
            both[:, :3] = 0.0
        if place == 2:
            both[:, 67:] = 0.0
        columns = np.zeros((256, 256))
        columns[:, :128] = mid[:, 2:130]
        columns[:, 128:192] = both[:, 3:67]
        columns[:, 192:194] = mid[:, :2]
        columns[:, 194:196] = mid[:, 130:]
        columns[:, 196:199] = both[:, :3]
        columns[:, 199:202] = both[:, 67:]
        out.append(columns.reshape(32, 8, 256).transpose(1, 0, 2).reshape(256, 256))
    return bf16_of(np.stack(out))


def nt(a, b):
    return lax.dot_general(a, b, (((1,), (1,)), ((), ())), preferred_element_type=F32)


def nn(a, b):
    return lax.dot_general(a, b, (((1,), (0,)), ((), ())), preferred_element_type=F32)


def tn(a, b):
    return lax.dot_general(a, b, (((0,), (0,)), ((), ())), preferred_element_type=F32)


def brick_place():
    return tuple(lax.axis_index(axis) for axis in ("gx", "gy", "gz"))


def pack_kernel(home, jac_hbm, fields, *rest):
    outs = rest[:6]
    spots, picker, jac, index_v, index_s, sem_jac, sem_index, sem_rows = rest[6:]
    copy_jac = pltpu.make_async_copy(jac_hbm, jac, sem_jac)
    copy_jac.start()
    ix, iy, iz = brick_place()
    me = (ix * 4 + iy) * 4 + iz
    slots = home[...]
    diff = (slots >> 10) - me
    tag = (slots & 1023) + 1
    masks = jnp.concatenate([jnp.where(diff == step, 1.0, 0.0) for step in STEPS], axis=0)
    upper = jnp.where(
        lax.broadcasted_iota(jnp.int32, (128, 128), 0)
        <= lax.broadcasted_iota(jnp.int32, (128, 128), 1),
        1.0,
        0.0,
    ).astype(BF16)
    counts = nn(masks.astype(BF16), upper)
    spots[...] = jnp.where(diff == 0, tag - 1, 1024)
    row = lax.broadcasted_iota(jnp.int32, (8, 128), 0)
    slot_id = lax.broadcasted_iota(jnp.int32, (16, 128), 0).astype(F32)
    for d in range(6):
        count = counts[d * 8 : d * 8 + 8]
        total = jnp.broadcast_to(count[:, 127:128], (8, 128))
        rank = count - 1.0
        for r in range(7):
            rank = rank + jnp.where(row > r, jnp.broadcast_to(total[r : r + 1], (8, 128)), 0.0)
        rank = jnp.where(masks[d * 8 : d * 8 + 8] > 0.5, rank, -1.0)
        for r in range(8):
            hit = jnp.broadcast_to(rank[r : r + 1], (16, 128)) == slot_id
            picker[d * 16 : d * 16 + 16, r * 128 : r * 128 + 128] = jnp.where(
                hit, 1.0, 0.0
            ).astype(BF16)
    picker[96:128, :] = jnp.zeros((32, 1024), BF16)
    lane = lax.broadcasted_iota(jnp.int32, (8, 128), 1)
    pieces = []
    for r in range(8):
        own_tag = jnp.broadcast_to(tag[r : r + 1], (8, 128))
        elem = lane + r * 128
        value = jnp.where(
            row == 0,
            elem >> 5,
            jnp.where(row == 1, elem & 31, jnp.where(row == 2, own_tag >> 5, own_tag & 31)),
        )
        pieces.append(value.astype(F32).astype(BF16))
    values = jnp.concatenate(pieces, axis=1)
    found = nt(values, picker[...])
    index = found[0:1] * 32.0 + found[1:2]
    index_v[...] = jnp.broadcast_to(index, (8, 128)).astype(jnp.int32)
    copy_index = pltpu.make_async_copy(index_v, index_s, sem_index)
    copy_index.start()
    copy_index.wait()
    copies = []
    for d in range(6):
        for s in range(16):
            start = pl.multiple_of(index_s[0, d * 16 + s] * 16, 16)
            copy = pltpu.make_async_copy(
                fields.at[pl.ds(start, 16)], outs[d].at[pl.ds(s * 16, 16)], sem_rows.at[d]
            )
            copy.start()
    copy_jac.wait()
    jac_rows = nn(picker[...], jac[...]).astype(BF16)
    tag_lane = lax.broadcasted_iota(jnp.int32, (16, 128), 1)
    tag_row = lax.broadcasted_iota(jnp.int32, (16, 128), 0)
    tag_hi = jnp.broadcast_to(found[2:3], (16, 128))
    tag_lo = jnp.broadcast_to(found[3:4], (16, 128))
    both = jnp.where(tag_row == 0, tag_hi, jnp.where(tag_row == 1, tag_lo, 0.0))
    for d in range(6):
        for c in range(4):
            outs[d][256 + c * 16 : 272 + c * 16, :] = jac_rows[
                d * 16 : d * 16 + 16, c * 128 : c * 128 + 128
            ]
        outs[d][320:336, :] = jnp.where((tag_lane >> 4) == d, both, 0.0).astype(BF16)
    for d in range(6):
        pltpu.make_async_copy(
            fields.at[pl.ds(0, 256)], outs[d].at[pl.ds(0, 256)], sem_rows.at[d]
        ).wait()


def pack(home, jac, fields_rows):
    vmem = pl.BlockSpec(memory_space=pltpu.VMEM)
    hbm = pl.BlockSpec(memory_space=pltpu.HBM)
    return pl.pallas_call(
        pack_kernel,
        out_shape=[jax.ShapeDtypeStruct((PAYLOAD, 128), BF16)] * 6
        + [jax.ShapeDtypeStruct((8, 128), jnp.int32)],
        in_specs=[vmem, hbm, hbm],
        out_specs=[vmem] * 7,
        scratch_shapes=[
            pltpu.VMEM((128, 1024), BF16),
            pltpu.VMEM((1024, 512), BF16),
            pltpu.VMEM((8, 128), jnp.int32),
            pltpu.SMEM((8, 128), jnp.int32),
            pltpu.SemaphoreType.DMA,
            pltpu.SemaphoreType.DMA,
            pltpu.SemaphoreType.DMA((6,)),
        ],
        compiler_params=pltpu.CompilerParams(vmem_limit_bytes=53 * MIB),
        name="pack",
    )(home, jac, fields_rows)


def local_call(kernel, outs, specs, operands, name, out_specs=None, scratch=(),
               aliases=None, flops=0, limit=16):
    vmem = pl.BlockSpec(memory_space=pltpu.VMEM)
    return pl.pallas_call(
        kernel,
        out_shape=list(outs),
        in_specs=specs,
        out_specs=out_specs or [vmem] * len(outs),
        scratch_shapes=list(scratch),
        input_output_aliases=aliases or {},
        compiler_params=pltpu.CompilerParams(vmem_limit_bytes=limit * MIB),
        cost_estimate=pl.CostEstimate(
            flops=flops, bytes_accessed=1_000_000, transcendentals=0
        ),
        name=name,
    )(*operands)


def jacobian_kernel(spots, jac, order, first_arrived, jac_t):
    ordered = nt(order[...], jac[...]).astype(BF16)
    for c in range(4):
        ids = lax.broadcasted_iota(jnp.int32, (256, 128), 0) + c * 256
        hit = jnp.concatenate(
            [
                jnp.where(
                    ids == jnp.broadcast_to(spots[r : r + 1, :], (256, 128)), 1.0, 0.0
                ).astype(BF16)
                for r in range(8)
            ],
            axis=1,
        )
        jac_t[:, c * 256 : c * 256 + 256] = nt(ordered, hit)


def place_kernel(spots, fields, _, rows):
    def place(e, carry):
        targets = [spots[e * 64 + u] for u in range(64)]
        values = [fields[e * 64 + u] for u in range(64)]
        for u in range(64):
            rows[targets[u]] = values[u].astype(F32)
        return carry

    lax.fori_loop(0, 16, place, 0)


def regroup(values):
    lane = lax.broadcasted_iota(jnp.int32, values[0].shape, 1)
    v = list(values)
    for bit, pairs in ((32, ((0, 1), (2, 3))), (64, ((0, 2), (1, 3)))):
        mask = (lane & bit) != 0
        for a, b in pairs:
            v[a], v[b] = (
                jnp.where(mask, pltpu.roll(v[b], bit, 1), v[a]),
                jnp.where(mask, v[b], pltpu.roll(v[a], 128 - bit, 1)),
            )
    return v


def brick_kernel(a0, a1, a2, a3, a4, a5, order, table, jac_in, rows, lhs, _,
                 jac_t, spot_v, spot_s, sem):
    arrays = (a0, a1, a2, a3, a4, a5)
    tags = jnp.zeros((8, 128), F32)
    for d in range(6):
        tags = tags + arrays[d][320:336, :].astype(F32)[0:8]
    spot = (tags[0:1] * 32.0 + tags[1:2]).astype(jnp.int32) - 1
    spot_v[...] = jnp.broadcast_to(jnp.where(spot < 0, 1024, spot), (8, 128))
    copy = pltpu.make_async_copy(spot_v, spot_s, sem)
    copy.start()
    jac = jnp.concatenate(
        [
            jnp.concatenate(
                [arrays[d][256 + c * 16 : 272 + c * 16, :] for c in range(4)], axis=1
            )
            for d in range(6)
        ]
        + [jnp.zeros((32, 512), BF16)],
        axis=0,
    )
    ordered = nt(order[...], jac).astype(BF16)
    for c in range(4):
        ids = lax.broadcasted_iota(jnp.int32, (256, 128), 0) + c * 256
        hit = jnp.where(ids == jnp.broadcast_to(spot, (256, 128)), 1.0, 0.0).astype(BF16)
        jac_t[:, c * 256 : c * 256 + 256] = jac_in[:, c * 256 : c * 256 + 256] + nt(ordered, hit)
    copy.wait()
    for d in range(6):
        for e in range(16):
            rows[spot_s[0, d * 16 + e]] = arrays[d][e * 16 : e * 16 + 16, :].astype(F32)
    flat = rows.reshape(1040 * 16, 128)
    for n in range(4):
        for f in range(4):
            pieces = [
                flat[pl.ds(n * 4096 + c * 4 + f, 256, stride=16), :].astype(BF16)
                for c in range(4)
            ]
            values = nt(table[...], jnp.concatenate(pieces, axis=1))
            values = (values * jac_t[:, n * 256 : n * 256 + 256]).astype(BF16)
            for half in range(2):
                ex, t = n // 2, n % 2 * 2 + half
                part = values[:, half * 128 : half * 128 + 128]
                for h in range(2):
                    blocks = regroup([part[k * 64 : k * 64 + 64] for k in range(h * 4, h * 4 + 4)])
                    for e in range(4):
                        at = ((t * 4 + f) * 4 + e) * 128 + ex * 64
                        lhs[at : at + 64, h * 128 : h * 128 + 128] = blocks[e]


def own_elements(spots, fields_elems, jac, first_arrived):
    vmem = pl.BlockSpec(memory_space=pltpu.VMEM)
    smem = pl.BlockSpec(memory_space=pltpu.SMEM)
    order = jnp.asarray(point_order())
    [jac_t] = local_call(
        jacobian_kernel,
        [jax.ShapeDtypeStruct((512, 1024), F32)],
        [vmem] * 3 + [pl.BlockSpec(memory_space=pl.ANY)],
        [spots, jac, order, first_arrived],
        "jacobians",
        flops=2_000_000_000,
    )
    [rows] = local_call(
        place_kernel,
        [jax.ShapeDtypeStruct((1040, 16, 128), F32)],
        [smem, vmem, pl.BlockSpec(memory_space=pl.ANY)],
        [spots.reshape(1024), fields_elems, jac_t],
        "place",
        flops=2_000_000_000,
    )
    return rows, jac_t


def all_elements(rows, jac_t, arrived):
    vmem = pl.BlockSpec(memory_space=pltpu.VMEM)
    return local_call(
        brick_kernel,
        [
            jax.ShapeDtypeStruct((8192, 256), BF16),
            jax.ShapeDtypeStruct((1040, 16, 128), F32),
        ],
        [vmem] * 10,
        [*arrived, jnp.asarray(point_order()), jnp.asarray(interp_table()), jac_t, rows],
        "brick",
        scratch=[
            pltpu.VMEM((512, 1024), F32),
            pltpu.VMEM((8, 128), jnp.int32),
            pltpu.SMEM((8, 128), jnp.int32),
            pltpu.SemaphoreType.DMA,
        ],
        aliases={9: 1},
        limit=36,
    )[0]


def halve(values, outputs, shift):
    results = []
    for o in range(outputs):
        total = None
        for tap in range(4):
            pair = [
                values[at]
                for at in (2 * o + tap - shift, 2 * o + 7 - tap - shift)
                if 0 <= at < len(values)
            ]
            if pair:
                term = TAPS[tap] * (pair[0] + pair[1] if len(pair) == 2 else pair[0])
                total = term if total is None else total + term
        results.append(total)
    return results


def along_y(ref, base, count, y_low, y_high):
    total = None
    for tap in range(4):
        pair = (
            ref[pl.ds(base + 5 + tap, count, stride=2), :]
            + ref[pl.ds(base + 12 - tap, count, stride=2), :]
        )
        total = TAPS[tap] * pair if total is None else total + TAPS[tap] * pair
    low = total[0:8] * y_low
    high = total[count - 8 : count] * y_high
    return low, total[8 : count - 8], high


def inner_sides():
    ix, iy, _ = brick_place()
    return tuple(jnp.where(flag, 1.0, 0.0) for flag in (ix > 0, ix < 7, iy > 0, iy < 3))


def clear_pads(ref, count, size, width):
    def pads(q, carry):
        zero = jnp.zeros((width, 128), F32)
        base = pl.multiple_of(q * size, 8)
        ref[pl.ds(base, width), :] = zero
        ref[pl.ds(base + size - width, width), :] = zero
        return carry

    lax.fori_loop(0, count, pads, 0, unroll=4)


def along_x(values, outputs, edge, x_low, x_high):
    results = halve(values, outputs, 7)
    return [
        r * x_low if o < edge else r * x_high if o >= outputs - edge else r
        for o, r in enumerate(results)
    ]


def first_x(wide, base, f, e, t, ref, x_low, x_high):
    values = [
        wide[pl.ds(pl.multiple_of(base + e * 128 + x * 8, 8), 8), :] for x in range(16)
    ]
    for o, value in enumerate(along_x(values, 12, 2, x_low, x_high)):
        at = (f * 12 + o) * 176 + 24 + e * 8 + t * 32
        ref[pl.ds(pl.multiple_of(at, 8), 8), :] = value


def first_a_kernel(wide, main_a, edge_a, ya):
    x_low, x_high, y_low, y_high = inner_sides()
    clear_pads(ya, 48, 176, 24)

    def quarter(t, carry):
        for f in range(4):
            for e in range(4):
                first_x(wide, t * 2048 + f * 512, f, e, t, ya, x_low, x_high)
        return carry

    lax.fori_loop(0, 4, quarter, 0)

    def first(q, carry):
        low, middle, high = along_y(ya, q * 176, 80, y_low, y_high)
        edge_a[pl.ds(pl.multiple_of(q * 16, 16), 8), :] = low
        edge_a[pl.ds(pl.multiple_of(q * 16 + 8, 8), 8), :] = high
        main_a[pl.ds(pl.multiple_of(q * 64, 64), 64), :] = middle
        return carry

    lax.fori_loop(0, 48, first, 0, unroll=16)


def filter_kernel(lhs, depths, wide_a, main_c, edge_c, to_low, to_high,
                  depth, wide_b, yb, mb, yc, pbz, pcz, sem):
    x_low, x_high, y_low, y_high = inner_sides()
    _, _, iz = brick_place()
    place = jnp.where(iz == 0, 0, jnp.where(iz == 3, 2, 1))
    copy = pltpu.make_async_copy(depths.at[place], depth, sem)
    copy.start()
    clear_pads(yb, 48, 176, 24)
    clear_pads(yc, 40, 112, 16)
    copy.wait()

    def quarter(t, carry):
        for f in range(4):
            start = pl.multiple_of(t * 2048 + f * 512, 512)
            operand = lhs[pl.ds(start, 512), :]
            both = nn(operand, depth[...])
            wide_a[pl.ds(pl.multiple_of(t * 2048 + f * 512, 512), 512), :] = both[:, 0:128]
            wide_b[f * 512 : f * 512 + 512, :] = both[:, 128:256]
        for f in range(4):
            for e in range(4):
                first_x(wide_b, f * 512, f, e, t, yb, x_low, x_high)
        return carry

    lax.fori_loop(0, 4, quarter, 0, unroll=4)

    def first(q, carry):
        low, middle, high = along_y(yb, q * 176, 80, y_low, y_high)
        base = pl.multiple_of(q * 80, 16)
        mb[pl.ds(base, 8), :] = low
        mb[pl.ds(base + 8, 64), :] = middle
        mb[pl.ds(base + 72, 8), :] = high
        pbz[pl.ds(pl.multiple_of(q * 16, 16), 16), :] = jnp.concatenate(
            [low, high], axis=0
        ).astype(BF16)
        pbz[pl.ds(pl.multiple_of(768 + q * 64, 64), 64), :] = middle.astype(BF16)
        return carry

    lax.fori_loop(0, 48, first, 0, unroll=16)

    def second_x(v, carry):
        for f in range(4):
            values = [
                mb[pl.ds(pl.multiple_of((f * 12 + o) * 80 + v * 8, 8), 8), :] for o in range(12)
            ]
            for o, value in enumerate(along_x(values, 10, 3, x_low, x_high)):
                at = (f * 10 + o) * 112 + 16 + v * 8
                yc[pl.ds(pl.multiple_of(at, 8), 8), :] = value
        return carry

    lax.fori_loop(0, 10, second_x, 0, unroll=10)

    def second(q, carry):
        low, middle, high = along_y(yc, q * 112, 48, y_low, y_high)
        edge_c[pl.ds(pl.multiple_of(q * 16, 16), 8), :] = low
        edge_c[pl.ds(pl.multiple_of(q * 16 + 8, 8), 8), :] = high
        main_c[pl.ds(pl.multiple_of(q * 32, 32), 32), :] = middle
        pcz[pl.ds(pl.multiple_of(q * 16, 16), 16), :] = jnp.concatenate(
            [low, high], axis=0
        ).astype(BF16)
        pcz[pl.ds(pl.multiple_of(640 + q * 32, 32), 32), :] = middle.astype(BF16)
        return carry

    lax.fori_loop(0, 40, second, 0, unroll=20)
    row = lax.broadcasted_iota(jnp.int32, (16, 128), 0)
    lane = lax.broadcasted_iota(jnp.int32, (16, 128), 1)

    def pick(count, low_lane, high_lane):
        low = (row < count) & (lane == row + low_lane)
        high = (row >= 8) & (row < 8 + count) & (lane == row - 8 + high_lane)
        return jnp.where(low | high, 1.0, 0.0).astype(BF16)

    mid = nt(pick(2, 64, 66), pbz[...])
    coarse = nt(pick(3, 68, 71), pcz[...])
    for ref, at in ((to_low, 0), (to_high, 8)):
        ref[:, 0:3840] = mid[at : at + 4].astype(BF16)
        ref[:, 3840:5760] = coarse[at : at + 4].astype(BF16)


def filters(uniform):
    vmem = pl.BlockSpec(memory_space=pltpu.VMEM)
    return local_call(
        filter_kernel,
        [
            jax.ShapeDtypeStruct((8192, 128), F32),
            jax.ShapeDtypeStruct((40 * 32, 128), F32),
            jax.ShapeDtypeStruct((40 * 16, 128), F32),
            jax.ShapeDtypeStruct((4, 5760), BF16),
            jax.ShapeDtypeStruct((4, 5760), BF16),
        ],
        [vmem, pl.BlockSpec(memory_space=pltpu.HBM)],
        [uniform, jnp.asarray(depth_tables())],
        "filters",
        scratch=[
            pltpu.VMEM((256, 256), BF16),
            pltpu.VMEM((2048, 128), F32),
            pltpu.VMEM((48 * 176, 128), F32),
            pltpu.VMEM((48 * 80, 128), F32),
            pltpu.VMEM((40 * 112, 128), F32),
            pltpu.VMEM((3840, 128), BF16),
            pltpu.VMEM((1920, 128), BF16),
            pltpu.SemaphoreType.DMA,
        ],
        limit=32,
    )


def first_a(wide):
    return local_call(
        first_a_kernel,
        [jax.ShapeDtypeStruct((48 * 64, 128), F32), jax.ShapeDtypeStruct((48 * 16, 128), F32)],
        [pl.BlockSpec(memory_space=pltpu.VMEM)],
        [wide],
        "first_a",
        scratch=[pltpu.VMEM((48 * 176, 128), F32)],
        flops=3_000_000_000,
    )


def depth_spread(first_lane_high, count):
    table = np.zeros((8, 128))
    for r in range(count):
        table[r, r] = 1.0
        table[4 + r, first_lane_high + r] = 1.0
    return bf16_of(table)


def y_edges_kernel(edge_a, edge_c, from_low, from_high, spread_a, spread_c,
                   to_low, to_high, sa, sc):
    lanes = jnp.concatenate([from_low[:, 0:768], from_high[:, 0:768]], axis=0)
    sa[...] = edge_a[...] + tn(lanes, spread_a[...])
    lanes = jnp.concatenate([from_low[:, 3840:4480], from_high[:, 3840:4480]], axis=0)
    sc[...] = edge_c[...] + tn(lanes, spread_c[...])
    for ref, ra, rc in ((to_low, 6, 5), (to_high, 8, 8)):
        for r in range(2):
            ref[r * 48 : r * 48 + 48, :] = sa[pl.ds(ra + r, 48, stride=16), :].astype(BF16)
        tail = [sc[pl.ds(rc + r, 40, stride=16), :] for r in range(3)] + [jnp.zeros((8, 128), F32)]
        ref[96:224, :] = jnp.concatenate(tail, axis=0).astype(BF16)


def vmem_call(kernel, out_shape, scratch, name, *operands, **options):
    vmem = pl.BlockSpec(memory_space=pltpu.VMEM)
    single = not isinstance(out_shape, list)
    return pl.pallas_call(
        kernel,
        out_shape=out_shape,
        in_specs=[vmem] * len(operands),
        out_specs=vmem if single else [vmem] * len(out_shape),
        scratch_shapes=scratch,
        compiler_params=pltpu.CompilerParams(vmem_limit_bytes=12 * MIB),
        name=name,
        **options,
    )(*operands)


def z_main_kernel(main_a, main_c, zl, zh, spread_a, spread_c, sa, sc):
    lanes = jnp.concatenate([zl[:, 768:3840], zh[:, 768:3840]], axis=0)
    sa[...] = main_a[...] + tn(lanes, spread_a[...])
    lanes = jnp.concatenate([zl[:, 4480:5760], zh[:, 4480:5760]], axis=0)
    sc[...] = main_c[...] + tn(lanes, spread_c[...])


def x_edges_kernel(sa, sc, yl, yh, to_low, to_high, fl, fh, pa, pc):
    fl[...] = yl[...].astype(F32)
    fh[...] = yh[...].astype(F32)
    for ref, xa, xc in ((to_low, 0, 0), (to_high, 10, 7)):
        for f in range(4):
            first = f * 12 + xa
            pa[...] = sa[first * 64 : first * 64 + 128, :]
            for x in range(2):
                for r in range(2):
                    row = r * 48 + first + x
                    low, high = x * 64 + r, x * 64 + 62 + r
                    pa[low : low + 1, :] += fl[row : row + 1, :]
                    pa[high : high + 1, :] += fh[row : row + 1, :]
            ref[f * 128 : f * 128 + 128, :] = pa[...].astype(BF16)
            first = f * 10 + xc
            at = f % 2 * 96
            pc[at : at + 96, :] = sc[first * 32 : first * 32 + 96, :]
            for x in range(3):
                for r in range(3):
                    row = 96 + r * 40 + first + x
                    low, high = at + x * 32 + r, at + x * 32 + 29 + r
                    pc[low : low + 1, :] += fl[row : row + 1, :]
                    pc[high : high + 1, :] += fh[row : row + 1, :]
            if f % 2 == 1:
                lane = lax.broadcasted_iota(jnp.int32, (96, 128), 1)
                start = 512 + f // 2 * 96
                ref[start : start + 96, :] = jnp.where(
                    lane < 64, pc[0:96, :], pltpu.roll(pc[96:192, :], 64, 1)
                ).astype(BF16)


def inside_kernel(sa_in, sc_in, yl, yh, mid, sa, sc, fl, fh, sems):
    sa[...] = sa_in[...]
    sc[...] = sc_in[...]
    fl[...] = yl[...].astype(F32)
    fh[...] = yh[...].astype(F32)
    for r in range(2):
        sa[pl.ds(r, 48, stride=64), :] += fl[r * 48 : r * 48 + 48, :]
        sa[pl.ds(62 + r, 48, stride=64), :] += fh[r * 48 : r * 48 + 48, :]
    for r in range(3):
        sc[pl.ds(r, 40, stride=32), :] += fl[96 + r * 40 : 136 + r * 40, :]
        sc[pl.ds(29 + r, 40, stride=32), :] += fh[96 + r * 40 : 136 + r * 40, :]
    planes = sa.reshape(48, 64, 128)
    copies = [
        pltpu.make_async_copy(
            planes.at[pl.ds(f * 12 + 4, 4)], mid.at[f].at[pl.ds(2, 4)], sems.at[f]
        )
        for f in range(4)
    ]
    for copy in copies:
        copy.start()
    for copy in copies:
        copy.wait()


def final_kernel(sa, sc, xl, xh, _, coarse, mid, planes, small, sems):
    copies = []
    for side, ref in enumerate((xl, xh)):
        for f in range(4):
            for x in range(2):
                plane = f * 12 + 2 + side * 6 + x
                at = f * 128 + x * 64
                planes[side * 4 + f, x] = sa[plane] + ref[at : at + 64, :].astype(F32)
            copy = pltpu.make_async_copy(
                planes.at[side * 4 + f],
                mid.at[f].at[pl.ds(side * 6, 2)],
                sems.at[side * 4 + f],
            )
            copy.start()
            copies.append(copy)
    for f in range(4):
        half = f % 2 * 64
        for x in range(4):
            base = (f * 10 + x + 3) * 32
            value = sc[base : base + 32, :][:, 0:64]
            start = 512 + f // 2 * 96 + x * 32
            if x < 3:
                value = value + xl[start : start + 32, :].astype(F32)[:, half : half + 64]
            if x >= 1:
                value = value + xh[start - 32 : start, :].astype(F32)[:, half : half + 64]
            small[f, x] = value
    copy = pltpu.make_async_copy(small, coarse, sems.at[8])
    copy.start()
    for copy in copies + [copy]:
        copy.wait()


def shifted(x, axis, by):
    size = lax.axis_size(axis)
    return lax.ppermute(x, axis, [(i, (i + by) % size) for i in range(size)])


def local_views(fields, home_slot):
    fields_rows = fields.reshape(1024, 4, 4, 128).transpose(0, 2, 1, 3).reshape(16384, 128)
    return fields_rows, fields_rows.reshape(1024, 16, 128), home_slot.reshape(8, 128)


def body(fields, jacobian, home_slot):
    fields_rows, fields_elems, home_tile = local_views(fields, home_slot)
    *payloads, spots = pack(home_tile, jacobian, fields_rows)
    arrived = [shifted(p, *move) for p, move in zip(payloads, SHIFTS)]
    rows, jac_t = own_elements(spots, fields_elems, jacobian, arrived[0])
    uniform = all_elements(rows, jac_t, arrived)
    wide_a, main_c, edge_c, z_low, z_high = filters(uniform)
    from_z_low = shifted(z_high, "gz", 1)
    from_z_high = shifted(z_low, "gz", -1)
    main_a, edge_a = first_a(wide_a)
    spread_a = jnp.asarray(depth_spread(126, 2))
    spread_c = jnp.asarray(depth_spread(61, 3))
    y_low, y_high = vmem_call(
        y_edges_kernel,
        [jax.ShapeDtypeStruct((224, 128), BF16)] * 2,
        [pltpu.VMEM((768, 128), F32), pltpu.VMEM((640, 128), F32)],
        "y_edges",
        edge_a, edge_c, from_z_low, from_z_high, spread_a, spread_c,
    )
    from_y_low = shifted(y_high, "gy", 1)
    from_y_high = shifted(y_low, "gy", -1)
    vmem = pl.BlockSpec(memory_space=pltpu.VMEM)
    shapes = [
        jax.ShapeDtypeStruct((48 * 64, 128), F32),
        jax.ShapeDtypeStruct((40 * 32, 128), F32),
    ]
    sum_a, sum_c = local_call(
        z_main_kernel,
        shapes,
        [vmem] * 6,
        [main_a, main_c, from_z_low, from_z_high, spread_a, spread_c],
        "z_main",
        flops=2_000_000_000,
    )
    x_low, x_high = local_call(
        x_edges_kernel,
        [jax.ShapeDtypeStruct((704, 128), BF16)] * 2,
        [vmem] * 4,
        [sum_a, sum_c, from_y_low, from_y_high],
        "x_edges",
        scratch=[
            pltpu.VMEM((224, 128), F32),
            pltpu.VMEM((224, 128), F32),
            pltpu.VMEM((128, 128), F32),
            pltpu.VMEM((192, 128), F32),
        ],
    )
    from_x_low = shifted(x_high, "gx", 1)
    from_x_high = shifted(x_low, "gx", -1)
    hbm = pl.BlockSpec(memory_space=pltpu.HBM)
    mid_shape = jax.ShapeDtypeStruct((4, 8, 64, 128), F32)
    mid, sum_a, sum_c = local_call(
        inside_kernel,
        [mid_shape] + shapes,
        [vmem] * 4,
        [sum_a, sum_c, from_y_low, from_y_high],
        "inside",
        out_specs=[hbm, vmem, vmem],
        scratch=[
            pltpu.VMEM((224, 128), F32),
            pltpu.VMEM((224, 128), F32),
            pltpu.SemaphoreType.DMA((4,)),
        ],
        flops=2_000_000_000,
    )
    coarse, mid = local_call(
        final_kernel,
        [jax.ShapeDtypeStruct((4, 4, 32, 64), F32), mid_shape],
        [vmem] * 4 + [hbm],
        [sum_a.reshape(48, 64, 128), sum_c, from_x_low, from_x_high, mid],
        "final",
        out_specs=[hbm, hbm],
        scratch=[
            pltpu.VMEM((8, 2, 64, 128), F32),
            pltpu.VMEM((4, 4, 32, 64), F32),
            pltpu.SemaphoreType.DMA((9,)),
        ],
        aliases={4: 1},
    )
    return mid, coarse


def solution(mesh):
    placed = (P(("gx", "gy", "gz"), None, None), P(("gx", "gy", "gz"), None), P(("gx", "gy", "gz")))
    return jax.shard_map(
        body,
        mesh=mesh,
        in_specs=placed,
        out_specs=(P(None, "gx", "gy", "gz"), P(None, "gx", "gy", "gz")),
        check_vma=False,
    )
```

```python
import jax
import jax.numpy as jnp
import numpy as np
from jax import lax
from jax.experimental import pallas as pl
from jax.experimental.pallas import tpu as pltpu
from jax.sharding import PartitionSpec as P

F32 = jnp.float32
BF16 = jnp.bfloat16
MIB = 1024 * 1024

GLL_NODES = np.array(
    [
        -1.0,
        -0.8717401485096066,
        -0.5917001814331423,
        -0.2092992179024789,
        0.2092992179024789,
        0.5917001814331423,
        0.8717401485096066,
        1.0,
    ]
)

SHIFTS = (('gz', 1), ('gz', -1), ('gy', 1), ('gy', -1), ('gx', 1), ('gx', -1))
STEPS = (1, -1, 4, -4, 16, -16)
PAYLOAD = 336


def gll_basis():
    targets = -1.0 + (2.0 * np.arange(8) + 1.0) / 8.0
    table = np.ones((8, 8))
    for node in range(8):
        for other in range(8):
            if other != node:
                table[:, node] *= (targets - GLL_NODES[other]) / (
                    GLL_NODES[node] - GLL_NODES[other]
                )
    return table


def plain_sinc(points):
    return np.sin(np.pi * points) / (np.pi * points)


def lanczos_taps():
    offsets = np.arange(8) - 3.5
    values = plain_sinc(offsets / 2.0) * plain_sinc(offsets / 4.0)
    return values / np.sum(values)


TAPS = [float(v) for v in lanczos_taps()]


def bf16_of(table):
    return np.asarray(table, np.float32).astype(jnp.bfloat16)


def interp_table():
    basis = gll_basis()
    table = np.einsum("ia,jb,kc->kijabc", basis, basis, basis).reshape(512, 512)
    return bf16_of(table)


def point_order():
    table = np.zeros((8, 8, 8, 8, 8, 8))
    for i in range(8):
        for j in range(8):
            for k in range(8):
                table[k, i, j, i, j, k] = 1.0
    return bf16_of(table.reshape(512, 512))


def depth_tables():
    taps = lanczos_taps()
    low = taps.astype(np.float32).astype(jnp.bfloat16).astype(np.float64)
    first = np.zeros((256, 132))
    for column in range(132):
        for tap in range(8):
            z = 2 * (column - 2) - 3 + tap
            if 0 <= z < 256:
                first[z, column] = low[tap]
    second = np.zeros((132, 70))
    for column in range(70):
        for tap in range(8):
            z = 2 * (column - 3) - 3 + tap + 2
            if 0 <= z < 132:
                second[z, column] = taps[tap]
    out = []
    for place in range(3):
        mid = first.copy()
        if place == 0:
            mid[:, :2] = 0.0
        if place == 2:
            mid[:, 130:] = 0.0
        both = mid @ second
        if place == 0:
            both[:, :3] = 0.0
        if place == 2:
            both[:, 67:] = 0.0
        columns = np.zeros((256, 256))
        columns[:, :128] = mid[:, 2:130]
        columns[:, 128:192] = both[:, 3:67]
        columns[:, 192:194] = mid[:, :2]
        columns[:, 194:196] = mid[:, 130:]
        columns[:, 196:199] = both[:, :3]
        columns[:, 199:202] = both[:, 67:]
        out.append(columns.reshape(32, 8, 256).transpose(1, 0, 2).reshape(256, 256))
    return bf16_of(np.stack(out))


def nt(a, b):
    return lax.dot_general(a, b, (((1,), (1,)), ((), ())), preferred_element_type=F32)


def nn(a, b):
    return lax.dot_general(a, b, (((1,), (0,)), ((), ())), preferred_element_type=F32)


def tn(a, b):
    return lax.dot_general(a, b, (((0,), (0,)), ((), ())), preferred_element_type=F32)


def brick_place():
    return tuple(lax.axis_index(axis) for axis in ("gx", "gy", "gz"))


def pack_kernel(home, jac_hbm, fields, *rest):
    outs = rest[:6]
    spots, picker, jac, index_v, index_s, sem_jac, sem_index, sem_rows = rest[6:]
    copy_jac = pltpu.make_async_copy(jac_hbm, jac, sem_jac)
    copy_jac.start()
    ix, iy, iz = brick_place()
    me = (ix * 4 + iy) * 4 + iz
    slots = home[...]
    diff = (slots >> 10) - me
    tag = (slots & 1023) + 1
    masks = jnp.concatenate([jnp.where(diff == step, 1.0, 0.0) for step in STEPS], axis=0)
    upper = jnp.where(
        lax.broadcasted_iota(jnp.int32, (128, 128), 0)
        <= lax.broadcasted_iota(jnp.int32, (128, 128), 1),
        1.0,
        0.0,
    ).astype(BF16)
    counts = nn(masks.astype(BF16), upper)
    spots[...] = jnp.where(diff == 0, tag - 1, 1024)
    row = lax.broadcasted_iota(jnp.int32, (8, 128), 0)
    slot_id = lax.broadcasted_iota(jnp.int32, (16, 128), 0).astype(F32)
    for d in range(6):
        count = counts[d * 8 : d * 8 + 8]
        total = jnp.broadcast_to(count[:, 127:128], (8, 128))
        rank = count - 1.0
        for r in range(7):
            rank = rank + jnp.where(row > r, jnp.broadcast_to(total[r : r + 1], (8, 128)), 0.0)
        rank = jnp.where(masks[d * 8 : d * 8 + 8] > 0.5, rank, -1.0)
        for r in range(8):
            hit = jnp.broadcast_to(rank[r : r + 1], (16, 128)) == slot_id
            picker[d * 16 : d * 16 + 16, r * 128 : r * 128 + 128] = jnp.where(
                hit, 1.0, 0.0
            ).astype(BF16)
    picker[96:128, :] = jnp.zeros((32, 1024), BF16)
    lane = lax.broadcasted_iota(jnp.int32, (8, 128), 1)
    pieces = []
    for r in range(8):
        own_tag = jnp.broadcast_to(tag[r : r + 1], (8, 128))
        elem = lane + r * 128
        value = jnp.where(
            row == 0,
            elem >> 5,
            jnp.where(row == 1, elem & 31, jnp.where(row == 2, own_tag >> 5, own_tag & 31)),
        )
        pieces.append(value.astype(F32).astype(BF16))
    values = jnp.concatenate(pieces, axis=1)
    found = nt(values, picker[...])
    index = found[0:1] * 32.0 + found[1:2]
    index_v[...] = jnp.broadcast_to(index, (8, 128)).astype(jnp.int32)
    copy_index = pltpu.make_async_copy(index_v, index_s, sem_index)
    copy_index.start()
    copy_index.wait()
    copies = []
    for d in range(6):
        for s in range(16):
            start = pl.multiple_of(index_s[0, d * 16 + s] * 16, 16)
            copy = pltpu.make_async_copy(
                fields.at[pl.ds(start, 16)], outs[d].at[pl.ds(s * 16, 16)], sem_rows.at[d]
            )
            copy.start()
    copy_jac.wait()
    jac_rows = nn(picker[...], jac[...]).astype(BF16)
    tag_lane = lax.broadcasted_iota(jnp.int32, (16, 128), 1)
    tag_row = lax.broadcasted_iota(jnp.int32, (16, 128), 0)
    tag_hi = jnp.broadcast_to(found[2:3], (16, 128))
    tag_lo = jnp.broadcast_to(found[3:4], (16, 128))
    both = jnp.where(tag_row == 0, tag_hi, jnp.where(tag_row == 1, tag_lo, 0.0))
    for d in range(6):
        for c in range(4):
            outs[d][256 + c * 16 : 272 + c * 16, :] = jac_rows[
                d * 16 : d * 16 + 16, c * 128 : c * 128 + 128
            ]
        outs[d][320:336, :] = jnp.where((tag_lane >> 4) == d, both, 0.0).astype(BF16)
    for d in range(6):
        pltpu.make_async_copy(
            fields.at[pl.ds(0, 256)], outs[d].at[pl.ds(0, 256)], sem_rows.at[d]
        ).wait()


def pack(home, jac, fields_rows):
    vmem = pl.BlockSpec(memory_space=pltpu.VMEM)
    hbm = pl.BlockSpec(memory_space=pltpu.HBM)
    return pl.pallas_call(
        pack_kernel,
        out_shape=[jax.ShapeDtypeStruct((PAYLOAD, 128), BF16)] * 6
        + [jax.ShapeDtypeStruct((8, 128), jnp.int32)],
        in_specs=[vmem, hbm, hbm],
        out_specs=[vmem] * 7,
        scratch_shapes=[
            pltpu.VMEM((128, 1024), BF16),
            pltpu.VMEM((1024, 512), BF16),
            pltpu.VMEM((8, 128), jnp.int32),
            pltpu.SMEM((8, 128), jnp.int32),
            pltpu.SemaphoreType.DMA,
            pltpu.SemaphoreType.DMA,
            pltpu.SemaphoreType.DMA((6,)),
        ],
        compiler_params=pltpu.CompilerParams(vmem_limit_bytes=53 * MIB),
        name="pack",
    )(home, jac, fields_rows)


def local_call(kernel, outs, specs, operands, name, out_specs=None, scratch=(),
               aliases=None, flops=0, limit=16):
    vmem = pl.BlockSpec(memory_space=pltpu.VMEM)
    return pl.pallas_call(
        kernel,
        out_shape=list(outs),
        in_specs=specs,
        out_specs=out_specs or [vmem] * len(outs),
        scratch_shapes=list(scratch),
        input_output_aliases=aliases or {},
        compiler_params=pltpu.CompilerParams(vmem_limit_bytes=limit * MIB),
        cost_estimate=pl.CostEstimate(
            flops=flops, bytes_accessed=1_000_000, transcendentals=0
        ),
        name=name,
    )(*operands)


def jacobian_kernel(spots, jac, order, first_arrived, jac_t):
    ordered = nt(order[...], jac[...]).astype(BF16)
    for c in range(4):
        ids = lax.broadcasted_iota(jnp.int32, (256, 128), 0) + c * 256
        hit = jnp.concatenate(
            [
                jnp.where(
                    ids == jnp.broadcast_to(spots[r : r + 1, :], (256, 128)), 1.0, 0.0
                ).astype(BF16)
                for r in range(8)
            ],
            axis=1,
        )
        jac_t[:, c * 256 : c * 256 + 256] = nt(ordered, hit)


def place_kernel(spots, fields, _, rows):
    def place(e, carry):
        targets = [spots[e * 64 + u] for u in range(64)]
        values = [fields[e * 64 + u] for u in range(64)]
        for u in range(64):
            rows[targets[u]] = values[u].astype(F32)
        return carry

    lax.fori_loop(0, 16, place, 0)


def regroup(values):
    lane = lax.broadcasted_iota(jnp.int32, values[0].shape, 1)
    v = list(values)
    for bit, pairs in ((32, ((0, 1), (2, 3))), (64, ((0, 2), (1, 3)))):
        mask = (lane & bit) != 0
        for a, b in pairs:
            v[a], v[b] = (
                jnp.where(mask, pltpu.roll(v[b], bit, 1), v[a]),
                jnp.where(mask, v[b], pltpu.roll(v[a], 128 - bit, 1)),
            )
    return v


def brick_kernel(a0, a1, a2, a3, a4, a5, order, table, jac_in, rows, lhs, _,
                 jac_t, spot_v, spot_s, sem):
    arrays = (a0, a1, a2, a3, a4, a5)
    tags = jnp.zeros((8, 128), F32)
    for d in range(6):
        tags = tags + arrays[d][320:336, :].astype(F32)[0:8]
    spot = (tags[0:1] * 32.0 + tags[1:2]).astype(jnp.int32) - 1
    spot_v[...] = jnp.broadcast_to(jnp.where(spot < 0, 1024, spot), (8, 128))
    copy = pltpu.make_async_copy(spot_v, spot_s, sem)
    copy.start()
    jac = jnp.concatenate(
        [
            jnp.concatenate(
                [arrays[d][256 + c * 16 : 272 + c * 16, :] for c in range(4)], axis=1
            )
            for d in range(6)
        ]
        + [jnp.zeros((32, 512), BF16)],
        axis=0,
    )
    ordered = nt(order[...], jac).astype(BF16)
    for c in range(4):
        ids = lax.broadcasted_iota(jnp.int32, (256, 128), 0) + c * 256
        hit = jnp.where(ids == jnp.broadcast_to(spot, (256, 128)), 1.0, 0.0).astype(BF16)
        jac_t[:, c * 256 : c * 256 + 256] = jac_in[:, c * 256 : c * 256 + 256] + nt(ordered, hit)
    copy.wait()
    for d in range(6):
        for e in range(16):
            rows[spot_s[0, d * 16 + e]] = arrays[d][e * 16 : e * 16 + 16, :].astype(F32)
    flat = rows.reshape(1040 * 16, 128)
    for n in range(4):
        for f in range(4):
            pieces = [
                flat[pl.ds(n * 4096 + c * 4 + f, 256, stride=16), :].astype(BF16)
                for c in range(4)
            ]
            values = nt(table[...], jnp.concatenate(pieces, axis=1))
            values = (values * jac_t[:, n * 256 : n * 256 + 256]).astype(BF16)
            for half in range(2):
                ex, t = n // 2, n % 2 * 2 + half
                part = values[:, half * 128 : half * 128 + 128]
                for h in range(2):
                    blocks = regroup([part[k * 64 : k * 64 + 64] for k in range(h * 4, h * 4 + 4)])
                    for e in range(4):
                        at = ((t * 4 + f) * 4 + e) * 128 + ex * 64
                        lhs[at : at + 64, h * 128 : h * 128 + 128] = blocks[e]


def own_elements(spots, fields_elems, jac, first_arrived):
    vmem = pl.BlockSpec(memory_space=pltpu.VMEM)
    smem = pl.BlockSpec(memory_space=pltpu.SMEM)
    order = jnp.asarray(point_order())
    [jac_t] = local_call(
        jacobian_kernel,
        [jax.ShapeDtypeStruct((512, 1024), F32)],
        [vmem] * 3 + [pl.BlockSpec(memory_space=pl.ANY)],
        [spots, jac, order, first_arrived],
        "jacobians",
        flops=2_000_000_000,
    )
    [rows] = local_call(
        place_kernel,
        [jax.ShapeDtypeStruct((1040, 16, 128), F32)],
        [smem, vmem, pl.BlockSpec(memory_space=pl.ANY)],
        [spots.reshape(1024), fields_elems, jac_t],
        "place",
        flops=2_000_000_000,
    )
    return rows, jac_t


def all_elements(rows, jac_t, arrived):
    vmem = pl.BlockSpec(memory_space=pltpu.VMEM)
    return local_call(
        brick_kernel,
        [
            jax.ShapeDtypeStruct((8192, 256), BF16),
            jax.ShapeDtypeStruct((1040, 16, 128), F32),
        ],
        [vmem] * 10,
        [*arrived, jnp.asarray(point_order()), jnp.asarray(interp_table()), jac_t, rows],
        "brick",
        scratch=[
            pltpu.VMEM((512, 1024), F32),
            pltpu.VMEM((8, 128), jnp.int32),
            pltpu.SMEM((8, 128), jnp.int32),
            pltpu.SemaphoreType.DMA,
        ],
        aliases={9: 1},
        limit=36,
    )[0]


def halve(values, outputs, shift):
    results = []
    for o in range(outputs):
        total = None
        for tap in range(4):
            pair = [
                values[at]
                for at in (2 * o + tap - shift, 2 * o + 7 - tap - shift)
                if 0 <= at < len(values)
            ]
            if pair:
                term = TAPS[tap] * (pair[0] + pair[1] if len(pair) == 2 else pair[0])
                total = term if total is None else total + term
        results.append(total)
    return results


def along_y(ref, base, count, y_low, y_high):
    total = None
    for tap in range(4):
        pair = (
            ref[pl.ds(base + 5 + tap, count, stride=2), :]
            + ref[pl.ds(base + 12 - tap, count, stride=2), :]
        )
        total = TAPS[tap] * pair if total is None else total + TAPS[tap] * pair
    low = total[0:8] * y_low
    high = total[count - 8 : count] * y_high
    return low, total[8 : count - 8], high


def inner_sides():
    ix, iy, _ = brick_place()
    return tuple(jnp.where(flag, 1.0, 0.0) for flag in (ix > 0, ix < 7, iy > 0, iy < 3))


def clear_pads(ref, count, size, width):
    def pads(q, carry):
        zero = jnp.zeros((width, 128), F32)
        base = pl.multiple_of(q * size, 8)
        ref[pl.ds(base, width), :] = zero
        ref[pl.ds(base + size - width, width), :] = zero
        return carry

    lax.fori_loop(0, count, pads, 0, unroll=count)


def along_x(values, outputs, edge, x_low, x_high):
    results = halve(values, outputs, 7)
    return [
        r * x_low if o < edge else r * x_high if o >= outputs - edge else r
        for o, r in enumerate(results)
    ]


def first_x(wide, base, f, e, t, ref, x_low, x_high):
    values = [
        wide[pl.ds(pl.multiple_of(base + e * 128 + x * 8, 8), 8), :] for x in range(16)
    ]
    for o, value in enumerate(along_x(values, 12, 2, x_low, x_high)):
        at = (f * 12 + o) * 176 + 24 + e * 8 + t * 32
        ref[pl.ds(pl.multiple_of(at, 8), 8), :] = value


def first_a_kernel(wide, main_a, edge_a, ya):
    x_low, x_high, y_low, y_high = inner_sides()
    clear_pads(ya, 48, 176, 24)

    def quarter(t, carry):
        for f in range(4):
            for e in range(4):
                first_x(wide, t * 2048 + f * 512, f, e, t, ya, x_low, x_high)
        return carry

    lax.fori_loop(0, 4, quarter, 0)

    def first(q, carry):
        low, middle, high = along_y(ya, q * 176, 80, y_low, y_high)
        edge_a[pl.ds(pl.multiple_of(q * 16, 16), 8), :] = low
        edge_a[pl.ds(pl.multiple_of(q * 16 + 8, 8), 8), :] = high
        main_a[pl.ds(pl.multiple_of(q * 64, 64), 64), :] = middle
        return carry

    lax.fori_loop(0, 48, first, 0, unroll=16)


def filter_kernel(lhs, depths, wide_a, main_c, edge_c, to_low, to_high,
                  depth, wide_b, yb, mb, yc, pbz, pcz, sem):
    x_low, x_high, y_low, y_high = inner_sides()
    _, _, iz = brick_place()
    place = jnp.where(iz == 0, 0, jnp.where(iz == 3, 2, 1))
    copy = pltpu.make_async_copy(depths.at[place], depth, sem)
    copy.start()
    copy.wait()
    clear_pads(yb, 48, 176, 24)
    clear_pads(yc, 40, 112, 16)

    def quarter(t, carry):
        for f in range(4):
            start = pl.multiple_of(t * 2048 + f * 512, 512)
            operand = lhs[pl.ds(start, 512), :]
            both = nn(operand, depth[...])
            wide_a[pl.ds(pl.multiple_of(t * 2048 + f * 512, 512), 512), :] = both[:, 0:128]
            wide_b[f * 512 : f * 512 + 512, :] = both[:, 128:256]
        for f in range(4):
            for e in range(4):
                first_x(wide_b, f * 512, f, e, t, yb, x_low, x_high)
        return carry

    lax.fori_loop(0, 4, quarter, 0, unroll=4)

    def first(q, carry):
        low, middle, high = along_y(yb, q * 176, 80, y_low, y_high)
        base = pl.multiple_of(q * 80, 16)
        mb[pl.ds(base, 8), :] = low
        mb[pl.ds(base + 8, 64), :] = middle
        mb[pl.ds(base + 72, 8), :] = high
        pbz[pl.ds(pl.multiple_of(q * 16, 16), 16), :] = jnp.concatenate(
            [low, high], axis=0
        ).astype(BF16)
        pbz[pl.ds(pl.multiple_of(768 + q * 64, 64), 64), :] = middle.astype(BF16)
        return carry

    lax.fori_loop(0, 48, first, 0, unroll=16)

    def second_x(v, carry):
        for f in range(4):
            values = [
                mb[pl.ds(pl.multiple_of((f * 12 + o) * 80 + v * 8, 8), 8), :] for o in range(12)
            ]
            for o, value in enumerate(along_x(values, 10, 3, x_low, x_high)):
                at = (f * 10 + o) * 112 + 16 + v * 8
                yc[pl.ds(pl.multiple_of(at, 8), 8), :] = value
        return carry

    lax.fori_loop(0, 10, second_x, 0, unroll=10)

    def second(q, carry):
        low, middle, high = along_y(yc, q * 112, 48, y_low, y_high)
        edge_c[pl.ds(pl.multiple_of(q * 16, 16), 8), :] = low
        edge_c[pl.ds(pl.multiple_of(q * 16 + 8, 8), 8), :] = high
        main_c[pl.ds(pl.multiple_of(q * 32, 32), 32), :] = middle
        pcz[pl.ds(pl.multiple_of(q * 16, 16), 16), :] = jnp.concatenate(
            [low, high], axis=0
        ).astype(BF16)
        pcz[pl.ds(pl.multiple_of(640 + q * 32, 32), 32), :] = middle.astype(BF16)
        return carry

    lax.fori_loop(0, 40, second, 0, unroll=20)
    row = lax.broadcasted_iota(jnp.int32, (16, 128), 0)
    lane = lax.broadcasted_iota(jnp.int32, (16, 128), 1)

    def pick(count, low_lane, high_lane):
        low = (row < count) & (lane == row + low_lane)
        high = (row >= 8) & (row < 8 + count) & (lane == row - 8 + high_lane)
        return jnp.where(low | high, 1.0, 0.0).astype(BF16)

    mid = nt(pick(2, 64, 66), pbz[...])
    coarse = nt(pick(3, 68, 71), pcz[...])
    for ref, at in ((to_low, 0), (to_high, 8)):
        ref[:, 0:3840] = mid[at : at + 4].astype(BF16)
        ref[:, 3840:5760] = coarse[at : at + 4].astype(BF16)


def filters(uniform):
    vmem = pl.BlockSpec(memory_space=pltpu.VMEM)
    return local_call(
        filter_kernel,
        [
            jax.ShapeDtypeStruct((8192, 128), F32),
            jax.ShapeDtypeStruct((40 * 32, 128), F32),
            jax.ShapeDtypeStruct((40 * 16, 128), F32),
            jax.ShapeDtypeStruct((4, 5760), BF16),
            jax.ShapeDtypeStruct((4, 5760), BF16),
        ],
        [vmem, pl.BlockSpec(memory_space=pltpu.HBM)],
        [uniform, jnp.asarray(depth_tables())],
        "filters",
        scratch=[
            pltpu.VMEM((256, 256), BF16),
            pltpu.VMEM((2048, 128), F32),
            pltpu.VMEM((48 * 176, 128), F32),
            pltpu.VMEM((48 * 80, 128), F32),
            pltpu.VMEM((40 * 112, 128), F32),
            pltpu.VMEM((3840, 128), BF16),
            pltpu.VMEM((1920, 128), BF16),
            pltpu.SemaphoreType.DMA,
        ],
        limit=32,
    )


def first_a(wide):
    return local_call(
        first_a_kernel,
        [jax.ShapeDtypeStruct((48 * 64, 128), F32), jax.ShapeDtypeStruct((48 * 16, 128), F32)],
        [pl.BlockSpec(memory_space=pltpu.VMEM)],
        [wide],
        "first_a",
        scratch=[pltpu.VMEM((48 * 176, 128), F32)],
        flops=3_000_000_000,
    )


def depth_spread(first_lane_high, count):
    table = np.zeros((8, 128))
    for r in range(count):
        table[r, r] = 1.0
        table[4 + r, first_lane_high + r] = 1.0
    return bf16_of(table)


def y_edges_kernel(edge_a, edge_c, from_low, from_high, spread_a, spread_c,
                   to_low, to_high, sa, sc):
    lanes = jnp.concatenate([from_low[:, 0:768], from_high[:, 0:768]], axis=0)
    sa[...] = edge_a[...] + tn(lanes, spread_a[...])
    lanes = jnp.concatenate([from_low[:, 3840:4480], from_high[:, 3840:4480]], axis=0)
    sc[...] = edge_c[...] + tn(lanes, spread_c[...])
    for ref, ra, rc in ((to_low, 6, 5), (to_high, 8, 8)):
        for r in range(2):
            ref[r * 48 : r * 48 + 48, :] = sa[pl.ds(ra + r, 48, stride=16), :].astype(BF16)
        tail = [sc[pl.ds(rc + r, 40, stride=16), :] for r in range(3)] + [jnp.zeros((8, 128), F32)]
        ref[96:224, :] = jnp.concatenate(tail, axis=0).astype(BF16)


def vmem_call(kernel, out_shape, scratch, name, *operands, **options):
    vmem = pl.BlockSpec(memory_space=pltpu.VMEM)
    single = not isinstance(out_shape, list)
    return pl.pallas_call(
        kernel,
        out_shape=out_shape,
        in_specs=[vmem] * len(operands),
        out_specs=vmem if single else [vmem] * len(out_shape),
        scratch_shapes=scratch,
        compiler_params=pltpu.CompilerParams(vmem_limit_bytes=12 * MIB),
        name=name,
        **options,
    )(*operands)


def z_main_kernel(main_a, main_c, zl, zh, spread_a, spread_c, sa, sc):
    lanes = jnp.concatenate([zl[:, 768:3840], zh[:, 768:3840]], axis=0)
    sa[...] = main_a[...] + tn(lanes, spread_a[...])
    lanes = jnp.concatenate([zl[:, 4480:5760], zh[:, 4480:5760]], axis=0)
    sc[...] = main_c[...] + tn(lanes, spread_c[...])


def x_edges_kernel(sa, sc, yl, yh, to_low, to_high, fl, fh, pa, pc):
    fl[...] = yl[...].astype(F32)
    fh[...] = yh[...].astype(F32)
    for ref, xa, xc in ((to_low, 0, 0), (to_high, 10, 7)):
        for f in range(4):
            first = f * 12 + xa
            pa[...] = sa[first * 64 : first * 64 + 128, :]
            for x in range(2):
                for r in range(2):
                    row = r * 48 + first + x
                    low, high = x * 64 + r, x * 64 + 62 + r
                    pa[low : low + 1, :] += fl[row : row + 1, :]
                    pa[high : high + 1, :] += fh[row : row + 1, :]
            ref[f * 128 : f * 128 + 128, :] = pa[...].astype(BF16)
            first = f * 10 + xc
            at = f % 2 * 96
            pc[at : at + 96, :] = sc[first * 32 : first * 32 + 96, :]
            for x in range(3):
                for r in range(3):
                    row = 96 + r * 40 + first + x
                    low, high = at + x * 32 + r, at + x * 32 + 29 + r
                    pc[low : low + 1, :] += fl[row : row + 1, :]
                    pc[high : high + 1, :] += fh[row : row + 1, :]
            if f % 2 == 1:
                lane = lax.broadcasted_iota(jnp.int32, (96, 128), 1)
                start = 512 + f // 2 * 96
                ref[start : start + 96, :] = jnp.where(
                    lane < 64, pc[0:96, :], pltpu.roll(pc[96:192, :], 64, 1)
                ).astype(BF16)


def inside_kernel(sa_in, sc_in, yl, yh, mid, sa, sc, fl, fh, sems):
    sa[...] = sa_in[...]
    sc[...] = sc_in[...]
    fl[...] = yl[...].astype(F32)
    fh[...] = yh[...].astype(F32)
    for r in range(2):
        sa[pl.ds(r, 48, stride=64), :] += fl[r * 48 : r * 48 + 48, :]
        sa[pl.ds(62 + r, 48, stride=64), :] += fh[r * 48 : r * 48 + 48, :]
    for r in range(3):
        sc[pl.ds(r, 40, stride=32), :] += fl[96 + r * 40 : 136 + r * 40, :]
        sc[pl.ds(29 + r, 40, stride=32), :] += fh[96 + r * 40 : 136 + r * 40, :]
    planes = sa.reshape(48, 64, 128)
    copies = [
        pltpu.make_async_copy(
            planes.at[pl.ds(f * 12 + 4, 4)], mid.at[f].at[pl.ds(2, 4)], sems.at[f]
        )
        for f in range(4)
    ]
    for copy in copies:
        copy.start()
    for copy in copies:
        copy.wait()


def final_kernel(sa, sc, xl, xh, _, coarse, mid, planes, small, sems):
    copies = []
    for side, ref in enumerate((xl, xh)):
        for f in range(4):
            for x in range(2):
                plane = f * 12 + 2 + side * 6 + x
                at = f * 128 + x * 64
                planes[side * 4 + f, x] = sa[plane] + ref[at : at + 64, :].astype(F32)
            copy = pltpu.make_async_copy(
                planes.at[side * 4 + f],
                mid.at[f].at[pl.ds(side * 6, 2)],
                sems.at[side * 4 + f],
            )
            copy.start()
            copies.append(copy)
    for f in range(4):
        half = f % 2 * 64
        for x in range(4):
            base = (f * 10 + x + 3) * 32
            value = sc[base : base + 32, :][:, 0:64]
            start = 512 + f // 2 * 96 + x * 32
            if x < 3:
                value = value + xl[start : start + 32, :].astype(F32)[:, half : half + 64]
            if x >= 1:
                value = value + xh[start - 32 : start, :].astype(F32)[:, half : half + 64]
            small[f, x] = value
    copy = pltpu.make_async_copy(small, coarse, sems.at[8])
    copy.start()
    for copy in copies + [copy]:
        copy.wait()


def shifted(x, axis, by):
    size = lax.axis_size(axis)
    return lax.ppermute(x, axis, [(i, (i + by) % size) for i in range(size)])


def local_views(fields, home_slot):
    fields_rows = fields.reshape(1024, 4, 4, 128).transpose(0, 2, 1, 3).reshape(16384, 128)
    return fields_rows, fields_rows.reshape(1024, 16, 128), home_slot.reshape(8, 128)


def body(fields, jacobian, home_slot):
    fields_rows, fields_elems, home_tile = local_views(fields, home_slot)
    *payloads, spots = pack(home_tile, jacobian, fields_rows)
    arrived = [shifted(p, *move) for p, move in zip(payloads, SHIFTS)]
    rows, jac_t = own_elements(spots, fields_elems, jacobian, arrived[0])
    uniform = all_elements(rows, jac_t, arrived)
    wide_a, main_c, edge_c, z_low, z_high = filters(uniform)
    from_z_low = shifted(z_high, "gz", 1)
    from_z_high = shifted(z_low, "gz", -1)
    main_a, edge_a = first_a(wide_a)
    spread_a = jnp.asarray(depth_spread(126, 2))
    spread_c = jnp.asarray(depth_spread(61, 3))
    y_low, y_high = vmem_call(
        y_edges_kernel,
        [jax.ShapeDtypeStruct((224, 128), BF16)] * 2,
        [pltpu.VMEM((768, 128), F32), pltpu.VMEM((640, 128), F32)],
        "y_edges",
        edge_a, edge_c, from_z_low, from_z_high, spread_a, spread_c,
    )
    from_y_low = shifted(y_high, "gy", 1)
    from_y_high = shifted(y_low, "gy", -1)
    vmem = pl.BlockSpec(memory_space=pltpu.VMEM)
    shapes = [
        jax.ShapeDtypeStruct((48 * 64, 128), F32),
        jax.ShapeDtypeStruct((40 * 32, 128), F32),
    ]
    sum_a, sum_c = local_call(
        z_main_kernel,
        shapes,
        [vmem] * 6,
        [main_a, main_c, from_z_low, from_z_high, spread_a, spread_c],
        "z_main",
        flops=2_000_000_000,
    )
    x_low, x_high = local_call(
        x_edges_kernel,
        [jax.ShapeDtypeStruct((704, 128), BF16)] * 2,
        [vmem] * 4,
        [sum_a, sum_c, from_y_low, from_y_high],
        "x_edges",
        scratch=[
            pltpu.VMEM((224, 128), F32),
            pltpu.VMEM((224, 128), F32),
            pltpu.VMEM((128, 128), F32),
            pltpu.VMEM((192, 128), F32),
        ],
    )
    from_x_low = shifted(x_high, "gx", 1)
    from_x_high = shifted(x_low, "gx", -1)
    hbm = pl.BlockSpec(memory_space=pltpu.HBM)
    mid_shape = jax.ShapeDtypeStruct((4, 8, 64, 128), F32)
    mid, sum_a, sum_c = local_call(
        inside_kernel,
        [mid_shape] + shapes,
        [vmem] * 4,
        [sum_a, sum_c, from_y_low, from_y_high],
        "inside",
        out_specs=[hbm, vmem, vmem],
        scratch=[
            pltpu.VMEM((224, 128), F32),
            pltpu.VMEM((224, 128), F32),
            pltpu.SemaphoreType.DMA((4,)),
        ],
        flops=2_000_000_000,
    )
    coarse, mid = local_call(
        final_kernel,
        [jax.ShapeDtypeStruct((4, 4, 32, 64), F32), mid_shape],
        [vmem] * 4 + [hbm],
        [sum_a.reshape(48, 64, 128), sum_c, from_x_low, from_x_high, mid],
        "final",
        out_specs=[hbm, hbm],
        scratch=[
            pltpu.VMEM((8, 2, 64, 128), F32),
            pltpu.VMEM((4, 4, 32, 64), F32),
            pltpu.SemaphoreType.DMA((9,)),
        ],
        aliases={4: 1},
    )
    return mid, coarse


def solution(mesh):
    placed = (P(("gx", "gy", "gz"), None, None), P(("gx", "gy", "gz"), None), P(("gx", "gy", "gz")))
    return jax.shard_map(
        body,
        mesh=mesh,
        in_specs=placed,
        out_specs=(P(None, "gx", "gy", "gz"), P(None, "gx", "gy", "gz")),
        check_vma=False,
    )
```
